32 devices in a mesh: dp: 8 (over y, x, core), expert: 4 (over z).
Axes of the slice: x: 2, y: 2, z: 4, core: 2. Of those that a mesh axis runs over, the one named last changes fastest.
Arguments:
- tokens: bfloat16 [12288, 2048], P(('dp', 'expert')), may hold values from -6 to 6
- cotangent: bfloat16 [12288, 2048], P(('dp', 'expert')), may hold values from -6 to 6
- attention_gain: bfloat16 [2048], P(('dp', 'expert')), may hold values from 0.5 to 1.5
- query_weight: bfloat16 [2048, 2048], P(('dp', 'expert')), may hold values from -0.125 to 0.125
- key_weight: bfloat16 [2048, 2048], P(('dp', 'expert')), may hold values from -0.125 to 0.125
- value_weight: bfloat16 [2048, 2048], P(('dp', 'expert')), may hold values from -0.125 to 0.125
- out_weight: bfloat16 [2048, 2048], P(('dp', 'expert')), may hold values from -3 to 3
- query_norm: bfloat16 [2048], P(('dp', 'expert')), may hold values from 0.099609375 to 1.8984375
- key_norm: bfloat16 [2048], P(('dp', 'expert')), may hold values from 0.099609375 to 1.8984375
- mixture_gain: bfloat16 [2048], P(('dp', 'expert')), may hold values from 0.5 to 1.5
- router_weight: bfloat16 [2048, 16], P(('dp', 'expert')), may hold values from -0.25 to 0.25
- gate_weight: bfloat16 [16, 2048, 1024], P('expert', 'dp'), may hold values from -0.125 to 0.125
- up_weight: bfloat16 [16, 2048, 1024], P('expert', 'dp'), may hold values from -0.125 to 0.125
- down_weight: bfloat16 [16, 1024, 2048], P('expert', 'dp'), may hold values from -1.5 to 1.5
- segments: int32 [8, 1536], P('dp'), may hold values from 0 to 4, as said below
- positions: int32 [8, 1536], P('dp'), may hold values from 0 to 1151, as said below
- priority: int32 [8, 1536], P('dp'), may hold values from 0 to 1535, each once within a row
- routes: int32 [8, 1536, 8], P('dp'), may hold values from 0 to 15, all different within a row; in each aligned block of 384 rows (0 to 383, 384 to 767, ..., all dimensions but the last counted through in order) at most 288 rows name the same one
Outputs:
- output: bfloat16 [12288, 2048], P(('dp', 'expert'))
- input_grad: float32 [12288, 2048], P(('dp', 'expert'))
- grad_attention_gain: float32 [2048], P(('dp', 'expert'))
- grad_query_weight: float32 [2048, 2048], P(('dp', 'expert'))
- grad_key_weight: float32 [2048, 2048], P(('dp', 'expert'))
- grad_value_weight: float32 [2048, 2048], P(('dp', 'expert'))
- grad_out_weight: float32 [2048, 2048], P(('dp', 'expert'))
- grad_query_norm: float32 [2048], P(('dp', 'expert'))
- grad_key_norm: float32 [2048], P(('dp', 'expert'))
- grad_mixture_gain: float32 [2048], P(('dp', 'expert'))
- grad_router_weight: float32 [2048, 16], P(('dp', 'expert'))
- grad_gate_weight: float32 [16, 2048, 1024], P('expert', 'dp')
- grad_up_weight: float32 [16, 2048, 1024], P('expert', 'dp')
- grad_down_weight: float32 [16, 1024, 2048], P('expert', 'dp')
The draws below stay inside these ranges and needn't reach their ends.
Inputs may be any that keep to these rules, and one draw needn't show every extreme that they name: In each group the 1536 rows form blocks of 128 rows, each block of one segment; segment 0 (the prompt) has 1024 rows and each of the segments 1 to 4 has 128 rows. The prompt's rows hold positions 0 to 1023, each once and rising along the rows; the rows of each continuation hold 1024 to 1151, rising. `priority`: each group's row lists the group's 1536 tokens, each once. `routes`: each token names 8 different experts; among the rows of one device (aligned blocks of 384 rows) no expert is named more than 288 times, and in some such block one expert exactly 288 times.
All inputs are finite; a program needn't handle non-finite values.
Results may differ from the reference program's by a relative error of at most 0.022.
Values may be sent and summed in bfloat16 or wider, within the bound.
A program may use at most 384 MiB of HBM per device.

```python
import math
import jax
import jax.numpy as jnp
import numpy as np
from jax import lax

D = 2048
HEADS = 16
HEAD_DIM = 128
FF = 1024
TOPK = 8
EXPERTS = 16
PROMPT = 1024
CLEN = 128
CONT = 4
GTOK = 1536
TOK_DEV = 384
GROUPS = 8
TOKENS = 12288
CAP = 768
MOST = 288


def block_layout(key):
    prompt_blocks = PROMPT // CLEN
    block_total = prompt_blocks + CONT
    group_keys = jax.random.split(jax.random.fold_in(key, 11), GROUPS)

    def one_group(group_key):
        arrangement = jax.random.permutation(group_key, block_total).astype(jnp.int32)
        is_prompt = arrangement < prompt_blocks
        prompt_rank = jnp.cumsum(is_prompt.astype(jnp.int32)) - 1
        block_segment = jnp.where(is_prompt, 0, arrangement - prompt_blocks + 1).astype(jnp.int32)
        block_start = jnp.where(is_prompt, prompt_rank * CLEN, PROMPT).astype(jnp.int32)
        offsets = jnp.arange(CLEN, dtype=jnp.int32)
        segment_rows = jnp.broadcast_to(block_segment[:, None], (block_total, CLEN)).reshape(-1)
        place_rows = (block_start[:, None] + offsets[None, :]).reshape(-1)
        return (segment_rows.astype(jnp.int32), place_rows.astype(jnp.int32))
    return jax.vmap(one_group)(group_keys)


def draw_segments(key, part):
    return block_layout(key)[0]


def draw_positions(key, part):
    return block_layout(key)[1]


def levels(key, extent, cuts, smallest, largest):
    def one(axis_at, blocks):
        draws = jax.random.uniform(jax.random.fold_in(jax.random.fold_in(key, 6), axis_at), (blocks,), jnp.float32, smallest / len(cuts), largest / len(cuts))
        return jnp.repeat(jnp.exp(draws), extent[axis_at] // blocks).reshape((-1,) + (1,) * (len(extent) - axis_at - 1))

    loudness = one(*cuts[0])
    for cut in cuts[1:]:
        loudness = loudness * one(*cut)
    return loudness


def shared_out(rng, own, number, rows, number_of, top, most, lean):
    order = jax.random.permutation(rng, number_of)
    heavy_load, ordinary = portions_of(number_of, rows * top, most, lean, True), portions_of(number_of, rows * top, most, lean, False)
    places = jnp.arange(number_of)

    def named(lengths, offset_by):
        used = int((lengths > 0).sum())
        fixed = max(1, used // 4)
        shifted = fixed + (places - fixed + offset_by * (used - fixed)) % max(1, number_of - fixed)
        return jnp.zeros((number_of,), jnp.int32).at[order[jnp.where(places < fixed, places, shifted)]].set(jnp.asarray(lengths, jnp.int32))

    lengths = jnp.where(number % 4 == 0, named(heavy_load, number // 4), named(ordinary, number - number // 4 - 1))
    mixed = jax.random.permutation(jax.random.fold_in(own, 3), number_of)
    donor, sink = mixed[0:number_of // 2 * 2:2], mixed[1:number_of // 2 * 2:2]
    slack = jnp.minimum(lengths[donor] - 1, most - lengths[sink]) // 2
    slack = jnp.where((donor == order[0]) | (sink == order[0]) | (lengths[sink] == 0), 0, jnp.maximum(slack, 0))
    shifted = jax.random.randint(jax.random.fold_in(own, 4), (number_of // 2,), 0, 1 << 20) % (slack + 1)
    lengths = lengths.at[donor].add(-shifted).at[sink].add(shifted)
    labels = jnp.searchsorted(jnp.cumsum(lengths), jnp.arange(rows * top), side="right").astype(jnp.int32)
    table = labels.reshape(top, rows).T
    table = table[jax.random.permutation(jax.random.fold_in(own, 1), rows)]
    offset_by = jax.random.randint(jax.random.fold_in(own, 2), (rows, 1), 0, top)
    return jnp.take_along_axis(table, (jnp.arange(top)[None, :] + offset_by) % top, axis=1)


def portions_of(number_of, total, most, slope, full):
    weights = [(1 << 20) // math.isqrt(standing ** slope) + 1 for standing in range(1, number_of + 1)]
    largest = most if full else min(most, max(-(-total // number_of), total * weights[0] // sum(weights)))
    least = 1 if total - largest >= number_of - 1 else 0
    counts, surplus = [largest] + [least] * (number_of - 1), total - largest - least * (number_of - 1)
    while surplus > 0:
        candidates = [i for i in range(1, number_of) if counts[i] < largest] or [i for i in range(1, number_of) if counts[i] < most]
        whole, remaining = sum([weights[i] for i in candidates]), surplus
        for i in candidates:
            extra = min(most - counts[i], max(1, remaining * weights[i] // whole), surplus)
            counts[i] = counts[i] + extra
            surplus = surplus - extra
    return np.array(counts)


def bell_draw(stream_key, extent, spread, limit, cuts=(), held_as=jnp.bfloat16):
    drawn = spread * jax.random.normal(stream_key, extent, jnp.float32)
    if cuts:
        drawn = drawn * levels(stream_key, extent, cuts, -0.22, 0.18)
    return jnp.clip(drawn, -limit, limit).astype(held_as)


def setup_inputs(seed: int = 0) -> dict:
    seeds = jax.random.split(jax.random.key(seed), 19)
    tokens = bell_draw(seeds[0], (TOKENS, D), 1.0, 6.0, ((0, 32),))
    cotangent = bell_draw(seeds[1], (TOKENS, D), 1.0, 6.0, ((0, 32),))
    attention_gain = jnp.clip(1.0 + 0.1 * jax.random.normal(seeds[2], (D,), jnp.float32), 0.5, 1.5).astype(jnp.bfloat16)
    query_weight = bell_draw(seeds[3], (D, D), D ** -0.5, 0.125, ((0, 32),))
    key_weight = bell_draw(seeds[4], (D, D), D ** -0.5, 0.125, ((0, 32),))
    value_weight = bell_draw(seeds[5], (D, D), D ** -0.5, 0.125, ((0, 32),))
    out_weight = bell_draw(seeds[6], (D, D), (max(D // 512, 1)) ** -0.5, 3.0, ((0, 32),))
    query_norm = jnp.clip(1.0 + 0.18 * jax.random.normal(seeds[7], (D,), jnp.float32), 0.099609375, 1.8984375).astype(jnp.bfloat16)
    key_norm = jnp.clip(1.0 + 0.18 * jax.random.normal(seeds[8], (D,), jnp.float32), 0.099609375, 1.8984375).astype(jnp.bfloat16)
    mixture_gain = jnp.clip(1.0 + 0.1 * jax.random.normal(seeds[9], (D,), jnp.float32), 0.5, 1.5).astype(jnp.bfloat16)
    router_weight = bell_draw(seeds[10], (D, EXPERTS), (D // 4) ** -0.5, 0.25, ((0, 32),))
    gate_weight = bell_draw(seeds[11], (EXPERTS, D, FF), D ** -0.5, 0.125, ((0, 4), (1, 8)))
    up_weight = bell_draw(seeds[12], (EXPERTS, D, FF), D ** -0.5, 0.125, ((0, 4), (1, 8)))
    down_weight = bell_draw(seeds[13], (EXPERTS, FF, D), (max(FF // 64, 1)) ** -0.5, 1.5, ((0, 4), (1, 8)))
    segments = draw_segments(jax.random.fold_in(seeds[18], 71), 0)
    positions = draw_positions(jax.random.fold_in(seeds[18], 71), 0)
    priority = jax.vmap(lambda own: jax.random.permutation(own, GTOK))(jax.random.split(seeds[16], GROUPS)).reshape((GROUPS, GTOK)).astype(jnp.int32)
    routes_keys = jax.random.split(jax.random.fold_in(seeds[17], 1), GROUPS * GTOK // TOK_DEV)
    routes_turns = jax.random.permutation(jax.random.fold_in(seeds[17], 3), GROUPS * GTOK // TOK_DEV)
    routes = jax.vmap(lambda own, number: shared_out(jax.random.fold_in(seeds[17], 2), own, number, TOK_DEV, EXPERTS, TOPK, MOST, 1))(routes_keys, routes_turns).reshape((GROUPS, GTOK, TOPK))
    return {"tokens": tokens, "cotangent": cotangent, "attention_gain": attention_gain, "query_weight": query_weight, "key_weight": key_weight, "value_weight": value_weight, "out_weight": out_weight, "query_norm": query_norm, "key_norm": key_norm, "mixture_gain": mixture_gain, "router_weight": router_weight, "gate_weight": gate_weight, "up_weight": up_weight, "down_weight": down_weight, "segments": segments, "positions": positions, "priority": priority, "routes": routes}


@jax.custom_vjp
def low(v):
    return lax.optimization_barrier(v.astype(jnp.bfloat16)).astype(jnp.float32)

@jax.custom_vjp
def low_back(v):
    return v

def low_keep(v):
    return (low(v), None)

def low_pass(kept, grad):
    return (grad,)

def back_keep(v):
    return (v, None)

def back_low(kept, grad):
    return (low(grad),)
low.defvjp(low_keep, low_pass)
low_back.defvjp(back_keep, back_low)
EPS = 1e-05
HIGH = lax.Precision.HIGHEST

def rms_scale(values, gain_vec):
    return values * lax.rsqrt(lax.optimization_barrier(jnp.mean(values * values, axis=-1, keepdims=True)) + EPS) * gain_vec

def rope_tables(places):
    frequency = 10000.0 ** (-jnp.arange(0, HEAD_DIM // 2, dtype=jnp.float32) * 2.0 / HEAD_DIM)
    angles = places.astype(jnp.float32)[:, None] * frequency[None, :]
    return (jnp.cos(angles)[:, None, :], jnp.sin(angles)[:, None, :])

def rotate(values, cosine_table, sine_table):
    half_dim = values.shape[-1] // 2
    first_half = values[..., :half_dim]
    second_half = values[..., half_dim:]
    return jnp.concatenate([first_half * cosine_table - second_half * sine_table, second_half * cosine_table + first_half * sine_table], axis=-1)

def slotting(group_routes, group_order):
    expert_ids = jnp.arange(EXPERTS, dtype=jnp.int32)
    route_hits = lax.optimization_barrier(jnp.sum((group_routes[:, :, None] == expert_ids[None, None, :]).astype(jnp.int32), axis=1))
    ranked = route_hits[group_order]
    before = jnp.cumsum(ranked, axis=0) - ranked
    inverse = jnp.zeros((GTOK,), jnp.int32).at[group_order].set(jnp.arange(GTOK, dtype=jnp.int32))
    global_slot = before[inverse]
    slots = jnp.take_along_axis(global_slot, group_routes, axis=1)
    kept_mask = slots < CAP
    flat_place = jnp.where(kept_mask, group_routes * CAP + slots, EXPERTS * CAP).astype(jnp.int32)
    return (kept_mask, flat_place)

def layer(params, tokens_group, group_segs, group_places, group_routes, kept_mask, flat_place):
    attention_gain, query_weight, key_weight, value_weight, out_weight, query_norm, key_norm, mixture_gain, router_weight, gate_weight, up_weight, down_weight = params
    normed = low(rms_scale(tokens_group, attention_gain))
    query = low_back(jnp.dot(normed, query_weight, precision=HIGH))
    keys = low_back(jnp.dot(normed, key_weight, precision=HIGH))
    values = low_back(jnp.dot(normed, value_weight, precision=HIGH))
    cosine_table, sine_table = rope_tables(group_places)
    query_rot = low(rotate(rms_scale(query, query_norm).reshape(GTOK, HEADS, HEAD_DIM), cosine_table, sine_table))
    key_rot = low(rotate(rms_scale(keys, key_norm).reshape(GTOK, HEADS, HEAD_DIM), cosine_table, sine_table))
    value_low = low(values).reshape(GTOK, HEADS, HEAD_DIM)
    raw = low_back(jnp.einsum('qhd,khd->hqk', query_rot, key_rot, precision=HIGH))
    shared = (group_segs[None, :] == 0) | (group_segs[None, :] == group_segs[:, None])
    visible_mask = shared & (group_places[None, :] <= group_places[:, None])
    scores = jnp.where(visible_mask[None], raw * HEAD_DIM ** (-0.5), -1e+30)
    probs = low(jax.nn.softmax(scores, axis=-1))
    mixed = jnp.einsum('hqk,khd->qhd', probs, value_low, precision=HIGH).reshape(GTOK, D)
    mixed = low(low_back(mixed))
    resid = tokens_group + low_back(jnp.dot(mixed, out_weight, precision=HIGH))
    mix = low(rms_scale(resid, mixture_gain))
    logits = low_back(jnp.dot(mix, router_weight, precision=HIGH))
    router = jax.nn.softmax(logits, axis=-1)
    weight = jnp.take_along_axis(router, group_routes, axis=1) * kept_mask.astype(jnp.float32)
    copies = jnp.broadcast_to(mix[:, None, :], (GTOK, TOPK, D)).reshape(GTOK * TOPK, D)
    slot_rows = jnp.zeros((EXPERTS * CAP + 1, D), jnp.float32).at[flat_place.reshape(-1)].add(copies)
    inputs = low_back(slot_rows[:EXPERTS * CAP].reshape(EXPERTS, CAP, D))
    gate_pre = low_back(jnp.einsum('esd,edf->esf', inputs, gate_weight, precision=HIGH))
    up_pre = low_back(jnp.einsum('esd,edf->esf', inputs, up_weight, precision=HIGH))
    hidden = low(jax.nn.silu(gate_pre) * up_pre)
    expert_out = low(low_back(jnp.einsum('esf,efd->esd', hidden, down_weight, precision=HIGH)))
    padded = jnp.concatenate([expert_out.reshape(EXPERTS * CAP, D), jnp.zeros((1, D), jnp.float32)], axis=0)
    picked = padded[flat_place]
    return resid + lax.optimization_barrier(jnp.sum(weight[:, :, None] * picked, axis=1))

def reference(tokens, cotangent, attention_gain, query_weight, key_weight, value_weight, out_weight, query_norm, key_norm, mixture_gain, router_weight, gate_weight, up_weight, down_weight, segments, positions, priority, routes):
    params = tuple((item.astype(jnp.float32) for item in (attention_gain, query_weight, key_weight, value_weight, out_weight, query_norm, key_norm, mixture_gain, router_weight, gate_weight, up_weight, down_weight)))

    def group_step(totals, scan_items):
        tokens_group, grad_group, group_segs, group_places, group_order, group_routes = scan_items
        kept_mask, flat_place = slotting(group_routes, group_order)

        def forward(param_set, layer_in):
            return layer(param_set, layer_in, group_segs, group_places, group_routes, kept_mask, flat_place)
        result, pullback = jax.vjp(forward, params, tokens_group.astype(jnp.float32))
        grad_params, grad_tokens = pullback(grad_group.astype(jnp.float32))
        totals = jax.tree.map(lambda total_now, grad_now: total_now + grad_now, totals, grad_params)
        return (totals, (result.astype(jnp.bfloat16), grad_tokens))
    start = jax.tree.map(jnp.zeros_like, params)
    scan_inputs = (tokens.reshape(GROUPS, GTOK, D), cotangent.reshape(GROUPS, GTOK, D), segments, positions, priority, routes)
    totals, (results, grads) = lax.scan(group_step, start, scan_inputs)
    return (results.reshape(TOKENS, D), grads.reshape(TOKENS, D), totals[0], totals[1], totals[2], totals[3], totals[4], totals[5], totals[6], totals[7], totals[8], totals[9], totals[10], totals[11])
```

```python
import functools

import jax
import jax.numpy as jnp
from jax import lax
from jax.experimental import pallas as pl
from jax.experimental.pallas import tpu as pltpu
from jax.sharding import PartitionSpec as P

HEADS = 16
HEAD_DIM = 128
TOPK = 8
EXPERTS = 16
GTOK = 1536
CAP = 768
PROMPT = 1024
CLEN = 128
BLOCKS = GTOK // CLEN
TILE = 256
EPS = 1e-05
BOTH = ("dp", "expert")
F32 = jnp.float32
BF16 = jnp.bfloat16
SCALE = HEAD_DIM ** (-0.5)
NEG = -1e30
SMALL = 128
MESH = pl.DeviceIdType.MESH


def norm_back(grad_rows, unit_rows, inverse, gain_vec):
    grad_unit = grad_rows * gain_vec
    inner_mean = jnp.mean(grad_unit * unit_rows, axis=-1, keepdims=True)
    return inverse * (grad_unit - unit_rows * inner_mean)


def cross_rows(left, right):
    return lax.dot_general(left, right, (((0,), (0,)), ((), ())), preferred_element_type=F32)


def by_transpose(left, right):
    return lax.dot_general(left, right, (((1,), (1,)), ((), ())), preferred_element_type=F32)


def plain(left, right):
    return lax.dot_general(left, right, (((1,), (0,)), ((), ())), preferred_element_type=F32)


def causal(rows):
    return lax.broadcasted_iota(jnp.int32, (rows, rows), 1) <= lax.broadcasted_iota(
        jnp.int32, (rows, rows), 0
    )


def tiles():
    out = []
    for i in range(PROMPT // TILE):
        keys = [(0, i * TILE, False)] if i else []
        out.append((i * TILE, TILE, keys + [(i * TILE, TILE, True)]))
    for c in range(PROMPT // CLEN, BLOCKS):
        out.append((c * CLEN, CLEN, [(0, PROMPT, False), (c * CLEN, CLEN, True)]))
    return out


def rope(values, cos_rows, sin_rows):
    return values * cos_rows + pltpu.roll(values, HEAD_DIM // 2, 1) * sin_rows


def attend_kernel(
    order, q_pre, k_pre, v_pre, inv_q, inv_k, gain_q, gain_k, cos, sin, q_rot, k_rot, v_out, mixed, lse
):
    for i in range(BLOCKS):
        here = pl.ds(i * CLEN, CLEN)
        there = pl.ds(pl.multiple_of(order[i] * CLEN, CLEN), CLEN)
        cos_rows, sin_rows = cos[there, :], sin[there, :]
        q_n = q_pre[there, :] * inv_q[there, :] * gain_q[...]
        k_n = k_pre[there, :] * inv_k[there, :] * gain_k[...]
        q_rot[here, :] = rope(q_n, cos_rows, sin_rows).astype(BF16)
        k_rot[here, :] = rope(k_n, cos_rows, sin_rows).astype(BF16)
        v_out[here, :] = v_pre[there, :].astype(BF16)
    for start, rows, keys in tiles():
        q = q_rot[pl.ds(start, rows), :]
        parts = []
        for k_start, k_rows, masked in keys:
            s = by_transpose(q, k_rot[pl.ds(k_start, k_rows), :]) * SCALE
            parts.append(jnp.where(causal(rows), s, NEG) if masked else s)
        top = functools.reduce(jnp.maximum, [jnp.max(s, axis=1, keepdims=True) for s in parts])
        exps = [jnp.exp(s - top) for s in parts]
        total = functools.reduce(lambda a, b: a + b, [jnp.sum(e, axis=1, keepdims=True) for e in exps])
        over = 1.0 / total
        result = None
        for e, (k_start, k_rows, _) in zip(exps, keys):
            term = plain((e * over).astype(BF16), v_out[pl.ds(k_start, k_rows), :])
            result = term if result is None else result + term
        lse[pl.ds(start, rows), :] = jnp.broadcast_to(top + jnp.log(total), (rows, HEAD_DIM))
        for j in range(rows // CLEN):
            block = start // CLEN + j
            there = pl.ds(pl.multiple_of(order[block] * CLEN, CLEN), CLEN)
            mixed[there, :] = result[j * CLEN : (j + 1) * CLEN].astype(BF16)


def attend(order, qkv, inv_q, inv_k, gain_q, gain_k, cos, sin):
    heads = qkv.shape[1] // (3 * HEAD_DIM)
    head = lambda off: pl.BlockSpec((GTOK, HEAD_DIM), lambda h, o: (0, h + off))
    whole = lambda w: pl.BlockSpec((GTOK, w), lambda h, o: (0, 0))
    gain = pl.BlockSpec((1, HEAD_DIM), lambda h, o: (0, h))
    wide = jax.ShapeDtypeStruct((GTOK, heads * HEAD_DIM), BF16)
    return pl.pallas_call(
        attend_kernel,
        grid_spec=pltpu.PrefetchScalarGridSpec(
            num_scalar_prefetch=1,
            grid=(heads,),
            in_specs=[head(0), head(heads), head(2 * heads), whole(1), whole(1), gain, gain]
            + [whole(HEAD_DIM)] * 2,
            out_specs=[head(0)] * 5,
        ),
        out_shape=[wide] * 4 + [jax.ShapeDtypeStruct((GTOK, heads * HEAD_DIM), F32)],
        compiler_params=pltpu.CompilerParams(vmem_limit_bytes=48 * 2**20),
    )(order, qkv, qkv, qkv, inv_q, inv_k, gain_q, gain_k, cos, sin)


def attend_back_kernel(
    order, q_rot, k_rot, v_in, lse, grad_mixed, cos, sin, dq_out, dk_out, dv_out, grads, dq, dk, dv
):
    for i in range(BLOCKS):
        there = pl.ds(pl.multiple_of(order[i] * CLEN, CLEN), CLEN)
        grads[pl.ds(i * CLEN, CLEN), :] = grad_mixed[there, :]
    dk[...] = jnp.zeros_like(dk)
    dv[...] = jnp.zeros_like(dv)
    for start, rows, keys in tiles():
        here = pl.ds(start, rows)
        q, g, level = q_rot[here, :], grads[here, :], lse[here, 0:1]
        probs, grad_probs, delta = [], [], 0.0
        for k_start, k_rows, masked in keys:
            s = by_transpose(q, k_rot[pl.ds(k_start, k_rows), :]) * SCALE
            s = jnp.where(causal(rows), s, NEG) if masked else s
            p = jnp.exp(s - level)
            gp = by_transpose(g, v_in[pl.ds(k_start, k_rows), :])
            delta = delta + jnp.sum(p * gp, axis=1, keepdims=True)
            probs.append(p)
            grad_probs.append(gp)
        total = None
        for p, gp, (k_start, k_rows, _) in zip(probs, grad_probs, keys):
            there = pl.ds(k_start, k_rows)
            raw = (p * (gp - delta) * SCALE).astype(BF16)
            term = plain(raw, k_rot[there, :])
            total = term if total is None else total + term
            dk[there, :] += cross_rows(raw, q)
            dv[there, :] += cross_rows(p.astype(BF16), g)
        dq[here, :] = total
    for i in range(BLOCKS):
        here = pl.ds(i * CLEN, CLEN)
        there = pl.ds(pl.multiple_of(order[i] * CLEN, CLEN), CLEN)
        cos_rows, sin_rows = cos[there, :], sin[there, :]
        dq_out[there, :] = rope(dq[here, :], cos_rows, -sin_rows)
        dk_out[there, :] = rope(dk[here, :], cos_rows, -sin_rows)
        dv_out[there, :] = dv[here, :].astype(BF16)


def attend_back(order, q_rot, k_rot, v_in, lse, grad_mixed, cos, sin):
    heads = q_rot.shape[1] // HEAD_DIM
    head = pl.BlockSpec((GTOK, HEAD_DIM), lambda h, o: (0, h))
    whole = pl.BlockSpec((GTOK, HEAD_DIM), lambda h, o: (0, 0))
    wide = lambda t: jax.ShapeDtypeStruct((GTOK, heads * HEAD_DIM), t)
    return pl.pallas_call(
        attend_back_kernel,
        grid_spec=pltpu.PrefetchScalarGridSpec(
            num_scalar_prefetch=1,
            grid=(heads,),
            in_specs=[head] * 5 + [whole] * 2,
            out_specs=[head] * 3,
            scratch_shapes=[
                pltpu.VMEM((GTOK, HEAD_DIM), BF16),
                pltpu.VMEM((GTOK, HEAD_DIM), F32),
                pltpu.VMEM((GTOK, HEAD_DIM), F32),
                pltpu.VMEM((GTOK, HEAD_DIM), F32),
            ],
        ),
        out_shape=[wide(F32), wide(F32), wide(BF16)],
        compiler_params=pltpu.CompilerParams(vmem_limit_bytes=48 * 2**20),
    )(order, q_rot, k_rot, v_in, lse, grad_mixed, cos, sin)


ANY=pl.BlockSpec(memory_space=pl.ANY); VM=pl.BlockSpec(memory_space=pltpu.VMEM)

def peer(i): return {"expert": i}

def greet_line(n):
    p=lax.axis_index("expert")
    bar=pltpu.get_barrier_semaphore()
    @pl.when(p>0)
    def _(): pl.semaphore_signal(bar,inc=1,device_id=peer(p-1))
    @pl.when(p<n-1)
    def _(): pl.semaphore_signal(bar,inc=1,device_id=peer(p+1))
    pl.semaphore_wait(bar,(p>0).astype(jnp.int32)+(p<n-1).astype(jnp.int32))
    return p

def greet_all(n):
    p=lax.axis_index("expert")
    bar=pltpu.get_barrier_semaphore()
    for s in range(1,n): pl.semaphore_signal(bar,inc=1,device_id=peer(lax.rem(p+s,n)))
    pl.semaphore_wait(bar,n-1)
    return p

def params(cid,mb=60): return pltpu.CompilerParams(collective_id=cid,has_side_effects=True,vmem_limit_bytes=mb*2**20)

def ag_kernel(n,rows,x,out,to_right,to_left,recv,local):
    p=greet_line(n)
    at=lambda j: out.at[pl.ds(pl.multiple_of(j*rows,rows),rows)]
    own=pltpu.make_async_copy(x,at(p),local); own.start()
    def copy(src,j,sems,q):
        return pltpu.make_async_remote_copy(src_ref=src,dst_ref=at(j),send_sem=sems.at[j],recv_sem=recv.at[j],device_id=peer(q),device_id_type=MESH)
    right=lambda src,j: copy(src,j,to_right,p+1)
    left=lambda src,j: copy(src,j,to_left,p-1)
    @pl.when(p<n-1)
    def _(): right(x,p).start()
    @pl.when(p>0)
    def _(): left(x,p).start()
    for s in range(1,n):
        j=p-s
        @pl.when(j>=0)
        def _():
            right(at(j),j).wait_recv()
            @pl.when(p<n-1)
            def _(): right(at(j),j).start()
        k=p+s
        @pl.when(k<n)
        def _():
            left(at(k),k).wait_recv()
            @pl.when(p>0)
            def _(): left(at(k),k).start()
    own.wait()
    for j in range(n):
        @pl.when((j<=p)&(p<n-1))
        def _(): right(x,j).wait_send()
        @pl.when((j>=p)&(p>0))
        def _(): left(x,j).wait_send()

def ag_z(x,n,cid):
    rows=x.shape[0]
    return pl.pallas_call(functools.partial(ag_kernel,n,rows),out_shape=jax.ShapeDtypeStruct((n*rows,)+x.shape[1:],x.dtype),
        in_specs=[ANY],out_specs=ANY,scratch_shapes=[pltpu.SemaphoreType.DMA((n,))]*3+[pltpu.SemaphoreType.DMA],
        compiler_params=params(cid))(x)

def rs_kernel(n,rows,C,depth,part,out,from_left,from_right,to_right,to_left,recv_r,recv_l):
    p=greet_line(n)
    size=rows//C
    def at(j,c): return part.at[pl.ds(pl.multiple_of(j*rows+c*size,size),size)]
    def right(j,c): return pltpu.make_async_remote_copy(src_ref=at(j,c),dst_ref=from_left.at[j*C+c],send_sem=to_right.at[j*C+c],recv_sem=recv_r.at[j*C+c],device_id=peer(p+1),device_id_type=MESH)
    def left(j,c): return pltpu.make_async_remote_copy(src_ref=at(j,c),dst_ref=from_right.at[j*C+c],send_sem=to_left.at[j*C+c],recv_sem=recv_l.at[j*C+c],device_id=peer(p-1),device_id_type=MESH)
    def add(j,c,buf):
        at(j,c)[...]=(at(j,c)[...].astype(F32)+buf[j*C+c].astype(F32)).astype(BF16)
    order=[(s,c) for s in range(n-1) for c in range(C)]
    for m,(s,c) in enumerate(order):
        j=n-1-s
        @pl.when(j>p)
        def _():
            @pl.when(p>0)
            def _():
                right(j,c).wait_recv(); add(j,c,from_left)
            if m>=depth:
                s0,c0=order[m-depth]
                right(n-1-s0,c0).wait_send()
            right(j,c).start()
        k=s
        @pl.when(k<p)
        def _():
            @pl.when(p<n-1)
            def _():
                left(k,c).wait_recv(); add(k,c,from_right)
            if m>=depth:
                s0,c0=order[m-depth]
                left(s0,c0).wait_send()
            left(k,c).start()
    for c in range(C):
        @pl.when(p>0)
        def _():
            right(p,c).wait_recv(); add(p,c,from_left)
        @pl.when(p<n-1)
        def _():
            left(p,c).wait_recv(); add(p,c,from_right)
        out[pl.ds(c*size,size)]=at(p,c)[...]
    for m,(s,c) in enumerate(order):
        j=n-1-s
        last_r=(n-1-p)*C
        @pl.when((j>p)&(m>=last_r-depth))
        def _(): right(j,c).wait_send()
        last_l=p*C
        @pl.when((s<p)&(m>=last_l-depth))
        def _(): left(s,c).wait_send()

def rs_z(part,n,cid,C=4,depth=2):
    rows=part.shape[0]//n; D=part.shape[1]
    return pl.pallas_call(functools.partial(rs_kernel,n,rows,C,depth),out_shape=jax.ShapeDtypeStruct((rows,D),BF16),
        in_specs=[VM],out_specs=VM,scratch_shapes=[pltpu.VMEM((n*C,rows//C,D),BF16)]*2+[pltpu.SemaphoreType.DMA((n*C,))]*4,
        compiler_params=params(cid))(part)

def a2a_kernel(n,rows,cols,x,out,send,recv,local):
    p=greet_all(n)
    src=lambda j: x.at[pl.ds(pl.multiple_of(j*rows,rows),rows)]
    dst=lambda c: out.at[:,pl.ds(pl.multiple_of(c*cols,cols),cols)]
    own=pltpu.make_async_copy(src(p),dst(p),local); own.start()
    def send_to(s):
        j=lax.rem(p+s,n)
        return pltpu.make_async_remote_copy(src_ref=src(j),dst_ref=dst(p),send_sem=send.at[s],recv_sem=recv.at[s],device_id=peer(j),device_id_type=MESH)
    for s in range(1,n): send_to(s).start()
    for s in range(1,n):
        c=lax.rem(p-s+n,n)
        pltpu.make_async_remote_copy(src_ref=src(p),dst_ref=dst(c),send_sem=send.at[s],recv_sem=recv.at[s],device_id=peer(c),device_id_type=MESH).wait_recv()
    for s in range(1,n): send_to(s).wait_send()
    own.wait()

def a2a_z(x,n,cid):
    rows=x.shape[0]//n; cols=x.shape[1]
    return pl.pallas_call(functools.partial(a2a_kernel,n,rows,cols),out_shape=jax.ShapeDtypeStruct((rows,n*cols),x.dtype),
        in_specs=[ANY],out_specs=ANY,scratch_shapes=[pltpu.SemaphoreType.DMA((n,))]*2+[pltpu.SemaphoreType.DMA],
        compiler_params=params(cid))(x)

def exchange_kernel(n, rows, x, out, send, recv, local):
    p = greet_all(n)
    at = lambda ref, j: ref.at[pl.ds(pl.multiple_of(j * rows, rows), rows)]
    own = pltpu.make_async_copy(at(x, p), at(out, p), local)
    own.start()

    def to(s):
        j = lax.rem(p + s, n)
        return pltpu.make_async_remote_copy(
            src_ref=at(x, j), dst_ref=at(out, p), send_sem=send.at[s], recv_sem=recv.at[s], device_id=peer(j),
            device_id_type=MESH,
        )

    for s in range(1, n):
        to(s).start()
    for s in range(1, n):
        to(s).wait_recv()
    for s in range(1, n):
        to(s).wait_send()
    own.wait()


def exchange_z(x, n, cid):
    return pl.pallas_call(
        functools.partial(exchange_kernel, n, x.shape[0] // n),
        out_shape=jax.ShapeDtypeStruct(x.shape, x.dtype),
        in_specs=[ANY],
        out_specs=ANY,
        scratch_shapes=[pltpu.SemaphoreType.DMA((n,))] * 2 + [pltpu.SemaphoreType.DMA],
        compiler_params=params(cid),
    )(x)


def sum_kernel(n,x,out,got,send,recv):
    p=greet_all(n)
    def send_to(s):
        return pltpu.make_async_remote_copy(src_ref=x,dst_ref=got.at[s],send_sem=send.at[s],recv_sem=recv.at[s],device_id=peer(lax.rem(p+s,n)),device_id_type=MESH)
    for s in range(1,n): send_to(s).start()
    tot=x[...]
    for s in range(1,n):
        send_to(s).wait_recv(); tot=tot+got[s]
    out[...]=tot
    for s in range(1,n): send_to(s).wait_send()

def sum_z(x,n,cid):
    return pl.pallas_call(functools.partial(sum_kernel,n),out_shape=jax.ShapeDtypeStruct(x.shape,x.dtype),in_specs=[VM],out_specs=VM,
        scratch_shapes=[pltpu.VMEM((n,)+x.shape,x.dtype)]+[pltpu.SemaphoreType.DMA((n,))]*2,compiler_params=params(cid))(x)


def row_moves(ways, dp):
    return [(d * ways + z, z * dp + d) for d in range(dp) for z in range(ways)]


def hops(up, down, count, ways):
    for _ in range(count):
        up = up + [lax.ppermute(up[-1], "expert", [(i, i + 1) for i in range(ways - 1)])]
        down = down + [lax.ppermute(down[-1], "expert", [(i + 1, i) for i in range(ways - 1)])]
    return up, down


def later(sent, other):
    up, down = sent
    last_up, last_down, other = lax.optimization_barrier((up[-1], down[-1], other))
    return up[:-1] + [last_up], down[:-1] + [last_down], other


def line_up(up, down, ways):
    line = jnp.concatenate(up[:0:-1] + down, axis=0)
    rows = down[0].shape[0]
    start = (ways - 1 - lax.axis_index("expert")) * rows
    return lax.dynamic_slice_in_dim(line, start, ways * rows, axis=0)


def block_order(segs, places):
    seg = segs.reshape(BLOCKS, CLEN)[:, 0]
    place = places.reshape(BLOCKS, CLEN)[:, 0]
    stand = jnp.where(seg == 0, place // CLEN, PROMPT // CLEN - 1 + seg)
    blocks = jnp.arange(BLOCKS, dtype=jnp.int32)
    return jnp.sum(jnp.where(stand[None, :] == blocks[:, None], blocks[None, :], 0), axis=1)


def slots(routes, priority):
    experts = jnp.arange(EXPERTS, dtype=jnp.int32)
    hits = jnp.any(routes[:, :, None] == experts[None, None, :], axis=1)
    index = jnp.arange(GTOK, dtype=jnp.int32)
    rank = jnp.sum(jnp.where(priority[:, None] == index[None, :], index[:, None], 0), axis=0)
    earlier = (rank[None, :] < rank[:, None]).astype(BF16)
    return hits, plain(earlier, hits.astype(BF16)).astype(jnp.int32)


def body(
    tokens,
    cotangent,
    attention_gain,
    query_weight,
    key_weight,
    value_weight,
    out_weight,
    query_norm,
    key_norm,
    mixture_gain,
    router_weight,
    gate_weight,
    up_weight,
    down_weight,
    segments,
    positions,
    priority,
    routes,
):
    tok_dev, width = tokens.shape
    experts_here = gate_weight.shape[0]
    ways = lax.axis_size("expert")
    z = lax.axis_index("expert")
    cols = width // ways
    first_row = z * tok_dev

    small = jnp.concatenate(
        [attention_gain[:, None], query_norm[:, None], key_norm[:, None], mixture_gain[:, None], router_weight],
        axis=1,
    )
    small = jnp.pad(small, ((0, 0), (0, SMALL - small.shape[1])))
    shard = jnp.stack([query_weight, key_weight, value_weight], axis=1)
    shard = shard.reshape(-1, 3, ways, cols).transpose(2, 0, 1, 3).reshape(ways, -1, 3 * cols)
    rest = jnp.concatenate([out_weight, small], axis=1)
    shard = jnp.concatenate([shard, jnp.broadcast_to(rest[None], (ways,) + rest.shape)], axis=2)
    shard = exchange_z(shard.reshape(-1, shard.shape[-1]), ways, 1)
    dense = lax.all_gather(shard, "dp", axis=0, tiled=True)
    qkv_weight = dense[:, : 3 * cols]
    out_full = dense[:, 3 * cols : 3 * cols + width]
    small = dense[:, 3 * cols + width :]
    attend_gain = small[:, 0].astype(F32)
    mix_gain = small[:, 3].astype(F32)
    router_full = small[:, 4 : 4 + EXPERTS]
    my_gains = lax.dynamic_slice_in_dim(small[:, 1:3], z * cols, cols, axis=0).astype(F32)
    gain_q, gain_k = my_gains[:, 0][None], my_gains[:, 1][None]
    out_mine = lax.dynamic_slice_in_dim(out_full, z * cols, cols, axis=0)
    tokens_all = ag_z(tokens, ways, 2)
    gate_full = lax.all_gather(gate_weight, "dp", axis=1, tiled=True)
    up_full = lax.all_gather(up_weight, "dp", axis=1, tiled=True)
    down_full = lax.all_gather(down_weight, "dp", axis=1, tiled=True)
    steps = [ways // 2, (3 * ways) // 4]
    early, tokens_all = lax.optimization_barrier((cotangent, tokens_all))
    sent = hops([early], [early], steps[0] - 1, ways)

    segs, places = segments[0], positions[0]
    order = block_order(segs, places)
    frequency = 10000.0 ** (-jnp.arange(0, HEAD_DIM // 2, dtype=F32) * 2.0 / HEAD_DIM)
    angles = places.astype(F32)[:, None] * frequency[None, :]
    cos, sin = jnp.cos(angles), jnp.sin(angles)
    cos = jnp.concatenate([cos, cos], axis=1)
    sin = jnp.concatenate([-sin, sin], axis=1)
    hits, slot = slots(routes[0], priority[0])
    my_hits = lax.dynamic_slice_in_dim(hits, z * experts_here, experts_here, axis=1)
    my_slot = lax.dynamic_slice_in_dim(slot, z * experts_here, experts_here, axis=1)
    my_slot = jnp.where(my_hits & (my_slot < CAP), my_slot, -1)
    chosen = my_slot.T[:, None, :] == jnp.arange(CAP, dtype=jnp.int32)[None, :, None]
    pick = chosen.astype(BF16)

    token_f = tokens_all.astype(F32)
    inverse_in = lax.rsqrt(jnp.mean(token_f * token_f, axis=-1, keepdims=True) + EPS)
    normed = (token_f * inverse_in * attend_gain).astype(BF16)
    qkv = plain(normed, qkv_weight)
    squares = jnp.sum(jnp.square(qkv[:, : 2 * cols]).reshape(GTOK, 2, cols), axis=-1)
    squares = sum_z(jnp.pad(squares.T, ((0, 6), (0, 0))), ways, 3)
    inv_q = lax.rsqrt(squares[0] / width + EPS)[:, None]
    inv_k = lax.rsqrt(squares[1] / width + EPS)[:, None]
    q_rot, k_rot, v_b, mixed_heads, lse = attend(order, qkv, inv_q, inv_k, gain_q, gain_k, cos, sin)
    mixed = a2a_z(mixed_heads, ways, 4)
    own_f = tokens.astype(F32)
    resid = own_f + plain(mixed, out_full)
    mix_inverse = lax.rsqrt(jnp.mean(resid * resid, axis=-1, keepdims=True) + EPS)
    mix_unit = resid * mix_inverse
    mix = (mix_unit * mix_gain).astype(BF16)
    mix_all = ag_z(mix, ways, 5)
    up, down, mix_all = later(sent, mix_all)
    sent = hops(up, down, steps[1] - steps[0], ways)

    router_all = jax.nn.softmax(plain(mix_all, router_full), axis=-1)
    my_weight = lax.dynamic_slice_in_dim(router_all, z * experts_here, experts_here, axis=1)
    slot_weight = jnp.sum(jnp.where(chosen, my_weight.T[:, None, :], 0.0), axis=-1)
    inputs = jnp.einsum("est,td->esd", pick, mix_all, preferred_element_type=F32).astype(BF16)
    up, down, inputs = later(sent, inputs)
    grad_all = line_up(*hops(up, down, ways - steps[1], ways), ways)
    gate_pre = jnp.einsum("esd,edf->esf", inputs, gate_full, preferred_element_type=F32)
    up_pre = jnp.einsum("esd,edf->esf", inputs, up_full, preferred_element_type=F32)
    sig = jax.nn.sigmoid(gate_pre)
    silu = gate_pre * sig
    hidden = (silu * up_pre).astype(BF16)
    grad_slots = jnp.einsum("est,td->esd", pick, grad_all, preferred_element_type=F32)
    grad_eo = (grad_slots * slot_weight[:, :, None]).astype(BF16)
    grad_down = jnp.einsum("esf,esd->efd", hidden, grad_eo, preferred_element_type=F32).astype(BF16)
    grad_eo, grad_down = lax.optimization_barrier((grad_eo, grad_down))
    out_down = lax.psum_scatter(grad_down, "dp", scatter_dimension=1, tiled=True).astype(F32)
    grad_hidden = jnp.einsum("esd,efd->esf", grad_eo, down_full, preferred_element_type=F32)
    grad_gate = (grad_hidden * up_pre * (sig * (1.0 + gate_pre * (1.0 - sig)))).astype(BF16)
    grad_up = (grad_hidden * silu).astype(BF16)
    grad_gate_w = jnp.einsum("esd,esf->edf", inputs, grad_gate, preferred_element_type=F32).astype(BF16)
    grad_gate, grad_up, grad_gate_w = lax.optimization_barrier((grad_gate, grad_up, grad_gate_w))
    out_gate = lax.psum_scatter(grad_gate_w, "dp", scatter_dimension=1, tiled=True).astype(F32)
    grad_up_w = jnp.einsum("esd,esf->edf", inputs, grad_up, preferred_element_type=F32).astype(BF16)
    grad_gate, grad_up, hidden, grad_up_w = lax.optimization_barrier((grad_gate, grad_up, hidden, grad_up_w))
    out_up = lax.psum_scatter(grad_up_w, "dp", scatter_dimension=1, tiled=True).astype(F32)

    expert_out = jnp.einsum("esf,efd->esd", hidden, down_full, preferred_element_type=F32).astype(BF16)
    slot_dots = jnp.sum(grad_slots * expert_out.astype(F32), axis=-1)
    my_route_grad = jnp.sum(jnp.where(chosen, slot_dots[:, :, None], 0.0), axis=1)
    route_grad = lax.all_to_all(my_route_grad, "expert", split_axis=1, concat_axis=0, tiled=True).T
    grad_in = (
        jnp.einsum("esf,edf->esd", grad_gate, gate_full, preferred_element_type=F32)
        + jnp.einsum("esf,edf->esd", grad_up, up_full, preferred_element_type=F32)
    ).astype(BF16)
    part = cross_rows(
        pick.reshape(experts_here * CAP, GTOK), grad_in.reshape(experts_here * CAP, width)
    ).astype(BF16)
    grad_routed = rs_z(part, ways, 6).astype(F32)
    spread = jnp.where(chosen, my_weight.T[:, None, :], 0.0).astype(BF16).reshape(experts_here * CAP, GTOK)
    part = cross_rows(spread, expert_out.reshape(experts_here * CAP, width)).astype(BF16)
    moe = lax.psum_scatter(part, "expert", scatter_dimension=0, tiled=True)
    output = (resid + moe.astype(F32)).astype(BF16)

    router = lax.dynamic_slice_in_dim(router_all, first_row, tok_dev, axis=0)
    grad_logits = (router * (route_grad - jnp.sum(router * route_grad, axis=-1, keepdims=True))).astype(BF16)
    grad_router_w = cross_rows(mix, grad_logits)
    grad_mix = grad_routed + by_transpose(grad_logits, router_full)
    grad_mix_gain = jnp.sum(grad_mix * mix_unit, axis=0)
    grad_resid = cotangent.astype(F32) + norm_back(grad_mix, mix_unit, mix_inverse, mix_gain)
    grad_branch = grad_resid.astype(BF16)
    branch_all = ag_z(grad_branch, ways, 7)
    grad_heads = by_transpose(branch_all, out_mine).astype(BF16)
    grad_out_w = cross_rows(mixed_heads, branch_all).astype(BF16)
    out_out = lax.psum_scatter(grad_out_w, "dp", scatter_dimension=0, tiled=True)
    out_out = lax.ppermute(out_out, BOTH, row_moves(ways, lax.axis_size("dp"))).astype(F32)

    dq, dk, dv = attend_back(order, q_rot, k_rot, v_b, lse, grad_heads, cos, sin)
    q_unit = qkv[:, :cols] * inv_q
    k_unit = qkv[:, cols : 2 * cols] * inv_k
    inner = jnp.stack(
        [jnp.sum(dq * gain_q * q_unit, axis=-1), jnp.sum(dk * gain_k * k_unit, axis=-1)], axis=0
    )
    inner = sum_z(jnp.pad(inner, ((0, 6), (0, 0))), ways, 8) / width
    grad_q_gain = jnp.sum(dq * q_unit, axis=0)
    grad_k_gain = jnp.sum(dk * k_unit, axis=0)
    grad_q = (inv_q * (dq * gain_q - q_unit * inner[0][:, None])).astype(BF16)
    grad_k = (inv_k * (dk * gain_k - k_unit * inner[1][:, None])).astype(BF16)
    grad_qkv = jnp.concatenate([grad_q, grad_k, dv], axis=1)
    grad_normed_part = by_transpose(grad_qkv, qkv_weight)
    grad_attend_gain = jnp.sum(grad_normed_part * (token_f * inverse_in), axis=0)
    grad_normed = rs_z(grad_normed_part.astype(BF16), ways, 9).astype(F32)
    own_inverse = lax.dynamic_slice_in_dim(inverse_in, first_row, tok_dev, axis=0)
    input_grad = grad_resid + norm_back(grad_normed, own_f * own_inverse, own_inverse, attend_gain)

    place = lambda part: lax.dynamic_update_slice(jnp.zeros((width,), F32), part, (z * cols,))
    extra = jnp.concatenate(
        [
            jnp.stack([grad_attend_gain, place(grad_q_gain), place(grad_k_gain), grad_mix_gain], axis=1),
            grad_router_w,
            jnp.zeros((width, SMALL - 4 - EXPERTS), F32),
        ],
        axis=1,
    )
    grad_qkv_w = jnp.concatenate([cross_rows(normed, grad_qkv), extra], axis=1).astype(BF16)
    grad_qkv_w = lax.psum_scatter(grad_qkv_w, "dp", scatter_dimension=0, tiled=True)
    grad_qkv_w = exchange_z(grad_qkv_w, ways, 10).reshape(ways, -1, 3 * cols + SMALL)
    grad_w = [
        grad_qkv_w[:, :, i * cols : (i + 1) * cols].transpose(1, 0, 2).reshape(-1, width).astype(F32)
        for i in range(3)
    ]
    packed = jnp.sum(grad_qkv_w[:, :, 3 * cols :].astype(F32), axis=0)
    return (
        output,
        input_grad,
        packed[:, 0],
        grad_w[0],
        grad_w[1],
        grad_w[2],
        out_out,
        packed[:, 1],
        packed[:, 2],
        packed[:, 3],
        packed[:, 4 : 4 + EXPERTS],
        out_gate,
        out_up,
        out_down,
    )


def solution(mesh):
    rows = P(BOTH, None)
    vec = P(BOTH)
    expert = P("expert", "dp", None)
    group = P("dp", None)
    return jax.shard_map(
        body,
        mesh=mesh,
        in_specs=(rows, rows, vec, rows, rows, rows, rows, vec, vec, vec, rows, expert, expert, expert)
        + (group, group, group, P("dp", None, None)),
        out_specs=(rows, rows, vec, rows, rows, rows, rows, vec, vec, vec, rows, expert, expert, expert),
        check_vma=False,
    )
```

```python
import functools

import jax
import jax.numpy as jnp
from jax import lax
from jax.experimental import pallas as pl
from jax.experimental.pallas import tpu as pltpu
from jax.sharding import PartitionSpec as P

HEADS = 16
HEAD_DIM = 128
TOPK = 8
EXPERTS = 16
GTOK = 1536
CAP = 768
PROMPT = 1024
CLEN = 128
BLOCKS = GTOK // CLEN
TILE = 256
EPS = 1e-05
BOTH = ("dp", "expert")
F32 = jnp.float32
BF16 = jnp.bfloat16
SCALE = HEAD_DIM ** (-0.5)
NEG = -1e30
SMALL = 128
MESH = pl.DeviceIdType.MESH


def norm_back(grad_rows, unit_rows, inverse, gain_vec):
    grad_unit = grad_rows * gain_vec
    inner_mean = jnp.mean(grad_unit * unit_rows, axis=-1, keepdims=True)
    return inverse * (grad_unit - unit_rows * inner_mean)


def cross_rows(left, right):
    return lax.dot_general(left, right, (((0,), (0,)), ((), ())), preferred_element_type=F32)


def by_transpose(left, right):
    return lax.dot_general(left, right, (((1,), (1,)), ((), ())), preferred_element_type=F32)


def plain(left, right):
    return lax.dot_general(left, right, (((1,), (0,)), ((), ())), preferred_element_type=F32)


def causal(rows):
    return lax.broadcasted_iota(jnp.int32, (rows, rows), 1) <= lax.broadcasted_iota(
        jnp.int32, (rows, rows), 0
    )


def tiles():
    out = []
    for i in range(PROMPT // TILE):
        keys = [(0, i * TILE, False)] if i else []
        out.append((i * TILE, TILE, keys + [(i * TILE, TILE, True)]))
    for c in range(PROMPT // CLEN, BLOCKS):
        out.append((c * CLEN, CLEN, [(0, PROMPT, False), (c * CLEN, CLEN, True)]))
    return out


def rope(values, cos_rows, sin_rows):
    return values * cos_rows + pltpu.roll(values, HEAD_DIM // 2, 1) * sin_rows


def attend_kernel(
    order, q_pre, k_pre, v_pre, inv_q, inv_k, gain_q, gain_k, cos, sin, q_rot, k_rot, v_out, mixed, lse
):
    for i in range(BLOCKS):
        here = pl.ds(i * CLEN, CLEN)
        there = pl.ds(pl.multiple_of(order[i] * CLEN, CLEN), CLEN)
        cos_rows, sin_rows = cos[there, :], sin[there, :]
        q_n = q_pre[there, :] * inv_q[there, :] * gain_q[...]
        k_n = k_pre[there, :] * inv_k[there, :] * gain_k[...]
        q_rot[here, :] = rope(q_n, cos_rows, sin_rows).astype(BF16)
        k_rot[here, :] = rope(k_n, cos_rows, sin_rows).astype(BF16)
        v_out[here, :] = v_pre[there, :].astype(BF16)
    for start, rows, keys in tiles():
        q = q_rot[pl.ds(start, rows), :]
        parts = []
        for k_start, k_rows, masked in keys:
            s = by_transpose(q, k_rot[pl.ds(k_start, k_rows), :]) * SCALE
            parts.append(jnp.where(causal(rows), s, NEG) if masked else s)
        top = functools.reduce(jnp.maximum, [jnp.max(s, axis=1, keepdims=True) for s in parts])
        exps = [jnp.exp(s - top) for s in parts]
        total = functools.reduce(lambda a, b: a + b, [jnp.sum(e, axis=1, keepdims=True) for e in exps])
        over = 1.0 / total
        result = None
        for e, (k_start, k_rows, _) in zip(exps, keys):
            term = plain((e * over).astype(BF16), v_out[pl.ds(k_start, k_rows), :])
            result = term if result is None else result + term
        lse[pl.ds(start, rows), :] = jnp.broadcast_to(top + jnp.log(total), (rows, HEAD_DIM))
        for j in range(rows // CLEN):
            block = start // CLEN + j
            there = pl.ds(pl.multiple_of(order[block] * CLEN, CLEN), CLEN)
            mixed[there, :] = result[j * CLEN : (j + 1) * CLEN].astype(BF16)


def attend(order, qkv, inv_q, inv_k, gain_q, gain_k, cos, sin):
    heads = qkv.shape[1] // (3 * HEAD_DIM)
    head = lambda off: pl.BlockSpec((GTOK, HEAD_DIM), lambda h, o: (0, h + off))
    whole = lambda w: pl.BlockSpec((GTOK, w), lambda h, o: (0, 0))
    gain = pl.BlockSpec((1, HEAD_DIM), lambda h, o: (0, h))
    wide = jax.ShapeDtypeStruct((GTOK, heads * HEAD_DIM), BF16)
    return pl.pallas_call(
        attend_kernel,
        grid_spec=pltpu.PrefetchScalarGridSpec(
            num_scalar_prefetch=1,
            grid=(heads,),
            in_specs=[head(0), head(heads), head(2 * heads), whole(1), whole(1), gain, gain]
            + [whole(HEAD_DIM)] * 2,
            out_specs=[head(0)] * 5,
        ),
        out_shape=[wide] * 4 + [jax.ShapeDtypeStruct((GTOK, heads * HEAD_DIM), F32)],
        compiler_params=pltpu.CompilerParams(vmem_limit_bytes=48 * 2**20),
    )(order, qkv, qkv, qkv, inv_q, inv_k, gain_q, gain_k, cos, sin)


def attend_back_kernel(
    order, q_rot, k_rot, v_in, lse, grad_mixed, cos, sin, dq_out, dk_out, dv_out, grads, dq, dk, dv
):
    for i in range(BLOCKS):
        there = pl.ds(pl.multiple_of(order[i] * CLEN, CLEN), CLEN)
        grads[pl.ds(i * CLEN, CLEN), :] = grad_mixed[there, :]
    dk[...] = jnp.zeros_like(dk)
    dv[...] = jnp.zeros_like(dv)
    for start, rows, keys in tiles():
        here = pl.ds(start, rows)
        q, g, level = q_rot[here, :], grads[here, :], lse[here, 0:1]
        probs, grad_probs, delta = [], [], 0.0
        for k_start, k_rows, masked in keys:
            s = by_transpose(q, k_rot[pl.ds(k_start, k_rows), :]) * SCALE
            s = jnp.where(causal(rows), s, NEG) if masked else s
            p = jnp.exp(s - level)
            gp = by_transpose(g, v_in[pl.ds(k_start, k_rows), :])
            delta = delta + jnp.sum(p * gp, axis=1, keepdims=True)
            probs.append(p)
            grad_probs.append(gp)
        total = None
        for p, gp, (k_start, k_rows, _) in zip(probs, grad_probs, keys):
            there = pl.ds(k_start, k_rows)
            raw = (p * (gp - delta) * SCALE).astype(BF16)
            term = plain(raw, k_rot[there, :])
            total = term if total is None else total + term
            dk[there, :] += cross_rows(raw, q)
            dv[there, :] += cross_rows(p.astype(BF16), g)
        dq[here, :] = total
    for i in range(BLOCKS):
        here = pl.ds(i * CLEN, CLEN)
        there = pl.ds(pl.multiple_of(order[i] * CLEN, CLEN), CLEN)
        cos_rows, sin_rows = cos[there, :], sin[there, :]
        dq_out[there, :] = rope(dq[here, :], cos_rows, -sin_rows)
        dk_out[there, :] = rope(dk[here, :], cos_rows, -sin_rows)
        dv_out[there, :] = dv[here, :].astype(BF16)


def attend_back(order, q_rot, k_rot, v_in, lse, grad_mixed, cos, sin):
    heads = q_rot.shape[1] // HEAD_DIM
    head = pl.BlockSpec((GTOK, HEAD_DIM), lambda h, o: (0, h))
    whole = pl.BlockSpec((GTOK, HEAD_DIM), lambda h, o: (0, 0))
    wide = lambda t: jax.ShapeDtypeStruct((GTOK, heads * HEAD_DIM), t)
    return pl.pallas_call(
        attend_back_kernel,
        grid_spec=pltpu.PrefetchScalarGridSpec(
            num_scalar_prefetch=1,
            grid=(heads,),
            in_specs=[head] * 5 + [whole] * 2,
            out_specs=[head] * 3,
            scratch_shapes=[
                pltpu.VMEM((GTOK, HEAD_DIM), BF16),
                pltpu.VMEM((GTOK, HEAD_DIM), F32),
                pltpu.VMEM((GTOK, HEAD_DIM), F32),
                pltpu.VMEM((GTOK, HEAD_DIM), F32),
            ],
        ),
        out_shape=[wide(F32), wide(F32), wide(BF16)],
        compiler_params=pltpu.CompilerParams(vmem_limit_bytes=48 * 2**20),
    )(order, q_rot, k_rot, v_in, lse, grad_mixed, cos, sin)


ANY=pl.BlockSpec(memory_space=pl.ANY); VM=pl.BlockSpec(memory_space=pltpu.VMEM)

def peer(i): return {"expert": i}

def greet_line(n):
    p=lax.axis_index("expert")
    bar=pltpu.get_barrier_semaphore()
    @pl.when(p>0)
    def _(): pl.semaphore_signal(bar,inc=1,device_id=peer(p-1))
    @pl.when(p<n-1)
    def _(): pl.semaphore_signal(bar,inc=1,device_id=peer(p+1))
    pl.semaphore_wait(bar,(p>0).astype(jnp.int32)+(p<n-1).astype(jnp.int32))
    return p

def greet_all(n):
    p=lax.axis_index("expert")
    bar=pltpu.get_barrier_semaphore()
    for s in range(1,n): pl.semaphore_signal(bar,inc=1,device_id=peer(lax.rem(p+s,n)))
    pl.semaphore_wait(bar,n-1)
    return p

def params(cid,mb=60): return pltpu.CompilerParams(collective_id=cid,has_side_effects=True,vmem_limit_bytes=mb*2**20)

def ag_kernel(n,rows,x,out,to_right,to_left,recv,local):
    p=greet_line(n)
    at=lambda j: out.at[pl.ds(pl.multiple_of(j*rows,rows),rows)]
    own=pltpu.make_async_copy(x,at(p),local); own.start()
    def copy(src,j,sems,q):
        return pltpu.make_async_remote_copy(src_ref=src,dst_ref=at(j),send_sem=sems.at[j],recv_sem=recv.at[j],device_id=peer(q),device_id_type=MESH)
    right=lambda src,j: copy(src,j,to_right,p+1)
    left=lambda src,j: copy(src,j,to_left,p-1)
    @pl.when(p<n-1)
    def _(): right(x,p).start()
    @pl.when(p>0)
    def _(): left(x,p).start()
    for s in range(1,n):
        j=p-s
        @pl.when(j>=0)
        def _():
            right(at(j),j).wait_recv()
            @pl.when(p<n-1)
            def _(): right(at(j),j).start()
        k=p+s
        @pl.when(k<n)
        def _():
            left(at(k),k).wait_recv()
            @pl.when(p>0)
            def _(): left(at(k),k).start()
    own.wait()
    for j in range(n):
        @pl.when((j<=p)&(p<n-1))
        def _(): right(x,j).wait_send()
        @pl.when((j>=p)&(p>0))
        def _(): left(x,j).wait_send()

def ag_z(x,n,cid):
    rows=x.shape[0]
    return pl.pallas_call(functools.partial(ag_kernel,n,rows),out_shape=jax.ShapeDtypeStruct((n*rows,)+x.shape[1:],x.dtype),
        in_specs=[ANY],out_specs=ANY,scratch_shapes=[pltpu.SemaphoreType.DMA((n,))]*3+[pltpu.SemaphoreType.DMA],
        compiler_params=params(cid))(x)

def rs_kernel(n,rows,C,depth,part,out,from_left,from_right,to_right,to_left,recv_r,recv_l):
    p=greet_line(n)
    size=rows//C
    def at(j,c): return part.at[pl.ds(pl.multiple_of(j*rows+c*size,size),size)]
    def right(j,c): return pltpu.make_async_remote_copy(src_ref=at(j,c),dst_ref=from_left.at[j*C+c],send_sem=to_right.at[j*C+c],recv_sem=recv_r.at[j*C+c],device_id=peer(p+1),device_id_type=MESH)
    def left(j,c): return pltpu.make_async_remote_copy(src_ref=at(j,c),dst_ref=from_right.at[j*C+c],send_sem=to_left.at[j*C+c],recv_sem=recv_l.at[j*C+c],device_id=peer(p-1),device_id_type=MESH)
    def add(j,c,buf):
        at(j,c)[...]=(at(j,c)[...].astype(F32)+buf[j*C+c].astype(F32)).astype(BF16)
    order=[(s,c) for s in range(n-1) for c in range(C)]
    for m,(s,c) in enumerate(order):
        j=n-1-s
        @pl.when(j>p)
        def _():
            @pl.when(p>0)
            def _():
                right(j,c).wait_recv(); add(j,c,from_left)
            if m>=depth:
                s0,c0=order[m-depth]
                right(n-1-s0,c0).wait_send()
            right(j,c).start()
        k=s
        @pl.when(k<p)
        def _():
            @pl.when(p<n-1)
            def _():
                left(k,c).wait_recv(); add(k,c,from_right)
            if m>=depth:
                s0,c0=order[m-depth]
                left(s0,c0).wait_send()
            left(k,c).start()
    for c in range(C):
        @pl.when(p>0)
        def _():
            right(p,c).wait_recv(); add(p,c,from_left)
        @pl.when(p<n-1)
        def _():
            left(p,c).wait_recv(); add(p,c,from_right)
        out[pl.ds(c*size,size)]=at(p,c)[...]
    for m,(s,c) in enumerate(order):
        j=n-1-s
        last_r=(n-1-p)*C
        @pl.when((j>p)&(m>=last_r-depth))
        def _(): right(j,c).wait_send()
        last_l=p*C
        @pl.when((s<p)&(m>=last_l-depth))
        def _(): left(s,c).wait_send()

def rs_z(part,n,cid,C=4,depth=2):
    rows=part.shape[0]//n; D=part.shape[1]
    return pl.pallas_call(functools.partial(rs_kernel,n,rows,C,depth),out_shape=jax.ShapeDtypeStruct((rows,D),BF16),
        in_specs=[VM],out_specs=VM,scratch_shapes=[pltpu.VMEM((n*C,rows//C,D),BF16)]*2+[pltpu.SemaphoreType.DMA((n*C,))]*4,
        compiler_params=params(cid))(part)

def a2a_kernel(n,rows,cols,x,out,send,recv,local):
    p=greet_all(n)
    src=lambda j: x.at[pl.ds(pl.multiple_of(j*rows,rows),rows)]
    dst=lambda c: out.at[:,pl.ds(pl.multiple_of(c*cols,cols),cols)]
    own=pltpu.make_async_copy(src(p),dst(p),local); own.start()
    def send_to(s):
        j=lax.rem(p+s,n)
        return pltpu.make_async_remote_copy(src_ref=src(j),dst_ref=dst(p),send_sem=send.at[s],recv_sem=recv.at[s],device_id=peer(j),device_id_type=MESH)
    for s in range(1,n): send_to(s).start()
    for s in range(1,n):
        c=lax.rem(p-s+n,n)
        pltpu.make_async_remote_copy(src_ref=src(p),dst_ref=dst(c),send_sem=send.at[s],recv_sem=recv.at[s],device_id=peer(c),device_id_type=MESH).wait_recv()
    for s in range(1,n): send_to(s).wait_send()
    own.wait()

def a2a_z(x,n,cid):
    rows=x.shape[0]//n; cols=x.shape[1]
    return pl.pallas_call(functools.partial(a2a_kernel,n,rows,cols),out_shape=jax.ShapeDtypeStruct((rows,n*cols),x.dtype),
        in_specs=[ANY],out_specs=ANY,scratch_shapes=[pltpu.SemaphoreType.DMA((n,))]*2+[pltpu.SemaphoreType.DMA],
        compiler_params=params(cid))(x)

def exchange_kernel(n, rows, x, out, send, recv, local):
    p = greet_all(n)
    at = lambda ref, j: ref.at[pl.ds(pl.multiple_of(j * rows, rows), rows)]
    own = pltpu.make_async_copy(at(x, p), at(out, p), local)
    own.start()

    def to(s):
        j = lax.rem(p + s, n)
        return pltpu.make_async_remote_copy(
            src_ref=at(x, j), dst_ref=at(out, p), send_sem=send.at[s], recv_sem=recv.at[s], device_id=peer(j),
            device_id_type=MESH,
        )

    for s in range(1, n):
        to(s).start()
    for s in range(1, n):
        to(s).wait_recv()
    for s in range(1, n):
        to(s).wait_send()
    own.wait()


def exchange_z(x, n, cid):
    return pl.pallas_call(
        functools.partial(exchange_kernel, n, x.shape[0] // n),
        out_shape=jax.ShapeDtypeStruct(x.shape, x.dtype),
        in_specs=[ANY],
        out_specs=ANY,
        scratch_shapes=[pltpu.SemaphoreType.DMA((n,))] * 2 + [pltpu.SemaphoreType.DMA],
        compiler_params=params(cid),
    )(x)


def sum_kernel(n,x,out,got,send,recv):
    p=greet_all(n)
    def send_to(s):
        return pltpu.make_async_remote_copy(src_ref=x,dst_ref=got.at[s],send_sem=send.at[s],recv_sem=recv.at[s],device_id=peer(lax.rem(p+s,n)),device_id_type=MESH)
    for s in range(1,n): send_to(s).start()
    tot=x[...]
    for s in range(1,n):
        send_to(s).wait_recv(); tot=tot+got[s]
    out[...]=tot
    for s in range(1,n): send_to(s).wait_send()

def sum_z(x,n,cid):
    return pl.pallas_call(functools.partial(sum_kernel,n),out_shape=jax.ShapeDtypeStruct(x.shape,x.dtype),in_specs=[VM],out_specs=VM,
        scratch_shapes=[pltpu.VMEM((n,)+x.shape,x.dtype)]+[pltpu.SemaphoreType.DMA((n,))]*2,compiler_params=params(cid))(x)


def row_moves(ways, dp):
    return [(d * ways + z, z * dp + d) for d in range(dp) for z in range(ways)]


def hops(up, down, count, ways):
    for _ in range(count):
        up = up + [lax.ppermute(up[-1], "expert", [(i, i + 1) for i in range(ways - 1)])]
        down = down + [lax.ppermute(down[-1], "expert", [(i + 1, i) for i in range(ways - 1)])]
    return up, down


def later(sent, other):
    up, down = sent
    last_up, last_down, other = lax.optimization_barrier((up[-1], down[-1], other))
    return up[:-1] + [last_up], down[:-1] + [last_down], other


def line_up(up, down, ways):
    line = jnp.concatenate(up[:0:-1] + down, axis=0)
    rows = down[0].shape[0]
    start = (ways - 1 - lax.axis_index("expert")) * rows
    return lax.dynamic_slice_in_dim(line, start, ways * rows, axis=0)


def block_order(segs, places):
    seg = segs.reshape(BLOCKS, CLEN)[:, 0]
    place = places.reshape(BLOCKS, CLEN)[:, 0]
    stand = jnp.where(seg == 0, place // CLEN, PROMPT // CLEN - 1 + seg)
    blocks = jnp.arange(BLOCKS, dtype=jnp.int32)
    return jnp.sum(jnp.where(stand[None, :] == blocks[:, None], blocks[None, :], 0), axis=1)


def slots(routes, priority):
    experts = jnp.arange(EXPERTS, dtype=jnp.int32)
    hits = jnp.any(routes[:, :, None] == experts[None, None, :], axis=1)
    index = jnp.arange(GTOK, dtype=jnp.int32)
    rank = jnp.sum(jnp.where(priority[:, None] == index[None, :], index[:, None], 0), axis=0)
    earlier = (rank[None, :] < rank[:, None]).astype(BF16)
    return hits, plain(earlier, hits.astype(BF16)).astype(jnp.int32)


def body(
    tokens,
    cotangent,
    attention_gain,
    query_weight,
    key_weight,
    value_weight,
    out_weight,
    query_norm,
    key_norm,
    mixture_gain,
    router_weight,
    gate_weight,
    up_weight,
    down_weight,
    segments,
    positions,
    priority,
    routes,
):
    tok_dev, width = tokens.shape
    experts_here = gate_weight.shape[0]
    ways = lax.axis_size("expert")
    z = lax.axis_index("expert")
    cols = width // ways
    first_row = z * tok_dev

    small = jnp.concatenate(
        [attention_gain[:, None], query_norm[:, None], key_norm[:, None], mixture_gain[:, None], router_weight],
        axis=1,
    )
    small = jnp.pad(small, ((0, 0), (0, SMALL - small.shape[1])))
    shard = jnp.stack([query_weight, key_weight, value_weight], axis=1)
    shard = shard.reshape(-1, 3, ways, cols).transpose(2, 0, 1, 3).reshape(ways, -1, 3 * cols)
    shard = jnp.concatenate([shard, jnp.broadcast_to(small[None], (ways,) + small.shape)], axis=2)
    shard = exchange_z(shard.reshape(-1, shard.shape[-1]), ways, 1)
    dense = lax.all_gather(shard, "dp", axis=0, tiled=True)
    qkv_weight = dense[:, : 3 * cols]
    small = dense[:, 3 * cols :]
    shard, out_weight, gate_weight, up_weight, down_weight = lax.optimization_barrier(
        (shard, out_weight, gate_weight, up_weight, down_weight)
    )
    out_full = lax.all_gather(out_weight, BOTH, axis=0, tiled=True)
    attend_gain = small[:, 0].astype(F32)
    mix_gain = small[:, 3].astype(F32)
    router_full = small[:, 4 : 4 + EXPERTS]
    my_gains = lax.dynamic_slice_in_dim(small[:, 1:3], z * cols, cols, axis=0).astype(F32)
    gain_q, gain_k = my_gains[:, 0][None], my_gains[:, 1][None]
    out_mine = lax.dynamic_slice_in_dim(out_full, z * cols, cols, axis=0)
    tokens_all = ag_z(tokens, ways, 2)
    gate_full = lax.all_gather(gate_weight, "dp", axis=1, tiled=True)
    up_full = lax.all_gather(up_weight, "dp", axis=1, tiled=True)
    down_full = lax.all_gather(down_weight, "dp", axis=1, tiled=True)
    steps = [ways // 2, (3 * ways) // 4]
    early, tokens_all = lax.optimization_barrier((cotangent, tokens_all))
    sent = hops([early], [early], steps[0] - 1, ways)

    segs, places = segments[0], positions[0]
    order = block_order(segs, places)
    frequency = 10000.0 ** (-jnp.arange(0, HEAD_DIM // 2, dtype=F32) * 2.0 / HEAD_DIM)
    angles = places.astype(F32)[:, None] * frequency[None, :]
    cos, sin = jnp.cos(angles), jnp.sin(angles)
    cos = jnp.concatenate([cos, cos], axis=1)
    sin = jnp.concatenate([-sin, sin], axis=1)
    hits, slot = slots(routes[0], priority[0])
    my_hits = lax.dynamic_slice_in_dim(hits, z * experts_here, experts_here, axis=1)
    my_slot = lax.dynamic_slice_in_dim(slot, z * experts_here, experts_here, axis=1)
    my_slot = jnp.where(my_hits & (my_slot < CAP), my_slot, -1)
    chosen = my_slot.T[:, None, :] == jnp.arange(CAP, dtype=jnp.int32)[None, :, None]
    pick = chosen.astype(BF16)

    token_f = tokens_all.astype(F32)
    inverse_in = lax.rsqrt(jnp.mean(token_f * token_f, axis=-1, keepdims=True) + EPS)
    normed = (token_f * inverse_in * attend_gain).astype(BF16)
    qkv = plain(normed, qkv_weight)
    squares = jnp.sum(jnp.square(qkv[:, : 2 * cols]).reshape(GTOK, 2, cols), axis=-1)
    squares = sum_z(jnp.pad(squares.T, ((0, 6), (0, 0))), ways, 3)
    inv_q = lax.rsqrt(squares[0] / width + EPS)[:, None]
    inv_k = lax.rsqrt(squares[1] / width + EPS)[:, None]
    q_rot, k_rot, v_b, mixed_heads, lse = attend(order, qkv, inv_q, inv_k, gain_q, gain_k, cos, sin)
    mixed = a2a_z(mixed_heads, ways, 4)
    own_f = tokens.astype(F32)
    resid = own_f + plain(mixed, out_full)
    mix_inverse = lax.rsqrt(jnp.mean(resid * resid, axis=-1, keepdims=True) + EPS)
    mix_unit = resid * mix_inverse
    mix = (mix_unit * mix_gain).astype(BF16)
    mix_all = ag_z(mix, ways, 5)
    up, down, mix_all = later(sent, mix_all)
    sent = hops(up, down, steps[1] - steps[0], ways)

    router_all = jax.nn.softmax(plain(mix_all, router_full), axis=-1)
    my_weight = lax.dynamic_slice_in_dim(router_all, z * experts_here, experts_here, axis=1)
    slot_weight = jnp.sum(jnp.where(chosen, my_weight.T[:, None, :], 0.0), axis=-1)
    inputs = jnp.einsum("est,td->esd", pick, mix_all, preferred_element_type=F32).astype(BF16)
    up, down, inputs = later(sent, inputs)
    grad_all = line_up(*hops(up, down, ways - steps[1], ways), ways)
    gate_pre = jnp.einsum("esd,edf->esf", inputs, gate_full, preferred_element_type=F32)
    up_pre = jnp.einsum("esd,edf->esf", inputs, up_full, preferred_element_type=F32)
    sig = jax.nn.sigmoid(gate_pre)
    silu = gate_pre * sig
    hidden = (silu * up_pre).astype(BF16)
    grad_slots = jnp.einsum("est,td->esd", pick, grad_all, preferred_element_type=F32)
    grad_eo = (grad_slots * slot_weight[:, :, None]).astype(BF16)
    grad_down = jnp.einsum("esf,esd->efd", hidden, grad_eo, preferred_element_type=F32).astype(BF16)
    grad_eo, grad_down = lax.optimization_barrier((grad_eo, grad_down))
    out_down = lax.psum_scatter(grad_down, "dp", scatter_dimension=1, tiled=True).astype(F32)
    grad_hidden = jnp.einsum("esd,efd->esf", grad_eo, down_full, preferred_element_type=F32)
    grad_gate = (grad_hidden * up_pre * (sig * (1.0 + gate_pre * (1.0 - sig)))).astype(BF16)
    grad_up = (grad_hidden * silu).astype(BF16)
    grad_gate_w = jnp.einsum("esd,esf->edf", inputs, grad_gate, preferred_element_type=F32).astype(BF16)
    grad_gate, grad_up, grad_gate_w = lax.optimization_barrier((grad_gate, grad_up, grad_gate_w))
    out_gate = lax.psum_scatter(grad_gate_w, "dp", scatter_dimension=1, tiled=True).astype(F32)
    grad_up_w = jnp.einsum("esd,esf->edf", inputs, grad_up, preferred_element_type=F32).astype(BF16)
    grad_gate, grad_up, hidden, grad_up_w = lax.optimization_barrier((grad_gate, grad_up, hidden, grad_up_w))
    out_up = lax.psum_scatter(grad_up_w, "dp", scatter_dimension=1, tiled=True).astype(F32)

    expert_out = jnp.einsum("esf,efd->esd", hidden, down_full, preferred_element_type=F32).astype(BF16)
    slot_dots = jnp.sum(grad_slots * expert_out.astype(F32), axis=-1)
    my_route_grad = jnp.sum(jnp.where(chosen, slot_dots[:, :, None], 0.0), axis=1)
    route_grad = lax.all_to_all(my_route_grad, "expert", split_axis=1, concat_axis=0, tiled=True).T
    grad_in = (
        jnp.einsum("esf,edf->esd", grad_gate, gate_full, preferred_element_type=F32)
        + jnp.einsum("esf,edf->esd", grad_up, up_full, preferred_element_type=F32)
    ).astype(BF16)
    part = cross_rows(
        pick.reshape(experts_here * CAP, GTOK), grad_in.reshape(experts_here * CAP, width)
    ).astype(BF16)
    part, out_down = lax.optimization_barrier((part, out_down))
    grad_routed = rs_z(part, ways, 6).astype(F32)
    spread = jnp.where(chosen, my_weight.T[:, None, :], 0.0).astype(BF16).reshape(experts_here * CAP, GTOK)
    part = cross_rows(spread, expert_out.reshape(experts_here * CAP, width)).astype(BF16)
    moe = lax.psum_scatter(part, "expert", scatter_dimension=0, tiled=True)

    router = lax.dynamic_slice_in_dim(router_all, first_row, tok_dev, axis=0)
    grad_logits = (router * (route_grad - jnp.sum(router * route_grad, axis=-1, keepdims=True))).astype(BF16)
    grad_router_w = cross_rows(mix, grad_logits)
    grad_mix = grad_routed + by_transpose(grad_logits, router_full)
    grad_mix_gain = jnp.sum(grad_mix * mix_unit, axis=0)
    grad_resid = cotangent.astype(F32) + norm_back(grad_mix, mix_unit, mix_inverse, mix_gain)
    grad_branch = grad_resid.astype(BF16)
    grad_branch, out_gate = lax.optimization_barrier((grad_branch, out_gate))
    branch_all = ag_z(grad_branch, ways, 7)
    grad_heads = by_transpose(branch_all, out_mine).astype(BF16)
    grad_out_w = cross_rows(mixed_heads, branch_all).astype(BF16)
    out_out = lax.psum_scatter(grad_out_w, "dp", scatter_dimension=0, tiled=True)
    out_out = lax.ppermute(out_out, BOTH, row_moves(ways, lax.axis_size("dp"))).astype(F32)

    grad_heads, out_up = lax.optimization_barrier((grad_heads, out_up))
    dq, dk, dv = attend_back(order, q_rot, k_rot, v_b, lse, grad_heads, cos, sin)
    q_unit = qkv[:, :cols] * inv_q
    k_unit = qkv[:, cols : 2 * cols] * inv_k
    inner = jnp.stack(
        [jnp.sum(dq * gain_q * q_unit, axis=-1), jnp.sum(dk * gain_k * k_unit, axis=-1)], axis=0
    )
    inner = sum_z(jnp.pad(inner, ((0, 6), (0, 0))), ways, 8) / width
    grad_q_gain = jnp.sum(dq * q_unit, axis=0)
    grad_k_gain = jnp.sum(dk * k_unit, axis=0)
    grad_q = (inv_q * (dq * gain_q - q_unit * inner[0][:, None])).astype(BF16)
    grad_k = (inv_k * (dk * gain_k - k_unit * inner[1][:, None])).astype(BF16)
    grad_qkv = jnp.concatenate([grad_q, grad_k, dv], axis=1)
    grad_normed_part = by_transpose(grad_qkv, qkv_weight)
    grad_attend_gain = jnp.sum(grad_normed_part * (token_f * inverse_in), axis=0)
    part, moe = lax.optimization_barrier((grad_normed_part.astype(BF16), moe))
    output = (resid + moe.astype(F32)).astype(BF16)
    grad_normed = rs_z(part, ways, 9).astype(F32)
    own_inverse = lax.dynamic_slice_in_dim(inverse_in, first_row, tok_dev, axis=0)
    input_grad = grad_resid + norm_back(grad_normed, own_f * own_inverse, own_inverse, attend_gain)

    place = lambda part: lax.dynamic_update_slice(jnp.zeros((width,), F32), part, (z * cols,))
    extra = jnp.concatenate(
        [
            jnp.stack([grad_attend_gain, place(grad_q_gain), place(grad_k_gain), grad_mix_gain], axis=1),
            grad_router_w,
            jnp.zeros((width, SMALL - 4 - EXPERTS), F32),
        ],
        axis=1,
    )
    grad_qkv_w = jnp.concatenate([cross_rows(normed, grad_qkv), extra], axis=1).astype(BF16)
    grad_qkv_w = lax.psum_scatter(grad_qkv_w, "dp", scatter_dimension=0, tiled=True)
    grad_qkv_w = exchange_z(grad_qkv_w, ways, 10).reshape(ways, -1, 3 * cols + SMALL)
    grad_w = [
        grad_qkv_w[:, :, i * cols : (i + 1) * cols].transpose(1, 0, 2).reshape(-1, width).astype(F32)
        for i in range(3)
    ]
    packed = jnp.sum(grad_qkv_w[:, :, 3 * cols :].astype(F32), axis=0)
    return (
        output,
        input_grad,
        packed[:, 0],
        grad_w[0],
        grad_w[1],
        grad_w[2],
        out_out,
        packed[:, 1],
        packed[:, 2],
        packed[:, 3],
        packed[:, 4 : 4 + EXPERTS],
        out_gate,
        out_up,
        out_down,
    )


def solution(mesh):
    rows = P(BOTH, None)
    vec = P(BOTH)
    expert = P("expert", "dp", None)
    group = P("dp", None)
    return jax.shard_map(
        body,
        mesh=mesh,
        in_specs=(rows, rows, vec, rows, rows, rows, rows, vec, vec, vec, rows, expert, expert, expert)
        + (group, group, group, P("dp", None, None)),
        out_specs=(rows, rows, vec, rows, rows, rows, rows, vec, vec, vec, rows, expert, expert, expert),
        check_vma=False,
    )
```

```python
import functools

import jax
import jax.numpy as jnp
from jax import lax
from jax.experimental import pallas as pl
from jax.experimental.pallas import tpu as pltpu
from jax.sharding import PartitionSpec as P

HEADS = 16
HEAD_DIM = 128
TOPK = 8
EXPERTS = 16
GTOK = 1536
CAP = 768
PROMPT = 1024
CLEN = 128
BLOCKS = GTOK // CLEN
TILE = 256
ROWS = 768
FTILE = 256
EPS = 1e-05
BOTH = ("dp", "expert")
F32 = jnp.float32
BF16 = jnp.bfloat16
SCALE = HEAD_DIM ** (-0.5)
NEG = -1e30
SMALL = 128
MESH = pl.DeviceIdType.MESH


def norm_back(grad_rows, unit_rows, inverse, gain_vec):
    grad_unit = grad_rows * gain_vec
    inner_mean = jnp.mean(grad_unit * unit_rows, axis=-1, keepdims=True)
    return inverse * (grad_unit - unit_rows * inner_mean)


def cross_rows(left, right):
    return lax.dot_general(left, right, (((0,), (0,)), ((), ())), preferred_element_type=F32)


def by_transpose(left, right):
    return lax.dot_general(left, right, (((1,), (1,)), ((), ())), preferred_element_type=F32)


def plain(left, right):
    return lax.dot_general(left, right, (((1,), (0,)), ((), ())), preferred_element_type=F32)


def causal(rows):
    return lax.broadcasted_iota(jnp.int32, (rows, rows), 1) <= lax.broadcasted_iota(
        jnp.int32, (rows, rows), 0
    )


def tiles():
    out = []
    for i in range(PROMPT // TILE):
        keys = [(0, i * TILE, False)] if i else []
        out.append((i * TILE, TILE, keys + [(i * TILE, TILE, True)]))
    for c in range(PROMPT // CLEN, BLOCKS):
        out.append((c * CLEN, CLEN, [(0, PROMPT, False), (c * CLEN, CLEN, True)]))
    return out


def rope(values, cos_rows, sin_rows):
    return values * cos_rows + pltpu.roll(values, HEAD_DIM // 2, 1) * sin_rows


def attend_kernel(
    order, q_pre, k_pre, v_pre, inv_q, inv_k, gain_q, gain_k, cos, sin, q_rot, k_rot, v_out, mixed, lse
):
    for i in range(BLOCKS):
        here = pl.ds(i * CLEN, CLEN)
        there = pl.ds(pl.multiple_of(order[i] * CLEN, CLEN), CLEN)
        cos_rows, sin_rows = cos[there, :], sin[there, :]
        q_n = q_pre[there, :] * inv_q[there, :] * gain_q[...]
        k_n = k_pre[there, :] * inv_k[there, :] * gain_k[...]
        q_rot[here, :] = rope(q_n, cos_rows, sin_rows).astype(BF16)
        k_rot[here, :] = rope(k_n, cos_rows, sin_rows).astype(BF16)
        v_out[here, :] = v_pre[there, :].astype(BF16)
    for start, rows, keys in tiles():
        q = q_rot[pl.ds(start, rows), :]
        parts = []
        for k_start, k_rows, masked in keys:
            s = by_transpose(q, k_rot[pl.ds(k_start, k_rows), :]) * SCALE
            parts.append(jnp.where(causal(rows), s, NEG) if masked else s)
        top = functools.reduce(jnp.maximum, [jnp.max(s, axis=1, keepdims=True) for s in parts])
        exps = [jnp.exp(s - top) for s in parts]
        total = functools.reduce(lambda a, b: a + b, [jnp.sum(e, axis=1, keepdims=True) for e in exps])
        over = 1.0 / total
        result = None
        for e, (k_start, k_rows, _) in zip(exps, keys):
            term = plain((e * over).astype(BF16), v_out[pl.ds(k_start, k_rows), :])
            result = term if result is None else result + term
        lse[pl.ds(start, rows), :] = jnp.broadcast_to(top + jnp.log(total), (rows, HEAD_DIM))
        for j in range(rows // CLEN):
            block = start // CLEN + j
            there = pl.ds(pl.multiple_of(order[block] * CLEN, CLEN), CLEN)
            mixed[there, :] = result[j * CLEN : (j + 1) * CLEN].astype(BF16)


def attend(order, qkv, inv_q, inv_k, gain_q, gain_k, cos, sin):
    heads = qkv.shape[1] // (3 * HEAD_DIM)
    head = lambda off: pl.BlockSpec((GTOK, HEAD_DIM), lambda h, o: (0, h + off))
    whole = lambda w: pl.BlockSpec((GTOK, w), lambda h, o: (0, 0))
    gain = pl.BlockSpec((1, HEAD_DIM), lambda h, o: (0, h))
    wide = jax.ShapeDtypeStruct((GTOK, heads * HEAD_DIM), BF16)
    return pl.pallas_call(
        attend_kernel,
        grid_spec=pltpu.PrefetchScalarGridSpec(
            num_scalar_prefetch=1,
            grid=(heads,),
            in_specs=[head(0), head(heads), head(2 * heads), whole(1), whole(1), gain, gain]
            + [whole(HEAD_DIM)] * 2,
            out_specs=[head(0)] * 5,
        ),
        out_shape=[wide] * 4 + [jax.ShapeDtypeStruct((GTOK, heads * HEAD_DIM), F32)],
        compiler_params=pltpu.CompilerParams(vmem_limit_bytes=48 * 2**20),
    )(order, qkv, qkv, qkv, inv_q, inv_k, gain_q, gain_k, cos, sin)


def attend_back_kernel(
    order, q_rot, k_rot, v_in, lse, grad_mixed, cos, sin, dq_out, dk_out, dv_out, grads, dq, dk, dv
):
    for i in range(BLOCKS):
        there = pl.ds(pl.multiple_of(order[i] * CLEN, CLEN), CLEN)
        grads[pl.ds(i * CLEN, CLEN), :] = grad_mixed[there, :]
    dk[...] = jnp.zeros_like(dk)
    dv[...] = jnp.zeros_like(dv)
    for start, rows, keys in tiles():
        here = pl.ds(start, rows)
        q, g, level = q_rot[here, :], grads[here, :], lse[here, 0:1]
        probs, grad_probs, delta = [], [], 0.0
        for k_start, k_rows, masked in keys:
            s = by_transpose(q, k_rot[pl.ds(k_start, k_rows), :]) * SCALE
            s = jnp.where(causal(rows), s, NEG) if masked else s
            p = jnp.exp(s - level)
            gp = by_transpose(g, v_in[pl.ds(k_start, k_rows), :])
            delta = delta + jnp.sum(p * gp, axis=1, keepdims=True)
            probs.append(p)
            grad_probs.append(gp)
        total = None
        for p, gp, (k_start, k_rows, _) in zip(probs, grad_probs, keys):
            there = pl.ds(k_start, k_rows)
            raw = (p * (gp - delta) * SCALE).astype(BF16)
            term = plain(raw, k_rot[there, :])
            total = term if total is None else total + term
            dk[there, :] += cross_rows(raw, q)
            dv[there, :] += cross_rows(p.astype(BF16), g)
        dq[here, :] = total
    for i in range(BLOCKS):
        here = pl.ds(i * CLEN, CLEN)
        there = pl.ds(pl.multiple_of(order[i] * CLEN, CLEN), CLEN)
        cos_rows, sin_rows = cos[there, :], sin[there, :]
        dq_out[there, :] = rope(dq[here, :], cos_rows, -sin_rows)
        dk_out[there, :] = rope(dk[here, :], cos_rows, -sin_rows)
        dv_out[there, :] = dv[here, :].astype(BF16)


def attend_back(order, q_rot, k_rot, v_in, lse, grad_mixed, cos, sin):
    heads = q_rot.shape[1] // HEAD_DIM
    head = pl.BlockSpec((GTOK, HEAD_DIM), lambda h, o: (0, h))
    whole = pl.BlockSpec((GTOK, HEAD_DIM), lambda h, o: (0, 0))
    wide = lambda t: jax.ShapeDtypeStruct((GTOK, heads * HEAD_DIM), t)
    return pl.pallas_call(
        attend_back_kernel,
        grid_spec=pltpu.PrefetchScalarGridSpec(
            num_scalar_prefetch=1,
            grid=(heads,),
            in_specs=[head] * 5 + [whole] * 2,
            out_specs=[head] * 3,
            scratch_shapes=[
                pltpu.VMEM((GTOK, HEAD_DIM), BF16),
                pltpu.VMEM((GTOK, HEAD_DIM), F32),
                pltpu.VMEM((GTOK, HEAD_DIM), F32),
                pltpu.VMEM((GTOK, HEAD_DIM), F32),
            ],
        ),
        out_shape=[wide(F32), wide(F32), wide(BF16)],
        compiler_params=pltpu.CompilerParams(vmem_limit_bytes=48 * 2**20),
    )(order, q_rot, k_rot, v_in, lse, grad_mixed, cos, sin)


ANY = pl.BlockSpec(memory_space=pl.ANY)
VM = pl.BlockSpec(memory_space=pltpu.VMEM)
DMA = pltpu.SemaphoreType.DMA


def params(cid, mib=60):
    return pltpu.CompilerParams(collective_id=cid, has_side_effects=True, vmem_limit_bytes=mib * 2**20)


def peer(i):
    return {"expert": i}


def remote(src, dst, send_sem, recv_sem, to):
    return pltpu.make_async_remote_copy(
        src_ref=src, dst_ref=dst, send_sem=send_sem, recv_sem=recv_sem, device_id=peer(to), device_id_type=MESH
    )


def greet_line(n):
    p = lax.axis_index("expert")
    bar = pltpu.get_barrier_semaphore()

    @pl.when(p > 0)
    def _():
        pl.semaphore_signal(bar, inc=1, device_id=peer(p - 1), device_id_type=MESH)

    @pl.when(p < n - 1)
    def _():
        pl.semaphore_signal(bar, inc=1, device_id=peer(p + 1), device_id_type=MESH)

    pl.semaphore_wait(bar, (p > 0).astype(jnp.int32) + (p < n - 1).astype(jnp.int32))
    return p


def greet_all(n):
    p = lax.axis_index("expert")
    bar = pltpu.get_barrier_semaphore()
    for s in range(1, n):
        pl.semaphore_signal(bar, inc=1, device_id=peer(lax.rem(p + s, n)), device_id_type=MESH)
    pl.semaphore_wait(bar, n - 1)
    return p


class Gather:
    sems = lambda n: [DMA((n,))] * 3

    def __init__(self, p, n, own, at, sems):
        self.p, self.n, self.own, self.at = p, n, own, at
        self.to_right, self.to_left, self.recv = sems

    def right(self, src, j):
        return remote(src, self.at(j), self.to_right.at[j], self.recv.at[j], self.p + 1)

    def left(self, src, j):
        return remote(src, self.at(j), self.to_left.at[j], self.recv.at[j], self.p - 1)

    def start(self):
        @pl.when(self.p < self.n - 1)
        def _():
            self.right(self.own, self.p).start()

        @pl.when(self.p > 0)
        def _():
            self.left(self.own, self.p).start()

    def step(self, s, use=None):
        p, n = self.p, self.n
        j, k = p - s, p + s

        @pl.when(j >= 0)
        def _():
            self.right(self.at(j), j).wait_recv()

            @pl.when(p < n - 1)
            def _():
                self.right(self.at(j), j).start()

        @pl.when(k < n)
        def _():
            self.left(self.at(k), k).wait_recv()

            @pl.when(p > 0)
            def _():
                self.left(self.at(k), k).start()

        if use is not None:
            for i, here in ((j, j >= 0), (k, k < n)):
                pl.when(here)(functools.partial(use, i))

    def finish(self):
        for j in range(self.n):

            @pl.when((j <= self.p) & (self.p < self.n - 1))
            def _():
                self.right(self.own, j).wait_send()

            @pl.when((j >= self.p) & (self.p > 0))
            def _():
                self.left(self.own, j).wait_send()


class Reduce:
    pieces, depth = 4, 2
    sems = lambda n: [DMA((n * Reduce.pieces,))] * 4
    boxes = lambda n, rows, width: [pltpu.VMEM((n * Reduce.pieces, rows // Reduce.pieces, width), BF16)] * 2

    def __init__(self, p, n, rows, part, make, boxes, sems):
        self.p, self.n, self.rows, self.part, self.make = p, n, rows, part, make
        self.from_left, self.from_right = boxes
        self.to_right, self.to_left, self.recv_r, self.recv_l = sems
        self.order = [(s, c) for s in range(n - 1) for c in range(self.pieces)]

    def at(self, j, c):
        size = self.rows // self.pieces
        return self.part.at[pl.ds(pl.multiple_of(j * self.rows + c * size, size), size)]

    def right(self, j, c):
        i = j * self.pieces + c
        return remote(self.at(j, c), self.from_left.at[i], self.to_right.at[i], self.recv_r.at[i], self.p + 1)

    def left(self, j, c):
        i = j * self.pieces + c
        return remote(self.at(j, c), self.from_right.at[i], self.to_left.at[i], self.recv_l.at[i], self.p - 1)

    def add(self, j, c, box):
        total = self.at(j, c)[...].astype(F32) + box[j * self.pieces + c].astype(F32)
        self.at(j, c)[...] = total.astype(BF16)

    def step(self, s):
        p, n = self.p, self.n
        j, k = n - 1 - s, s
        pl.when(j > p)(lambda: self.make(j))
        pl.when(k < p)(lambda: self.make(k))
        for c in range(self.pieces):
            m = s * self.pieces + c

            @pl.when(j > p)
            def _():
                @pl.when(p > 0)
                def _():
                    self.right(j, c).wait_recv()
                    self.add(j, c, self.from_left)

                if m >= self.depth:
                    s0, c0 = self.order[m - self.depth]
                    self.right(n - 1 - s0, c0).wait_send()
                self.right(j, c).start()

            @pl.when(k < p)
            def _():
                @pl.when(p < n - 1)
                def _():
                    self.left(k, c).wait_recv()
                    self.add(k, c, self.from_right)

                if m >= self.depth:
                    s0, c0 = self.order[m - self.depth]
                    self.left(s0, c0).wait_send()
                self.left(k, c).start()

    def finish(self, out, base=None):
        p, n, size = self.p, self.n, self.rows // self.pieces
        self.make(p)
        for c in range(self.pieces):

            @pl.when(p > 0)
            def _():
                self.right(p, c).wait_recv()
                self.add(p, c, self.from_left)

            @pl.when(p < n - 1)
            def _():
                self.left(p, c).wait_recv()
                self.add(p, c, self.from_right)

            here = pl.ds(c * size, size)
            if base is None:
                out[here] = self.at(p, c)[...]
            else:
                out[here] = (base[here].astype(F32) + self.at(p, c)[...].astype(F32)).astype(out.dtype)
        for m, (s, c) in enumerate(self.order):
            pl.when((n - 1 - s > p) & (m >= (n - 1 - p) * self.pieces - self.depth))(
                lambda s=s, c=c: self.right(n - 1 - s, c).wait_send()
            )
            pl.when((s < p) & (m >= p * self.pieces - self.depth))(lambda s=s, c=c: self.left(s, c).wait_send())


def rows_of(ref, rows):
    return lambda j: ref.at[pl.ds(pl.multiple_of(j * rows, rows), rows)]


def ag_kernel(n, rows, x, out, to_right, to_left, recv, local):
    p = greet_line(n)
    at = rows_of(out, rows)
    own = pltpu.make_async_copy(x, at(p), local)
    own.start()
    line = Gather(p, n, x, at, (to_right, to_left, recv))
    line.start()
    for s in range(1, n):
        line.step(s)
    own.wait()
    line.finish()


def ag_z(x, n, cid):
    rows = x.shape[0]
    return pl.pallas_call(
        functools.partial(ag_kernel, n, rows),
        out_shape=jax.ShapeDtypeStruct((n * rows,) + x.shape[1:], x.dtype),
        in_specs=[ANY],
        out_specs=ANY,
        scratch_shapes=Gather.sems(n) + [DMA],
        compiler_params=params(cid),
    )(x)


def gather_kernel(n, rows, x, slot, small, grads, logits, rows_out, grads_out, *rest):
    shards, picked, picked_grads, to_right, to_left, recv, out_sems = rest
    p = greet_line(n)
    experts = slot.shape[1]
    line = Gather(p, n, x, lambda j: shards.at[j], (to_right, to_left, recv))
    line.start()

    def pick(j, e):
        places = lax.broadcasted_iota(jnp.int32, (CAP, rows), 0)
        return (slot[j, e : e + 1] == places).astype(F32).astype(BF16)

    def use(j, block, first=False):
        logits[pl.ds(pl.multiple_of(j * rows, rows), rows), :] = plain(block[...], small[...])
        for e in range(experts):
            new = plain(pick(j, e), block[...])
            picked[e] = new.astype(BF16) if first else (picked[e].astype(F32) + new).astype(BF16)

    def copy_out(e, src, dst, k):
        return pltpu.make_async_copy(src.at[e], dst.at[e], out_sems.at[k, e])

    use(p, x, True)
    for e in range(experts):
        for j in range(n):
            new = plain(pick(j, e), grads[j * rows : (j + 1) * rows])
            picked_grads[e] = new.astype(BF16) if j == 0 else (picked_grads[e].astype(F32) + new).astype(BF16)
        copy_out(e, picked_grads, grads_out, 1).start()
    for s in range(1, n):
        line.step(s, lambda j: use(j, shards.at[j]))
    for e in range(experts):
        copy_out(e, picked, rows_out, 0).start()
    for e in range(experts):
        copy_out(e, picked, rows_out, 0).wait()
        copy_out(e, picked_grads, grads_out, 1).wait()
    line.finish()


def gather_rows(x, slot, small, grads, n, cid):
    rows, width = x.shape
    experts = slot.shape[1]
    wide = (experts, CAP, width)
    return pl.pallas_call(
        functools.partial(gather_kernel, n, rows),
        out_shape=[
            jax.ShapeDtypeStruct((n * rows, small.shape[1]), F32),
            jax.ShapeDtypeStruct(wide, BF16),
            jax.ShapeDtypeStruct(wide, BF16),
        ],
        in_specs=[VM] * 4,
        out_specs=[VM, ANY, ANY],
        scratch_shapes=[pltpu.VMEM((n, rows, width), BF16), pltpu.VMEM(wide, BF16), pltpu.VMEM(wide, BF16)]
        + Gather.sems(n)
        + [DMA((2, experts))],
        compiler_params=params(cid),
    )(x, slot, small, grads)


def rs_kernel(n, rows, part, out, left_box, right_box, *sems):
    p = greet_line(n)
    line = Reduce(p, n, rows, part, lambda j: None, (left_box, right_box), sems)
    for s in range(n - 1):
        line.step(s)
    line.finish(out)


def rs_z(part, n, cid):
    rows, width = part.shape[0] // n, part.shape[1]
    return pl.pallas_call(
        functools.partial(rs_kernel, n, rows),
        out_shape=jax.ShapeDtypeStruct((rows, width), BF16),
        in_specs=[VM],
        out_specs=VM,
        scratch_shapes=Reduce.boxes(n, rows, width) + Reduce.sems(n),
        compiler_params=params(cid),
    )(part)


def combine(part, rows, slot, weight, blocks):
    def make(j):
        total, e = None, 0
        for block in blocks:
            for i in range(block.shape[0]):
                places = lax.broadcasted_iota(jnp.int32, (rows, CAP), 1)
                chosen = slot[j, :, e : e + 1] == places
                scale = 1.0 if weight is None else weight[j, :, e : e + 1]
                term = plain(jnp.where(chosen, scale, 0.0).astype(BF16), block[i])
                total = term if total is None else total + term
                e += 1
        part[pl.ds(pl.multiple_of(j * rows, rows), rows), :] = total.astype(BF16)

    return make


def combine_kernel(n, rows, slot, low, high, out, part, left_box, right_box, *sems):
    p = greet_line(n)
    make = combine(part, rows, slot, None, (low, high))
    line = Reduce(p, n, rows, part, make, (left_box, right_box), sems)
    for s in range(n - 1):
        line.step(s)
    line.finish(out)


def combine_z(slot, low, high, n, cid):
    rows, width = slot.shape[1], low.shape[2]
    return pl.pallas_call(
        functools.partial(combine_kernel, n, rows),
        out_shape=jax.ShapeDtypeStruct((rows, width), BF16),
        in_specs=[VM] * 3,
        out_specs=VM,
        scratch_shapes=[pltpu.VMEM((n * rows, width), BF16)] + Reduce.boxes(n, rows, width) + Reduce.sems(n),
        compiler_params=params(cid),
    )(slot, low, high)


def both_kernel(n, rows, x, slot, weight, low, high, base, all_out, out, part, left_box, right_box, *sems):
    p = greet_line(n)
    at = rows_of(all_out, rows)
    own = pltpu.make_async_copy(x, at(p), sems[7])
    own.start()
    gather = Gather(p, n, x, at, sems[:3])
    gather.start()
    make = combine(part, rows, slot, weight, (low, high))
    line = Reduce(p, n, rows, part, make, (left_box, right_box), sems[3:7])
    for s in range(n - 1):
        line.step(s)
        gather.step(s + 1)
    line.finish(out, base)
    own.wait()
    gather.finish()


def gather_and_combine(x, slot, weight, low, high, base, n, cid):
    rows, width = x.shape
    return pl.pallas_call(
        functools.partial(both_kernel, n, rows),
        out_shape=[jax.ShapeDtypeStruct((n * rows, width), x.dtype), jax.ShapeDtypeStruct((rows, width), BF16)],
        in_specs=[ANY] + [VM] * 5,
        out_specs=[ANY, VM],
        scratch_shapes=[pltpu.VMEM((n * rows, width), BF16)]
        + Reduce.boxes(n, rows, width)
        + Gather.sems(n)
        + Reduce.sems(n)
        + [DMA],
        compiler_params=params(cid),
    )(x, slot, weight, low, high, base)


def a2a_kernel(n,rows,cols,x,out,send,recv,local):
    p=greet_all(n)
    src=lambda j: x.at[pl.ds(pl.multiple_of(j*rows,rows),rows)]
    dst=lambda c: out.at[:,pl.ds(pl.multiple_of(c*cols,cols),cols)]
    own=pltpu.make_async_copy(src(p),dst(p),local); own.start()
    def send_to(s):
        j=lax.rem(p+s,n)
        return pltpu.make_async_remote_copy(src_ref=src(j),dst_ref=dst(p),send_sem=send.at[s],recv_sem=recv.at[s],device_id=peer(j),device_id_type=MESH)
    for s in range(1,n): send_to(s).start()
    for s in range(1,n):
        c=lax.rem(p-s+n,n)
        pltpu.make_async_remote_copy(src_ref=src(p),dst_ref=dst(c),send_sem=send.at[s],recv_sem=recv.at[s],device_id=peer(c),device_id_type=MESH).wait_recv()
    for s in range(1,n): send_to(s).wait_send()
    own.wait()

def a2a_z(x,n,cid):
    rows=x.shape[0]//n; cols=x.shape[1]
    return pl.pallas_call(functools.partial(a2a_kernel,n,rows,cols),out_shape=jax.ShapeDtypeStruct((rows,n*cols),x.dtype),
        in_specs=[ANY],out_specs=ANY,scratch_shapes=[DMA((n,))]*2+[DMA],
        compiler_params=params(cid))(x)

def exchange_kernel(n, rows, x, out, send, recv, local):
    p = greet_all(n)
    at = lambda ref, j: ref.at[pl.ds(pl.multiple_of(j * rows, rows), rows)]
    own = pltpu.make_async_copy(at(x, p), at(out, p), local)
    own.start()

    def to(s):
        j = lax.rem(p + s, n)
        return pltpu.make_async_remote_copy(
            src_ref=at(x, j), dst_ref=at(out, p), send_sem=send.at[s], recv_sem=recv.at[s], device_id=peer(j),
            device_id_type=MESH,
        )

    for s in range(1, n):
        to(s).start()
    for s in range(1, n):
        to(s).wait_recv()
    for s in range(1, n):
        to(s).wait_send()
    own.wait()


def exchange_z(x, n, cid):
    return pl.pallas_call(
        functools.partial(exchange_kernel, n, x.shape[0] // n),
        out_shape=jax.ShapeDtypeStruct(x.shape, x.dtype),
        in_specs=[ANY],
        out_specs=ANY,
        scratch_shapes=[DMA((n,))] * 2 + [DMA],
        compiler_params=params(cid),
    )(x)


def sum_kernel(n,x,out,got,send,recv):
    p=greet_all(n)
    def send_to(s):
        return pltpu.make_async_remote_copy(src_ref=x,dst_ref=got.at[s],send_sem=send.at[s],recv_sem=recv.at[s],device_id=peer(lax.rem(p+s,n)),device_id_type=MESH)
    for s in range(1,n): send_to(s).start()
    tot=x[...]
    for s in range(1,n):
        send_to(s).wait_recv(); tot=tot+got[s]
    out[...]=tot
    for s in range(1,n): send_to(s).wait_send()

def sum_z(x,n,cid):
    return pl.pallas_call(functools.partial(sum_kernel,n),out_shape=jax.ShapeDtypeStruct(x.shape,x.dtype),in_specs=[VM],out_specs=VM,
        scratch_shapes=[pltpu.VMEM((n,)+x.shape,x.dtype)]+[DMA((n,))]*2,compiler_params=params(cid))(x)


def expert_kernel(
    slot, weight, x, g, gate, up, down, eo_out, gin_out, route_out, gu_out, gd_out, xt, w_col, both, scaled, eo, gin
):
    f = pl.program_id(1)
    tile = gate.shape[2]
    chunks = CAP // ROWS
    tokens = slot.shape[2]
    x, g = x.at[0], g.at[0]

    def one_hot(start):
        place = lax.broadcasted_iota(jnp.int32, (ROWS, tokens), 0) + start
        return slot[0] == place

    @pl.when(f == 0)
    def _():
        @pl.loop(0, chunks)
        def _(c):
            here = pl.ds(pl.multiple_of(c * ROWS, ROWS), ROWS)
            chosen = one_hot(c * ROWS)
            w_col[here, :] = jnp.sum(jnp.where(chosen, weight[0], 0.0), axis=1, keepdims=True)
            eo[here, :] = jnp.zeros((ROWS, x.shape[1]), F32)
            gin[here, :] = jnp.zeros((ROWS, x.shape[1]), F32)

        xt[...] = x[...].T

    @pl.loop(0, chunks)
    def _(c):
        here = pl.ds(pl.multiple_of(c * ROWS, ROWS), ROWS)
        a = plain(x[here, :], gate[0])
        b = plain(x[here, :], up[0])
        h = by_transpose(g[here, :], down[0]) * w_col[here, :]
        sig = 1.0 / (1.0 + jnp.exp(-a))
        silu = a * sig
        hidden = silu * b
        gg = (h * b * (sig * (1.0 + a * (1.0 - sig)))).astype(BF16)
        gu = (h * silu).astype(BF16)
        both[here, 0:tile] = gg
        both[here, tile : 2 * tile] = gu
        scaled[here, :] = (hidden * w_col[here, :]).astype(BF16)
        eo[here, :] += plain(hidden.astype(BF16), down[0])
        gin[here, :] += by_transpose(gg, gate[0]) + by_transpose(gu, up[0])

    pieces, rows = gu_out.shape[0], gu_out.shape[2]

    grad_both = plain(xt[...], both[...]).astype(BF16)
    for c in range(pieces):
        gu_out[c, 0] = grad_both[c * rows : (c + 1) * rows]

    down_rows = gd_out.shape[2]
    grad_down = cross_rows(scaled[...], g[...]).astype(BF16)
    for c in range(gd_out.shape[0]):
        gd_out[c, 0] = grad_down[c * down_rows : (c + 1) * down_rows]

    @pl.when(f == pl.num_programs(1) - 1)
    def _():
        eo_out[0] = eo[...].astype(BF16)
        gin_out[0] = gin[...].astype(BF16)
        route = jnp.zeros((1, tokens), F32)
        for c in range(chunks):
            here = pl.ds(c * ROWS, ROWS)
            dots = jnp.sum(eo[here, :].astype(BF16).astype(F32) * g[here, :].astype(F32), axis=1, keepdims=True)
            route = route + jnp.sum(jnp.where(one_hot(c * ROWS), dots, 0.0), axis=0, keepdims=True)
        route_out[0] = route


def experts(first, count, dp, slot, weight, x, g, gate, up, down):
    tokens, width = slot.shape[2], x.shape[2]
    ff = gate.shape[2]
    steps = ff // FTILE
    line = pl.BlockSpec((1, 1, tokens), lambda e, f: (first + e, 0, 0))
    column = pl.BlockSpec((1, width, FTILE), lambda e, f: (first + e, 0, f))
    row = pl.BlockSpec((1, FTILE, width), lambda e, f: (first + e, f, 0))
    slots_in = pl.BlockSpec((1, CAP, width), lambda e, f: (first + e, 0, 0), pipeline_mode=pl.Buffered(2))
    slots_out = pl.BlockSpec((1, CAP, width), lambda e, f: (e, 0, 0), pipeline_mode=pl.Buffered(1))
    down_rows = ff // dp
    return pl.pallas_call(
        expert_kernel,
        grid=(count, steps),
        in_specs=[line, line, slots_in, slots_in, column, column, row],
        out_specs=[
            slots_out,
            slots_out,
            pl.BlockSpec((1, 1, tokens), lambda e, f: (e, 0, 0)),
            pl.BlockSpec((dp, 1, width // dp, 2 * FTILE), lambda e, f: (0, e, 0, f)),
            pl.BlockSpec((FTILE // down_rows, 1, down_rows, width), lambda e, f: (f, e, 0, 0)),
        ],
        out_shape=[
            jax.ShapeDtypeStruct((count, CAP, width), BF16),
            jax.ShapeDtypeStruct((count, CAP, width), BF16),
            jax.ShapeDtypeStruct((count, 1, tokens), F32),
            jax.ShapeDtypeStruct((dp, count, width // dp, 2 * ff), BF16),
            jax.ShapeDtypeStruct((dp, count, down_rows, width), BF16),
        ],
        scratch_shapes=[
            pltpu.VMEM((width, CAP), BF16),
            pltpu.VMEM((CAP, 1), F32),
            pltpu.VMEM((CAP, 2 * FTILE), BF16),
            pltpu.VMEM((CAP, FTILE), BF16),
            pltpu.VMEM((CAP, width), F32),
            pltpu.VMEM((CAP, width), F32),
        ],
        compiler_params=pltpu.CompilerParams(vmem_limit_bytes=60 * 2**20),
    )(slot, weight, x, g, gate, up, down)


def row_moves(ways, dp):
    return [(d * ways + z, z * dp + d) for d in range(dp) for z in range(ways)]


def hops(up, down, count, ways):
    for _ in range(count):
        up = up + [lax.ppermute(up[-1], "expert", [(i, i + 1) for i in range(ways - 1)])]
        down = down + [lax.ppermute(down[-1], "expert", [(i + 1, i) for i in range(ways - 1)])]
    return up, down


def later(sent, other):
    up, down = sent
    last_up, last_down, other = lax.optimization_barrier((up[-1], down[-1], other))
    return up[:-1] + [last_up], down[:-1] + [last_down], other


def line_up(up, down, ways):
    line = jnp.concatenate(up[:0:-1] + down, axis=0)
    rows = down[0].shape[0]
    start = (ways - 1 - lax.axis_index("expert")) * rows
    return lax.dynamic_slice_in_dim(line, start, ways * rows, axis=0)


def block_order(segs, places):
    seg = segs.reshape(BLOCKS, CLEN)[:, 0]
    place = places.reshape(BLOCKS, CLEN)[:, 0]
    stand = jnp.where(seg == 0, place // CLEN, PROMPT // CLEN - 1 + seg)
    blocks = jnp.arange(BLOCKS, dtype=jnp.int32)
    return jnp.sum(jnp.where(stand[None, :] == blocks[:, None], blocks[None, :], 0), axis=1)


def slots(routes, priority):
    experts = jnp.arange(EXPERTS, dtype=jnp.int32)
    hits = jnp.any(routes[:, :, None] == experts[None, None, :], axis=1)
    index = jnp.arange(GTOK, dtype=jnp.int32)
    rank = jnp.sum(jnp.where(priority[:, None] == index[None, :], index[:, None], 0), axis=0)
    earlier = (rank[None, :] < rank[:, None]).astype(BF16)
    return hits, plain(earlier, hits.astype(BF16)).astype(jnp.int32)


def body(
    tokens,
    cotangent,
    attention_gain,
    query_weight,
    key_weight,
    value_weight,
    out_weight,
    query_norm,
    key_norm,
    mixture_gain,
    router_weight,
    gate_weight,
    up_weight,
    down_weight,
    segments,
    positions,
    priority,
    routes,
):
    tok_dev, width = tokens.shape
    experts_here = gate_weight.shape[0]
    ways = lax.axis_size("expert")
    z = lax.axis_index("expert")
    cols = width // ways
    first_row = z * tok_dev

    small = jnp.concatenate(
        [attention_gain[:, None], query_norm[:, None], key_norm[:, None], mixture_gain[:, None], router_weight],
        axis=1,
    )
    small = jnp.pad(small, ((0, 0), (0, SMALL - small.shape[1])))
    shard = jnp.stack([query_weight, key_weight, value_weight], axis=1)
    shard = shard.reshape(-1, 3, ways, cols).transpose(2, 0, 1, 3).reshape(ways, -1, 3 * cols)
    shard = jnp.concatenate([shard, jnp.broadcast_to(small[None], (ways,) + small.shape)], axis=2)
    shard = exchange_z(shard.reshape(-1, shard.shape[-1]), ways, 1)
    dense = lax.all_gather(shard, "dp", axis=0, tiled=True)
    qkv_weight = dense[:, : 3 * cols]
    small = dense[:, 3 * cols :]
    shard, out_weight, gate_weight, up_weight, down_weight = lax.optimization_barrier(
        (shard, out_weight, gate_weight, up_weight, down_weight)
    )
    out_full = lax.all_gather(out_weight, BOTH, axis=0, tiled=True)
    attend_gain = small[:, 0].astype(F32)
    mix_gain = small[:, 3].astype(F32)
    router_full = small[:, 4 : 4 + EXPERTS]
    my_gains = lax.dynamic_slice_in_dim(small[:, 1:3], z * cols, cols, axis=0).astype(F32)
    gain_q, gain_k = my_gains[:, 0][None], my_gains[:, 1][None]
    out_mine = lax.dynamic_slice_in_dim(out_full, z * cols, cols, axis=0)
    tokens_all = ag_z(tokens, ways, 2)
    gate_full = lax.all_gather(gate_weight, "dp", axis=1, tiled=True)
    up_full = lax.all_gather(up_weight, "dp", axis=1, tiled=True)
    down_full = lax.all_gather(down_weight, "dp", axis=1, tiled=True)
    steps = [ways // 2, (3 * ways) // 4]
    early, tokens_all = lax.optimization_barrier((cotangent, tokens_all))
    sent = hops([early], [early], steps[0] - 1, ways)

    segs, places = segments[0], positions[0]
    order = block_order(segs, places)
    frequency = 10000.0 ** (-jnp.arange(0, HEAD_DIM // 2, dtype=F32) * 2.0 / HEAD_DIM)
    angles = places.astype(F32)[:, None] * frequency[None, :]
    cos, sin = jnp.cos(angles), jnp.sin(angles)
    cos = jnp.concatenate([cos, cos], axis=1)
    sin = jnp.concatenate([-sin, sin], axis=1)
    hits, slot = slots(routes[0], priority[0])
    my_hits = lax.dynamic_slice_in_dim(hits, z * experts_here, experts_here, axis=1)
    my_slot = lax.dynamic_slice_in_dim(slot, z * experts_here, experts_here, axis=1)
    my_slot = jnp.where(my_hits & (my_slot < CAP), my_slot, -1)
    slot_lines = my_slot.T[:, None, :]
    slot_shards = my_slot.T.reshape(experts_here, ways, tok_dev).transpose(1, 0, 2)
    slot_cols = my_slot.reshape(ways, tok_dev, experts_here)

    token_f = tokens_all.astype(F32)
    inverse_in = lax.rsqrt(jnp.mean(token_f * token_f, axis=-1, keepdims=True) + EPS)
    normed = (token_f * inverse_in * attend_gain).astype(BF16)
    qkv = plain(normed, qkv_weight)
    squares = jnp.sum(jnp.square(qkv[:, : 2 * cols]).reshape(GTOK, 2, cols), axis=-1)
    squares = sum_z(jnp.pad(squares.T, ((0, 6), (0, 0))), ways, 3)
    up, down, squares = later(sent, squares)
    sent = hops(up, down, steps[1] - steps[0], ways)
    inv_q = lax.rsqrt(squares[0] / width + EPS)[:, None]
    inv_k = lax.rsqrt(squares[1] / width + EPS)[:, None]
    q_rot, k_rot, v_b, mixed_heads, lse = attend(order, qkv, inv_q, inv_k, gain_q, gain_k, cos, sin)
    up, down, mixed_heads = later(sent, mixed_heads)
    grad_all = line_up(*hops(up, down, ways - steps[1], ways), ways)
    mixed = a2a_z(mixed_heads, ways, 4)
    own_f = tokens.astype(F32)
    resid = own_f + plain(mixed, out_full)
    mix_inverse = lax.rsqrt(jnp.mean(resid * resid, axis=-1, keepdims=True) + EPS)
    mix_unit = resid * mix_inverse
    mix = (mix_unit * mix_gain).astype(BF16)
    logits, inputs, grad_rows = gather_rows(mix, slot_shards, small, grad_all, ways, 5)

    router_all = jax.nn.softmax(logits[:, 4 : 4 + EXPERTS], axis=-1)
    my_weight = lax.dynamic_slice_in_dim(router_all, z * experts_here, experts_here, axis=1)
    weight_lines = my_weight.T[:, None, :]
    weight_cols = my_weight.reshape(ways, tok_dev, experts_here)
    half = experts_here // 2
    work = (half, lax.axis_size("dp"), slot_lines, weight_lines, inputs, grad_rows, gate_full, up_full, down_full)
    out_low, in_low, route_low, both_low, down_low = experts(0, *work)
    sum_both_low = lax.psum_scatter(both_low, "dp", scatter_dimension=0, tiled=True)
    sum_down_low = lax.psum_scatter(down_low, "dp", scatter_dimension=0, tiled=True)
    out_high, in_high, route_high, both_high, down_high = experts(half, *work)
    sum_both_high = lax.psum_scatter(both_high, "dp", scatter_dimension=0, tiled=True)
    sum_down_high = lax.psum_scatter(down_high, "dp", scatter_dimension=0, tiled=True)
    my_route_grad = jnp.concatenate([route_low, route_high], axis=0)[:, 0]
    route_grad = lax.all_to_all(my_route_grad, "expert", split_axis=1, concat_axis=0, tiled=True).T
    grad_routed = combine_z(slot_cols, in_low, in_high, ways, 6).astype(F32)

    router = lax.dynamic_slice_in_dim(router_all, first_row, tok_dev, axis=0)
    grad_logits = (router * (route_grad - jnp.sum(router * route_grad, axis=-1, keepdims=True))).astype(BF16)
    grad_router_w = cross_rows(mix, grad_logits)
    grad_mix = grad_routed + by_transpose(grad_logits, router_full)
    grad_mix_gain = jnp.sum(grad_mix * mix_unit, axis=0)
    grad_resid = cotangent.astype(F32) + norm_back(grad_mix, mix_unit, mix_inverse, mix_gain)
    grad_branch = grad_resid.astype(BF16)
    grad_branch, sum_both_low, sum_down_low = lax.optimization_barrier((grad_branch, sum_both_low, sum_down_low))
    branch_all, output = gather_and_combine(grad_branch, slot_cols, weight_cols, out_low, out_high, resid, ways, 7)
    grad_heads = by_transpose(branch_all, out_mine).astype(BF16)
    grad_out_w = cross_rows(mixed_heads, branch_all).astype(BF16)
    out_out = lax.psum_scatter(grad_out_w, "dp", scatter_dimension=0, tiled=True)
    out_out = lax.ppermute(out_out, BOTH, row_moves(ways, lax.axis_size("dp"))).astype(F32)

    grad_heads, sum_both_high = lax.optimization_barrier((grad_heads, sum_both_high))
    dq, dk, dv = attend_back(order, q_rot, k_rot, v_b, lse, grad_heads, cos, sin)
    q_unit = qkv[:, :cols] * inv_q
    k_unit = qkv[:, cols : 2 * cols] * inv_k
    inner = jnp.stack(
        [jnp.sum(dq * gain_q * q_unit, axis=-1), jnp.sum(dk * gain_k * k_unit, axis=-1)], axis=0
    )
    inner = sum_z(jnp.pad(inner, ((0, 6), (0, 0))), ways, 8) / width
    grad_q_gain = jnp.sum(dq * q_unit, axis=0)
    grad_k_gain = jnp.sum(dk * k_unit, axis=0)
    grad_q = (inv_q * (dq * gain_q - q_unit * inner[0][:, None])).astype(BF16)
    grad_k = (inv_k * (dk * gain_k - k_unit * inner[1][:, None])).astype(BF16)
    grad_qkv = jnp.concatenate([grad_q, grad_k, dv], axis=1)
    grad_normed_part = by_transpose(grad_qkv, qkv_weight)
    grad_attend_gain = jnp.sum(grad_normed_part * (token_f * inverse_in), axis=0)
    part, sum_down_high = lax.optimization_barrier((grad_normed_part.astype(BF16), sum_down_high))
    grad_normed = rs_z(part, ways, 9).astype(F32)
    own_inverse = lax.dynamic_slice_in_dim(inverse_in, first_row, tok_dev, axis=0)
    input_grad = grad_resid + norm_back(grad_normed, own_f * own_inverse, own_inverse, attend_gain)

    place = lambda part: lax.dynamic_update_slice(jnp.zeros((width,), F32), part, (z * cols,))
    extra = jnp.concatenate(
        [
            jnp.stack([grad_attend_gain, place(grad_q_gain), place(grad_k_gain), grad_mix_gain], axis=1),
            grad_router_w,
            jnp.zeros((width, SMALL - 4 - EXPERTS), F32),
        ],
        axis=1,
    )
    grad_qkv_w = jnp.concatenate([cross_rows(normed, grad_qkv), extra], axis=1).astype(BF16)
    grad_qkv_w = lax.psum_scatter(grad_qkv_w, "dp", scatter_dimension=0, tiled=True)
    grad_qkv_w = exchange_z(grad_qkv_w, ways, 10).reshape(ways, -1, 3 * cols + SMALL)
    grad_w = [
        grad_qkv_w[:, :, i * cols : (i + 1) * cols].transpose(1, 0, 2).reshape(-1, width).astype(F32)
        for i in range(3)
    ]
    sums = jnp.concatenate([sum_both_low[0], sum_both_high[0]], axis=0).astype(F32)
    sums = sums.reshape(sums.shape[:2] + (-1, 2, FTILE))
    out_gate = sums[:, :, :, 0].reshape(gate_weight.shape)
    out_up = sums[:, :, :, 1].reshape(gate_weight.shape)
    out_down = jnp.concatenate([sum_down_low[0], sum_down_high[0]], axis=0).astype(F32)
    packed = jnp.sum(grad_qkv_w[:, :, 3 * cols :].astype(F32), axis=0)
    return (
        output,
        input_grad,
        packed[:, 0],
        grad_w[0],
        grad_w[1],
        grad_w[2],
        out_out,
        packed[:, 1],
        packed[:, 2],
        packed[:, 3],
        packed[:, 4 : 4 + EXPERTS],
        out_gate,
        out_up,
        out_down,
    )


def solution(mesh):
    rows = P(BOTH, None)
    vec = P(BOTH)
    expert = P("expert", "dp", None)
    group = P("dp", None)
    return jax.shard_map(
        body,
        mesh=mesh,
        in_specs=(rows, rows, vec, rows, rows, rows, rows, vec, vec, vec, rows, expert, expert, expert)
        + (group, group, group, P("dp", None, None)),
        out_specs=(rows, rows, vec, rows, rows, rows, rows, vec, vec, vec, rows, expert, expert, expert),
        check_vma=False,
    )
```

```python
import functools

import jax
import jax.numpy as jnp
from jax import lax
from jax.experimental import pallas as pl
from jax.experimental.pallas import tpu as pltpu
from jax.sharding import PartitionSpec as P

HEADS = 16
HEAD_DIM = 128
TOPK = 8
EXPERTS = 16
GTOK = 1536
CAP = 768
PROMPT = 1024
CLEN = 128
BLOCKS = GTOK // CLEN
TILE = 256
ROWS = 768
FTILE = 256
NTILE = 384
EPS = 1e-05
BOTH = ("dp", "expert")
F32 = jnp.float32
BF16 = jnp.bfloat16
SCALE = HEAD_DIM ** (-0.5)
NEG = -1e30
SMALL = 128
MESH = pl.DeviceIdType.MESH


def norm_back(grad_rows, unit_rows, inverse, gain_vec):
    grad_unit = grad_rows * gain_vec
    inner_mean = jnp.mean(grad_unit * unit_rows, axis=-1, keepdims=True)
    return inverse * (grad_unit - unit_rows * inner_mean)


def cross_rows(left, right):
    return lax.dot_general(left, right, (((0,), (0,)), ((), ())), preferred_element_type=F32)


def by_transpose(left, right):
    return lax.dot_general(left, right, (((1,), (1,)), ((), ())), preferred_element_type=F32)


def plain(left, right):
    return lax.dot_general(left, right, (((1,), (0,)), ((), ())), preferred_element_type=F32)


def causal(rows):
    return lax.broadcasted_iota(jnp.int32, (rows, rows), 1) <= lax.broadcasted_iota(
        jnp.int32, (rows, rows), 0
    )


def tiles():
    out = []
    for i in range(PROMPT // TILE):
        keys = [(0, i * TILE, False)] if i else []
        out.append((i * TILE, TILE, keys + [(i * TILE, TILE, True)]))
    for c in range(PROMPT // CLEN, BLOCKS):
        out.append((c * CLEN, CLEN, [(0, PROMPT, False), (c * CLEN, CLEN, True)]))
    return out


def rope(values, cos_rows, sin_rows):
    return values * cos_rows + pltpu.roll(values, HEAD_DIM // 2, 1) * sin_rows


def attend_kernel(
    order, q_pre, k_pre, v_pre, inv_q, inv_k, gain_q, gain_k, cos, sin, q_rot, k_rot, v_out, mixed, lse
):
    for i in range(BLOCKS):
        here = pl.ds(i * CLEN, CLEN)
        there = pl.ds(pl.multiple_of(order[i] * CLEN, CLEN), CLEN)
        cos_rows, sin_rows = cos[there, :], sin[there, :]
        q_n = q_pre[there, :] * inv_q[there, :] * gain_q[...]
        k_n = k_pre[there, :] * inv_k[there, :] * gain_k[...]
        q_rot[here, :] = rope(q_n, cos_rows, sin_rows).astype(BF16)
        k_rot[here, :] = rope(k_n, cos_rows, sin_rows).astype(BF16)
        v_out[here, :] = v_pre[there, :].astype(BF16)
    for start, rows, keys in tiles():
        q = q_rot[pl.ds(start, rows), :]
        parts = []
        for k_start, k_rows, masked in keys:
            s = by_transpose(q, k_rot[pl.ds(k_start, k_rows), :]) * SCALE
            parts.append(jnp.where(causal(rows), s, NEG) if masked else s)
        top = functools.reduce(jnp.maximum, [jnp.max(s, axis=1, keepdims=True) for s in parts])
        exps = [jnp.exp(s - top) for s in parts]
        total = functools.reduce(lambda a, b: a + b, [jnp.sum(e, axis=1, keepdims=True) for e in exps])
        over = 1.0 / total
        result = None
        for e, (k_start, k_rows, _) in zip(exps, keys):
            term = plain((e * over).astype(BF16), v_out[pl.ds(k_start, k_rows), :])
            result = term if result is None else result + term
        lse[pl.ds(start, rows), :] = jnp.broadcast_to(top + jnp.log(total), (rows, HEAD_DIM))
        for j in range(rows // CLEN):
            block = start // CLEN + j
            there = pl.ds(pl.multiple_of(order[block] * CLEN, CLEN), CLEN)
            mixed[there, :] = result[j * CLEN : (j + 1) * CLEN].astype(BF16)


def attend(order, qkv, inv_q, inv_k, gain_q, gain_k, cos, sin):
    heads = qkv.shape[1] // (3 * HEAD_DIM)
    head = lambda off: pl.BlockSpec((GTOK, HEAD_DIM), lambda h, o: (0, h + off))
    whole = lambda w: pl.BlockSpec((GTOK, w), lambda h, o: (0, 0))
    gain = pl.BlockSpec((1, HEAD_DIM), lambda h, o: (0, h))
    wide = jax.ShapeDtypeStruct((GTOK, heads * HEAD_DIM), BF16)
    return pl.pallas_call(
        attend_kernel,
        grid_spec=pltpu.PrefetchScalarGridSpec(
            num_scalar_prefetch=1,
            grid=(heads,),
            in_specs=[head(0), head(heads), head(2 * heads), whole(1), whole(1), gain, gain]
            + [whole(HEAD_DIM)] * 2,
            out_specs=[head(0)] * 5,
        ),
        out_shape=[wide] * 4 + [jax.ShapeDtypeStruct((GTOK, heads * HEAD_DIM), F32)],
        compiler_params=pltpu.CompilerParams(vmem_limit_bytes=48 * 2**20),
    )(order, qkv, qkv, qkv, inv_q, inv_k, gain_q, gain_k, cos, sin)


def attend_back_kernel(
    order, q_rot, k_rot, v_in, lse, grad_mixed, cos, sin, dq_out, dk_out, dv_out, grads, dq, dk, dv
):
    for i in range(BLOCKS):
        there = pl.ds(pl.multiple_of(order[i] * CLEN, CLEN), CLEN)
        grads[pl.ds(i * CLEN, CLEN), :] = grad_mixed[there, :]
    dk[...] = jnp.zeros_like(dk)
    dv[...] = jnp.zeros_like(dv)
    for start, rows, keys in tiles():
        here = pl.ds(start, rows)
        q, g, level = q_rot[here, :], grads[here, :], lse[here, 0:1]
        probs, grad_probs, delta = [], [], 0.0
        for k_start, k_rows, masked in keys:
            s = by_transpose(q, k_rot[pl.ds(k_start, k_rows), :]) * SCALE
            s = jnp.where(causal(rows), s, NEG) if masked else s
            p = jnp.exp(s - level)
            gp = by_transpose(g, v_in[pl.ds(k_start, k_rows), :])
            delta = delta + jnp.sum(p * gp, axis=1, keepdims=True)
            probs.append(p)
            grad_probs.append(gp)
        total = None
        for p, gp, (k_start, k_rows, _) in zip(probs, grad_probs, keys):
            there = pl.ds(k_start, k_rows)
            raw = (p * (gp - delta) * SCALE).astype(BF16)
            term = plain(raw, k_rot[there, :])
            total = term if total is None else total + term
            dk[there, :] += cross_rows(raw, q)
            dv[there, :] += cross_rows(p.astype(BF16), g)
        dq[here, :] = total
    for i in range(BLOCKS):
        here = pl.ds(i * CLEN, CLEN)
        there = pl.ds(pl.multiple_of(order[i] * CLEN, CLEN), CLEN)
        cos_rows, sin_rows = cos[there, :], sin[there, :]
        dq_out[there, :] = rope(dq[here, :], cos_rows, -sin_rows)
        dk_out[there, :] = rope(dk[here, :], cos_rows, -sin_rows)
        dv_out[there, :] = dv[here, :].astype(BF16)


def attend_back(order, q_rot, k_rot, v_in, lse, grad_mixed, cos, sin):
    heads = q_rot.shape[1] // HEAD_DIM
    head = pl.BlockSpec((GTOK, HEAD_DIM), lambda h, o: (0, h))
    whole = pl.BlockSpec((GTOK, HEAD_DIM), lambda h, o: (0, 0))
    wide = lambda t: jax.ShapeDtypeStruct((GTOK, heads * HEAD_DIM), t)
    return pl.pallas_call(
        attend_back_kernel,
        grid_spec=pltpu.PrefetchScalarGridSpec(
            num_scalar_prefetch=1,
            grid=(heads,),
            in_specs=[head] * 5 + [whole] * 2,
            out_specs=[head] * 3,
            scratch_shapes=[
                pltpu.VMEM((GTOK, HEAD_DIM), BF16),
                pltpu.VMEM((GTOK, HEAD_DIM), F32),
                pltpu.VMEM((GTOK, HEAD_DIM), F32),
                pltpu.VMEM((GTOK, HEAD_DIM), F32),
            ],
        ),
        out_shape=[wide(F32), wide(F32), wide(BF16)],
        compiler_params=pltpu.CompilerParams(vmem_limit_bytes=48 * 2**20),
    )(order, q_rot, k_rot, v_in, lse, grad_mixed, cos, sin)


ANY = pl.BlockSpec(memory_space=pl.ANY)
VM = pl.BlockSpec(memory_space=pltpu.VMEM)
DMA = pltpu.SemaphoreType.DMA


def params(cid, mib=60):
    return pltpu.CompilerParams(collective_id=cid, has_side_effects=True, vmem_limit_bytes=mib * 2**20)


def peer(i):
    return {"expert": i}


def remote(src, dst, send_sem, recv_sem, to):
    return pltpu.make_async_remote_copy(
        src_ref=src,
        dst_ref=dst,
        send_sem=send_sem,
        recv_sem=recv_sem,
        device_id=to if isinstance(to, dict) else peer(to),
        device_id_type=MESH,
    )


def greet_line(n, others=()):
    p = lax.axis_index("expert")
    bar = pltpu.get_barrier_semaphore()

    @pl.when(p > 0)
    def _():
        pl.semaphore_signal(bar, inc=1, device_id=peer(p - 1), device_id_type=MESH)

    @pl.when(p < n - 1)
    def _():
        pl.semaphore_signal(bar, inc=1, device_id=peer(p + 1), device_id_type=MESH)

    for other in others:
        pl.semaphore_signal(bar, inc=1, device_id=other, device_id_type=MESH)
    pl.semaphore_wait(bar, (p > 0).astype(jnp.int32) + (p < n - 1).astype(jnp.int32) + len(others))
    return p


def greet_all(n):
    p = lax.axis_index("expert")
    bar = pltpu.get_barrier_semaphore()
    for s in range(1, n):
        pl.semaphore_signal(bar, inc=1, device_id=peer(lax.rem(p + s, n)), device_id_type=MESH)
    pl.semaphore_wait(bar, n - 1)
    return p


class Gather:
    sems = lambda n, pieces=1: [DMA((n * pieces,))] * 3

    def __init__(self, p, n, own, at, sems, pieces=1):
        self.p, self.n, self.own, self.at, self.pieces = p, n, own, at, pieces
        self.to_right, self.to_left, self.recv = sems

    def right(self, src, j, c):
        i = j * self.pieces + c
        return remote(src, self.at(j, c), self.to_right.at[i], self.recv.at[i], self.p + 1)

    def left(self, src, j, c):
        i = j * self.pieces + c
        return remote(src, self.at(j, c), self.to_left.at[i], self.recv.at[i], self.p - 1)

    def start(self, c=0):
        @pl.when(self.p < self.n - 1)
        def _():
            self.right(self.own(c), self.p, c).start()

        @pl.when(self.p > 0)
        def _():
            self.left(self.own(c), self.p, c).start()

    def step(self, s, use=None, c=0):
        p, n = self.p, self.n
        j, k = p - s, p + s

        @pl.when(j >= 0)
        def _():
            self.right(self.at(j, c), j, c).wait_recv()

            @pl.when(p < n - 1)
            def _():
                self.right(self.at(j, c), j, c).start()

        @pl.when(k < n)
        def _():
            self.left(self.at(k, c), k, c).wait_recv()

            @pl.when(p > 0)
            def _():
                self.left(self.at(k, c), k, c).start()

        if use is not None:
            for i, here in ((j, j >= 0), (k, k < n)):
                pl.when(here)(functools.partial(use, i))

    def finish(self):
        for j in range(self.n):
            for c in range(self.pieces):

                @pl.when((j <= self.p) & (self.p < self.n - 1))
                def _():
                    self.right(self.own(c), j, c).wait_send()

                @pl.when((j >= self.p) & (self.p > 0))
                def _():
                    self.left(self.own(c), j, c).wait_send()


class Reduce:
    pieces, depth = 4, 2
    sems = lambda n: [DMA((n * Reduce.pieces,))] * 4
    boxes = lambda n, rows, width: [pltpu.VMEM((n * Reduce.pieces, rows // Reduce.pieces, width), BF16)] * 2

    def __init__(self, p, n, rows, part, make, boxes, sems):
        self.p, self.n, self.rows, self.part, self.make = p, n, rows, part, make
        self.from_left, self.from_right = boxes
        self.to_right, self.to_left, self.recv_r, self.recv_l = sems
        self.order = [(s, c) for s in range(n - 1) for c in range(self.pieces)]

    def at(self, j, c):
        size = self.rows // self.pieces
        return self.part.at[pl.ds(pl.multiple_of(j * self.rows + c * size, size), size)]

    def right(self, j, c):
        i = j * self.pieces + c
        return remote(self.at(j, c), self.from_left.at[i], self.to_right.at[i], self.recv_r.at[i], self.p + 1)

    def left(self, j, c):
        i = j * self.pieces + c
        return remote(self.at(j, c), self.from_right.at[i], self.to_left.at[i], self.recv_l.at[i], self.p - 1)

    def add(self, j, c, box):
        total = self.at(j, c)[...].astype(F32) + box[j * self.pieces + c].astype(F32)
        self.at(j, c)[...] = total.astype(BF16)

    def make_step(self, s):
        j, k = self.n - 1 - s, s
        pl.when(j > self.p)(lambda: self.make(j))
        pl.when(k < self.p)(lambda: self.make(k))

    def piece(self, s, c):
        p, n = self.p, self.n
        j, k = n - 1 - s, s
        m = s * self.pieces + c

        @pl.when(j > p)
        def _():
            @pl.when(p > 0)
            def _():
                self.right(j, c).wait_recv()
                self.add(j, c, self.from_left)

            if m >= self.depth:
                s0, c0 = self.order[m - self.depth]
                self.right(n - 1 - s0, c0).wait_send()
            self.right(j, c).start()

        @pl.when(k < p)
        def _():
            @pl.when(p < n - 1)
            def _():
                self.left(k, c).wait_recv()
                self.add(k, c, self.from_right)

            if m >= self.depth:
                s0, c0 = self.order[m - self.depth]
                self.left(s0, c0).wait_send()
            self.left(k, c).start()

    def step(self, s):
        self.make_step(s)
        for c in range(self.pieces):
            self.piece(s, c)

    def finish(self, out, base=None):
        p, n, size = self.p, self.n, self.rows // self.pieces
        self.make(p)
        for c in range(self.pieces):

            @pl.when(p > 0)
            def _():
                self.right(p, c).wait_recv()
                self.add(p, c, self.from_left)

            @pl.when(p < n - 1)
            def _():
                self.left(p, c).wait_recv()
                self.add(p, c, self.from_right)

            here = pl.ds(c * size, size)
            if base is None:
                out[here] = self.at(p, c)[...]
            else:
                out[here] = (base[here].astype(F32) + self.at(p, c)[...].astype(F32)).astype(out.dtype)
        for m, (s, c) in enumerate(self.order):
            pl.when((n - 1 - s > p) & (m >= (n - 1 - p) * self.pieces - self.depth))(
                lambda s=s, c=c: self.right(n - 1 - s, c).wait_send()
            )
            pl.when((s < p) & (m >= p * self.pieces - self.depth))(lambda s=s, c=c: self.left(s, c).wait_send())


def rows_of(ref, rows):
    return lambda j: ref.at[pl.ds(pl.multiple_of(j * rows, rows), rows)]


def ag_kernel(n, rows, x, *rest):
    count = (len(rest) - 7) // 2
    blocks, out, fulls = rest[:count], rest[count], rest[count + 1 : 2 * count + 1]
    to_right, to_left, recv, local, sent, came = rest[2 * count + 1 :]
    d = lax.axis_index("dp")
    core, by_x, by_y = lax.rem(d, 2), lax.rem(d // 2, 2), d // 4
    d_x, d_y, d_c = d + 2 - 4 * by_x, d + 4 - 8 * by_y, d + 1 - 2 * core
    d_far = d_x + 4 - 8 * by_y
    x_way, y_way, c_way = {"dp": d_x}, {"dp": d_y}, {"dp": d_c}
    p = greet_line(n, (x_way, y_way, c_way) if count else ())
    at = rows_of(out, rows)
    own = pltpu.make_async_copy(x, at(p), local.at[0])
    own.start()
    line = Gather(p, n, lambda c: x, lambda j, c: at(j), (to_right, to_left, recv))
    line.start()

    def send(a, src, first, size, kind, way):
        dst = fulls[a].at[pl.ds(pl.multiple_of(first, size), size)]
        return remote(dst if src is None else src, dst, sent.at[a, kind], came.at[a, kind], way)

    def moves(a):
        size = blocks[a].shape[0]
        half = size // 2
        return [
            lambda: send(a, blocks[a], d * size, size, 0, x_way),
            lambda: send(a, blocks[a], d * size, size, 1, y_way),
            lambda: send(a, blocks[a], d * size, size, 2, c_way),
            lambda: send(a, None, d_x * size, half, 3, y_way),
            lambda: send(a, None, d_y * size + half, half, 4, x_way),
            lambda: send(a, None, d_x * size, size, 5, c_way),
            lambda: send(a, None, d_y * size, size, 6, c_way),
            lambda: send(a, None, d_far * size, size, 7, c_way),
        ]

    all_moves = [moves(a) for a in range(count)]
    locals_ = [
        pltpu.make_async_copy(
            blocks[a],
            fulls[a].at[pl.ds(pl.multiple_of(d * blocks[a].shape[0], blocks[a].shape[0]), blocks[a].shape[0])],
            local.at[a + 1],
        )
        for a in range(count)
    ]
    for a in range(count):
        locals_[a].start()
        for k in range(3):
            all_moves[a][k]().start()
    for a in range(count):
        for k in (0, 1):
            all_moves[a][k]().wait_recv()
        for k in (3, 4, 5, 6):
            all_moves[a][k]().start()
    line.step(1)
    for a in range(count):
        for k in (3, 4):
            all_moves[a][k]().wait_recv()
        all_moves[a][7]().start()
    for s in range(2, n):
        line.step(s)
    for a in range(count):
        locals_[a].wait()
        for k in (2, 5, 6, 7):
            all_moves[a][k]().wait_recv()
        for k in range(8):
            all_moves[a][k]().wait_send()
    own.wait()
    line.finish()


def ag_z(x, n, cid, blocks=()):
    rows = x.shape[0]
    count = len(blocks)
    grown = lambda b, k: jax.ShapeDtypeStruct((k * b.shape[0],) + b.shape[1:], b.dtype)
    return pl.pallas_call(
        functools.partial(ag_kernel, n, rows),
        out_shape=[grown(x, n)] + [grown(b, 8) for b in blocks],
        in_specs=[ANY] * (1 + count),
        out_specs=[ANY] * (1 + count),
        scratch_shapes=Gather.sems(n) + [DMA((1 + count,)), DMA((max(count, 1), 8)), DMA((max(count, 1), 8))],
        compiler_params=params(cid),
    )(x, *blocks)


def gather_kernel(n, rows, x, slot, small, grads, logits, rows_out, grads_out, *rest):
    shards, picked, picked_grads, to_right, to_left, recv, out_sems = rest
    p = greet_line(n)
    experts = slot.shape[1]
    line = Gather(p, n, lambda c: x, lambda j, c: shards.at[j], (to_right, to_left, recv))
    line.start()

    def pick(j, e):
        places = lax.broadcasted_iota(jnp.int32, (CAP, rows), 0)
        return (slot[j, e : e + 1] == places).astype(F32).astype(BF16)

    def use(j, block, first=False):
        logits[pl.ds(pl.multiple_of(j * rows, rows), rows), :] = plain(block[...], small[...])
        for e in range(experts):
            new = plain(pick(j, e), block[...])
            picked[e] = new.astype(BF16) if first else (picked[e].astype(F32) + new).astype(BF16)

    def copy_out(e, src, dst, k):
        return pltpu.make_async_copy(src.at[e], dst.at[e], out_sems.at[k, e])

    use(p, x, True)
    for e in range(experts):
        for j in range(n):
            new = plain(pick(j, e), grads[j * rows : (j + 1) * rows])
            picked_grads[e] = new.astype(BF16) if j == 0 else (picked_grads[e].astype(F32) + new).astype(BF16)
        copy_out(e, picked_grads, grads_out, 1).start()
    for s in range(1, n):
        line.step(s, lambda j: use(j, shards.at[j]))
    for e in range(experts):
        copy_out(e, picked, rows_out, 0).start()
    for e in range(experts):
        copy_out(e, picked, rows_out, 0).wait()
        copy_out(e, picked_grads, grads_out, 1).wait()
    line.finish()


def gather_rows(x, slot, small, grads, n, cid):
    rows, width = x.shape
    experts = slot.shape[1]
    wide = (experts, CAP, width)
    return pl.pallas_call(
        functools.partial(gather_kernel, n, rows),
        out_shape=[
            jax.ShapeDtypeStruct((n * rows, small.shape[1]), F32),
            jax.ShapeDtypeStruct(wide, BF16),
            jax.ShapeDtypeStruct(wide, BF16),
        ],
        in_specs=[VM] * 4,
        out_specs=[VM, ANY, ANY],
        scratch_shapes=[pltpu.VMEM((n, rows, width), BF16), pltpu.VMEM(wide, BF16), pltpu.VMEM(wide, BF16)]
        + Gather.sems(n)
        + [DMA((2, experts))],
        compiler_params=params(cid),
    )(x, slot, small, grads)


def rs_kernel(n, rows, part, out, left_box, right_box, *sems):
    p = greet_line(n)
    line = Reduce(p, n, rows, part, lambda j: None, (left_box, right_box), sems)
    for s in range(n - 1):
        line.step(s)
    line.finish(out)


def rs_z(part, n, cid):
    rows, width = part.shape[0] // n, part.shape[1]
    return pl.pallas_call(
        functools.partial(rs_kernel, n, rows),
        out_shape=jax.ShapeDtypeStruct((rows, width), BF16),
        in_specs=[VM],
        out_specs=VM,
        scratch_shapes=Reduce.boxes(n, rows, width) + Reduce.sems(n),
        compiler_params=params(cid),
    )(part)


def combine(part, rows, slot, weight, blocks):
    def make(j):
        total, e = None, 0
        for block in blocks:
            for i in range(block.shape[0]):
                places = lax.broadcasted_iota(jnp.int32, (rows, CAP), 1)
                chosen = slot[j, :, e : e + 1] == places
                scale = 1.0 if weight is None else weight[j, :, e : e + 1]
                term = plain(jnp.where(chosen, scale, 0.0).astype(BF16), block[i])
                total = term if total is None else total + term
                e += 1
        part[pl.ds(pl.multiple_of(j * rows, rows), rows), :] = total.astype(BF16)

    return make


def combine_kernel(n, rows, slot, low, high, out, part, left_box, right_box, *sems):
    p = greet_line(n)
    make = combine(part, rows, slot, None, (low, high))
    line = Reduce(p, n, rows, part, make, (left_box, right_box), sems)
    for s in range(n - 1):
        line.step(s)
    line.finish(out)


def combine_z(slot, low, high, n, cid):
    rows, width = slot.shape[1], low.shape[2]
    return pl.pallas_call(
        functools.partial(combine_kernel, n, rows),
        out_shape=jax.ShapeDtypeStruct((rows, width), BF16),
        in_specs=[VM] * 3,
        out_specs=VM,
        scratch_shapes=[pltpu.VMEM((n * rows, width), BF16)] + Reduce.boxes(n, rows, width) + Reduce.sems(n),
        compiler_params=params(cid),
    )(slot, low, high)


def both_kernel(n, rows, x, slot, weight, low, high, base, all_out, out, part, left_box, right_box, *sems):
    p = greet_line(n)
    at = rows_of(all_out, rows)
    own = pltpu.make_async_copy(x, at(p), sems[7])
    own.start()
    size = rows // Reduce.pieces
    piece = lambda j, c: all_out.at[pl.ds(pl.multiple_of(j * rows + c * size, size), size)]
    gather = Gather(p, n, lambda c: x.at[pl.ds(c * size, size)], piece, sems[:3], Reduce.pieces)
    make = combine(part, rows, slot, weight, (low, high))
    line = Reduce(p, n, rows, part, make, (left_box, right_box), sems[3:7])
    for s in range(n):
        if s == 0:
            gather.start(0)
            gather.start(1)
        if s < n - 1:
            line.make_step(s)
        for c in range(Reduce.pieces):
            if s:
                gather.step(s, c=c)
            elif c > 1:
                gather.start(c)
            if s < n - 1:
                line.piece(s, c)
    line.finish(out, base)
    own.wait()
    gather.finish()


def gather_and_combine(x, slot, weight, low, high, base, n, cid):
    rows, width = x.shape
    return pl.pallas_call(
        functools.partial(both_kernel, n, rows),
        out_shape=[jax.ShapeDtypeStruct((n * rows, width), x.dtype), jax.ShapeDtypeStruct((rows, width), BF16)],
        in_specs=[ANY] + [VM] * 5,
        out_specs=[ANY, VM],
        scratch_shapes=[pltpu.VMEM((n * rows, width), BF16)]
        + Reduce.boxes(n, rows, width)
        + Gather.sems(n, Reduce.pieces)
        + Reduce.sems(n)
        + [DMA],
        compiler_params=params(cid),
    )(x, slot, weight, low, high, base)


def a2a_kernel(n,rows,cols,x,out,send,recv,local):
    p=greet_all(n)
    src=lambda j: x.at[pl.ds(pl.multiple_of(j*rows,rows),rows)]
    dst=lambda c: out.at[:,pl.ds(pl.multiple_of(c*cols,cols),cols)]
    own=pltpu.make_async_copy(src(p),dst(p),local); own.start()
    def send_to(s):
        j=lax.rem(p+s,n)
        return pltpu.make_async_remote_copy(src_ref=src(j),dst_ref=dst(p),send_sem=send.at[s],recv_sem=recv.at[s],device_id=peer(j),device_id_type=MESH)
    for s in range(1,n): send_to(s).start()
    for s in range(1,n):
        c=lax.rem(p-s+n,n)
        pltpu.make_async_remote_copy(src_ref=src(p),dst_ref=dst(c),send_sem=send.at[s],recv_sem=recv.at[s],device_id=peer(c),device_id_type=MESH).wait_recv()
    for s in range(1,n): send_to(s).wait_send()
    own.wait()

def a2a_z(x,n,cid):
    rows=x.shape[0]//n; cols=x.shape[1]
    return pl.pallas_call(functools.partial(a2a_kernel,n,rows,cols),out_shape=jax.ShapeDtypeStruct((rows,n*cols),x.dtype),
        in_specs=[ANY],out_specs=ANY,scratch_shapes=[DMA((n,))]*2+[DMA],
        compiler_params=params(cid))(x)

def exchange_kernel(n, rows, x, out, send, recv, local):
    p = greet_all(n)
    at = lambda ref, j: ref.at[pl.ds(pl.multiple_of(j * rows, rows), rows)]
    own = pltpu.make_async_copy(at(x, p), at(out, p), local)
    own.start()

    def to(s):
        j = lax.rem(p + s, n)
        return pltpu.make_async_remote_copy(
            src_ref=at(x, j), dst_ref=at(out, p), send_sem=send.at[s], recv_sem=recv.at[s], device_id=peer(j),
            device_id_type=MESH,
        )

    for s in range(1, n):
        to(s).start()
    for s in range(1, n):
        to(s).wait_recv()
    for s in range(1, n):
        to(s).wait_send()
    own.wait()


def exchange_z(x, n, cid):
    return pl.pallas_call(
        functools.partial(exchange_kernel, n, x.shape[0] // n),
        out_shape=jax.ShapeDtypeStruct(x.shape, x.dtype),
        in_specs=[ANY],
        out_specs=ANY,
        scratch_shapes=[DMA((n,))] * 2 + [DMA],
        compiler_params=params(cid),
    )(x)


def sum_kernel(n,x,out,got,send,recv):
    p=greet_all(n)
    def send_to(s):
        return pltpu.make_async_remote_copy(src_ref=x,dst_ref=got.at[s],send_sem=send.at[s],recv_sem=recv.at[s],device_id=peer(lax.rem(p+s,n)),device_id_type=MESH)
    for s in range(1,n): send_to(s).start()
    tot=x[...]
    for s in range(1,n):
        send_to(s).wait_recv(); tot=tot+got[s]
    out[...]=tot
    for s in range(1,n): send_to(s).wait_send()

def sum_z(x,n,cid):
    return pl.pallas_call(functools.partial(sum_kernel,n),out_shape=jax.ShapeDtypeStruct(x.shape,x.dtype),in_specs=[VM],out_specs=VM,
        scratch_shapes=[pltpu.VMEM((n,)+x.shape,x.dtype)]+[DMA((n,))]*2,compiler_params=params(cid))(x)


def expert_kernel(
    slot, weight, x, g, gate, up, down, eo_out, gin_out, route_out, gu_out, gd_out, xt, w_col, both, scaled, eo, gin
):
    f = pl.program_id(1)
    tile = gate.shape[2]
    chunks = CAP // ROWS
    tokens = slot.shape[2]
    x, g = x.at[0], g.at[0]

    def one_hot(start):
        place = lax.broadcasted_iota(jnp.int32, (ROWS, tokens), 0) + start
        return slot[0] == place

    @pl.when(f == 0)
    def _():
        @pl.loop(0, chunks)
        def _(c):
            here = pl.ds(pl.multiple_of(c * ROWS, ROWS), ROWS)
            chosen = one_hot(c * ROWS)
            w_col[here, :] = jnp.sum(jnp.where(chosen, weight[0], 0.0), axis=1, keepdims=True)
            eo[here, :] = jnp.zeros((ROWS, x.shape[1]), F32)
            gin[here, :] = jnp.zeros((ROWS, x.shape[1]), F32)

        xt[...] = x[...].T

    @pl.loop(0, chunks)
    def _(c):
        here = pl.ds(pl.multiple_of(c * ROWS, ROWS), ROWS)
        a = plain(x[here, :], gate[0])
        b = plain(x[here, :], up[0])
        h = by_transpose(g[here, :], down[0]) * w_col[here, :]
        sig = 1.0 / (1.0 + jnp.exp(-a))
        silu = a * sig
        hidden = silu * b
        gg = (h * b * (sig * (1.0 + a * (1.0 - sig)))).astype(BF16)
        gu = (h * silu).astype(BF16)
        both[here, 0:tile] = gg
        both[here, tile : 2 * tile] = gu
        scaled[here, :] = (hidden * w_col[here, :]).astype(BF16)
        eo[here, :] += plain(hidden.astype(BF16), down[0])
        gin[here, :] += by_transpose(gg, gate[0]) + by_transpose(gu, up[0])

    pieces, rows = gu_out.shape[0], gu_out.shape[3]

    grad_both = plain(xt[...], both[...]).astype(BF16)
    for c in range(pieces):
        gu_out[c, 0, 0] = grad_both[c * rows : (c + 1) * rows, :tile]
        gu_out[c, 1, 0] = grad_both[c * rows : (c + 1) * rows, tile:]

    down_rows = gd_out.shape[2]
    grad_down = cross_rows(scaled[...], g[...]).astype(BF16)
    for c in range(gd_out.shape[0]):
        gd_out[c, 0] = grad_down[c * down_rows : (c + 1) * down_rows]

    @pl.when(f == pl.num_programs(1) - 1)
    def _():
        eo_out[0] = eo[...].astype(BF16)
        gin_out[0] = gin[...].astype(BF16)
        route = jnp.zeros((1, tokens), F32)
        for c in range(chunks):
            here = pl.ds(c * ROWS, ROWS)
            dots = jnp.sum(eo[here, :].astype(BF16).astype(F32) * g[here, :].astype(F32), axis=1, keepdims=True)
            route = route + jnp.sum(jnp.where(one_hot(c * ROWS), dots, 0.0), axis=0, keepdims=True)
        route_out[0] = route


def experts(first, count, dp, slot, weight, x, g, gate, up, down):
    tokens, width = slot.shape[2], x.shape[2]
    ff = gate.shape[2]
    steps = ff // FTILE
    line = pl.BlockSpec((1, 1, tokens), lambda e, f: (first + e, 0, 0))
    column = pl.BlockSpec((1, width, FTILE), lambda e, f: (first + e, 0, f))
    row = pl.BlockSpec((1, FTILE, width), lambda e, f: (first + e, f, 0))
    slots_in = pl.BlockSpec((1, CAP, width), lambda e, f: (first + e, 0, 0), pipeline_mode=pl.Buffered(2))
    slots_out = pl.BlockSpec((1, CAP, width), lambda e, f: (e, 0, 0), pipeline_mode=pl.Buffered(1))
    down_rows = ff // dp
    return pl.pallas_call(
        expert_kernel,
        grid=(count, steps),
        in_specs=[line, line, slots_in, slots_in, column, column, row],
        out_specs=[
            slots_out,
            slots_out,
            pl.BlockSpec((1, 1, tokens), lambda e, f: (e, 0, 0)),
            pl.BlockSpec((dp, 2, 1, width // dp, FTILE), lambda e, f: (0, 0, e, 0, f)),
            pl.BlockSpec((FTILE // down_rows, 1, down_rows, width), lambda e, f: (f, e, 0, 0)),
        ],
        out_shape=[
            jax.ShapeDtypeStruct((count, CAP, width), BF16),
            jax.ShapeDtypeStruct((count, CAP, width), BF16),
            jax.ShapeDtypeStruct((count, 1, tokens), F32),
            jax.ShapeDtypeStruct((dp, 2, count, width // dp, ff), BF16),
            jax.ShapeDtypeStruct((dp, count, down_rows, width), BF16),
        ],
        scratch_shapes=[
            pltpu.VMEM((width, CAP), BF16),
            pltpu.VMEM((CAP, 1), F32),
            pltpu.VMEM((CAP, 2 * FTILE), BF16),
            pltpu.VMEM((CAP, FTILE), BF16),
            pltpu.VMEM((CAP, width), F32),
            pltpu.VMEM((CAP, width), F32),
        ],
        compiler_params=pltpu.CompilerParams(vmem_limit_bytes=60 * 2**20),
    )(slot, weight, x, g, gate, up, down)


def row_moves(ways, dp):
    return [(d * ways + z, z * dp + d) for d in range(dp) for z in range(ways)]


def hops(up, down, count, ways):
    for _ in range(count):
        h = len(up)
        up = up + [lax.ppermute(up[-1], "expert", [(i, i + 1) for i in range(h - 1, ways - 1)])]
        down = down + [lax.ppermute(down[-1], "expert", [(i + 1, i) for i in range(ways - h)])]
    return up, down


def later(sent, other):
    up, down = sent
    last_up, last_down, other = lax.optimization_barrier((up[-1], down[-1], other))
    return up[:-1] + [last_up], down[:-1] + [last_down], other


def line_up(up, down, ways):
    line = jnp.concatenate(up[:0:-1] + down, axis=0)
    rows = down[0].shape[0]
    start = (ways - 1 - lax.axis_index("expert")) * rows
    return lax.dynamic_slice_in_dim(line, start, ways * rows, axis=0)


def norm_qkv_kernel(columns, x, gain, weight, out, normed, inverse):
    values = x[...].astype(F32)
    inv = lax.rsqrt(jnp.mean(values * values, axis=1, keepdims=True) + EPS)
    rows = (values * inv * gain[...]).astype(BF16)
    inverse[...] = inv
    normed[...] = rows
    out[...] = plain(rows, weight[:, :columns])


def norm_qkv(x, gain, weight, columns):
    tokens, width = x.shape
    tile = lambda w: pl.BlockSpec((NTILE, w), lambda i: (i, 0))
    return pl.pallas_call(
        functools.partial(norm_qkv_kernel, columns),
        grid=(tokens // NTILE,),
        in_specs=[
            tile(width),
            pl.BlockSpec((1, width), lambda i: (0, 0)),
            pl.BlockSpec(weight.shape, lambda i: (0, 0), pipeline_mode=pl.Buffered(1)),
        ],
        out_specs=[tile(columns), tile(width), tile(1)],
        out_shape=[
            jax.ShapeDtypeStruct((tokens, columns), F32),
            jax.ShapeDtypeStruct((tokens, width), BF16),
            jax.ShapeDtypeStruct((tokens, 1), F32),
        ],
        compiler_params=pltpu.CompilerParams(vmem_limit_bytes=48 * 2**20),
    )(x, gain, weight)


def block_order(segs, places):
    seg = segs.reshape(BLOCKS, CLEN)[:, 0]
    place = places.reshape(BLOCKS, CLEN)[:, 0]
    stand = jnp.where(seg == 0, place // CLEN, PROMPT // CLEN - 1 + seg)
    blocks = jnp.arange(BLOCKS, dtype=jnp.int32)
    return jnp.sum(jnp.where(stand[None, :] == blocks[:, None], blocks[None, :], 0), axis=1)


def slots(routes, priority):
    experts = jnp.arange(EXPERTS, dtype=jnp.int32)
    hits = jnp.any(routes[:, :, None] == experts[None, None, :], axis=1)
    index = jnp.arange(GTOK, dtype=jnp.int32)
    rank = jnp.sum(jnp.where(priority[:, None] == index[None, :], index[:, None], 0), axis=0)
    earlier = (rank[None, :] < rank[:, None]).astype(BF16)
    return hits, plain(earlier, hits.astype(BF16)).astype(jnp.int32)


def body(
    tokens,
    cotangent,
    attention_gain,
    query_weight,
    key_weight,
    value_weight,
    out_weight,
    query_norm,
    key_norm,
    mixture_gain,
    router_weight,
    gate_weight,
    up_weight,
    down_weight,
    segments,
    positions,
    priority,
    routes,
):
    tok_dev, width = tokens.shape
    experts_here = gate_weight.shape[0]
    ways = lax.axis_size("expert")
    z = lax.axis_index("expert")
    cols = width // ways
    first_row = z * tok_dev

    small = jnp.concatenate(
        [attention_gain[:, None], query_norm[:, None], key_norm[:, None], mixture_gain[:, None], router_weight],
        axis=1,
    )
    small = jnp.pad(small, ((0, 0), (0, SMALL - small.shape[1])))
    shard = jnp.stack([query_weight, key_weight, value_weight], axis=1)
    shard = shard.reshape(-1, 3, ways, cols).transpose(2, 0, 1, 3).reshape(ways, -1, 3 * cols)
    rest = jnp.concatenate([small, out_weight], axis=1)
    shard = jnp.concatenate([shard, jnp.broadcast_to(rest[None], (ways,) + rest.shape)], axis=2)
    shard = exchange_z(shard.reshape(-1, shard.shape[-1]), ways, 1)
    shards = shard[:, : 3 * cols + SMALL], shard[:, 3 * cols + SMALL :]
    if lax.axis_size("dp") == 8:
        tokens_all, dense, out_full = ag_z(tokens, ways, 2, shards)
    else:
        (tokens_all,) = ag_z(tokens, ways, 2)
        dense, out_full = (lax.all_gather(s, "dp", axis=0, tiled=True) for s in shards)
    qkv_weight = dense[:, : 3 * cols]
    small = dense[:, 3 * cols :]
    attend_gain = small[:, 0].astype(F32)
    mix_gain = small[:, 3].astype(F32)
    router_full = small[:, 4 : 4 + EXPERTS]
    my_gains = lax.dynamic_slice_in_dim(small[:, 1:3], z * cols, cols, axis=0).astype(F32)
    gain_q, gain_k = my_gains[:, 0][None], my_gains[:, 1][None]
    out_mine = lax.dynamic_slice_in_dim(out_full, z * cols, cols, axis=0)
    gate_full = lax.all_gather(gate_weight, "dp", axis=1, tiled=True)
    up_full = lax.all_gather(up_weight, "dp", axis=1, tiled=True)
    down_full = lax.all_gather(down_weight, "dp", axis=1, tiled=True)
    steps = [ways // 2, (3 * ways) // 4]
    early, tokens_all = lax.optimization_barrier((cotangent, tokens_all))
    sent = hops([early], [early], steps[0] - 1, ways)

    segs, places = segments[0], positions[0]
    order = block_order(segs, places)
    frequency = 10000.0 ** (-jnp.arange(0, HEAD_DIM // 2, dtype=F32) * 2.0 / HEAD_DIM)
    angles = places.astype(F32)[:, None] * frequency[None, :]
    cos, sin = jnp.cos(angles), jnp.sin(angles)
    cos = jnp.concatenate([cos, cos], axis=1)
    sin = jnp.concatenate([-sin, sin], axis=1)
    hits, slot = slots(routes[0], priority[0])
    my_hits = lax.dynamic_slice_in_dim(hits, z * experts_here, experts_here, axis=1)
    my_slot = lax.dynamic_slice_in_dim(slot, z * experts_here, experts_here, axis=1)
    my_slot = jnp.where(my_hits & (my_slot < CAP), my_slot, -1)
    slot_lines = my_slot.T[:, None, :]
    slot_shards = my_slot.T.reshape(experts_here, ways, tok_dev).transpose(1, 0, 2)
    slot_cols = my_slot.reshape(ways, tok_dev, experts_here)

    qkv, normed, inverse_in = norm_qkv(tokens_all, attend_gain[None], dense, 3 * cols)
    squares = jnp.sum(jnp.square(qkv[:, : 2 * cols]).reshape(GTOK, 2, cols), axis=-1)
    squares = sum_z(jnp.pad(squares.T, ((0, 6), (0, 0))), ways, 3)
    up, down, squares = later(sent, squares)
    sent = hops(up, down, steps[1] - steps[0], ways)
    inv_q = lax.rsqrt(squares[0] / width + EPS)[:, None]
    inv_k = lax.rsqrt(squares[1] / width + EPS)[:, None]
    q_rot, k_rot, v_b, mixed_heads, lse = attend(order, qkv, inv_q, inv_k, gain_q, gain_k, cos, sin)
    up, down, mixed_heads = later(sent, mixed_heads)
    grad_all = line_up(*hops(up, down, ways - steps[1], ways), ways)
    mixed = a2a_z(mixed_heads, ways, 4)
    own_f = tokens.astype(F32)
    resid = own_f + plain(mixed, out_full)
    mix_inverse = lax.rsqrt(jnp.mean(resid * resid, axis=-1, keepdims=True) + EPS)
    mix_unit = resid * mix_inverse
    mix = (mix_unit * mix_gain).astype(BF16)
    logits, inputs, grad_rows = gather_rows(mix, slot_shards, small, grad_all, ways, 5)

    router_all = jax.nn.softmax(logits[:, 4 : 4 + EXPERTS], axis=-1)
    my_weight = lax.dynamic_slice_in_dim(router_all, z * experts_here, experts_here, axis=1)
    weight_lines = my_weight.T[:, None, :]
    weight_cols = my_weight.reshape(ways, tok_dev, experts_here)
    half = experts_here // 2
    work = (half, lax.axis_size("dp"), slot_lines, weight_lines, inputs, grad_rows, gate_full, up_full, down_full)
    out_low, in_low, route_low, both_low, down_low = experts(0, *work)
    sum_both_low = lax.psum_scatter(both_low, "dp", scatter_dimension=0, tiled=True)
    sum_down_low = lax.psum_scatter(down_low, "dp", scatter_dimension=0, tiled=True)
    out_high, in_high, route_high, both_high, down_high = experts(half, *work)
    sum_both_high = lax.psum_scatter(both_high, "dp", scatter_dimension=0, tiled=True)
    sum_down_high = lax.psum_scatter(down_high, "dp", scatter_dimension=0, tiled=True)
    my_route_grad = jnp.concatenate([route_low, route_high], axis=0)[:, 0]
    route_grad = lax.all_to_all(my_route_grad, "expert", split_axis=1, concat_axis=0, tiled=True).T
    grad_routed = combine_z(slot_cols, in_low, in_high, ways, 6).astype(F32)

    router = lax.dynamic_slice_in_dim(router_all, first_row, tok_dev, axis=0)
    grad_logits = (router * (route_grad - jnp.sum(router * route_grad, axis=-1, keepdims=True))).astype(BF16)
    grad_router_w = cross_rows(mix, grad_logits)
    grad_mix = grad_routed + by_transpose(grad_logits, router_full)
    grad_mix_gain = jnp.sum(grad_mix * mix_unit, axis=0)
    grad_resid = cotangent.astype(F32) + norm_back(grad_mix, mix_unit, mix_inverse, mix_gain)
    grad_branch = grad_resid.astype(BF16)
    grad_branch, sum_both_low, sum_down_low = lax.optimization_barrier((grad_branch, sum_both_low, sum_down_low))
    branch_all, output = gather_and_combine(grad_branch, slot_cols, weight_cols, out_low, out_high, resid, ways, 7)
    grad_heads = by_transpose(branch_all, out_mine).astype(BF16)
    grad_out_w = cross_rows(mixed_heads, branch_all).astype(BF16)
    out_out = lax.psum_scatter(grad_out_w, "dp", scatter_dimension=0, tiled=True)
    out_out = lax.ppermute(out_out, BOTH, row_moves(ways, lax.axis_size("dp"))).astype(F32)

    grad_heads, sum_both_high = lax.optimization_barrier((grad_heads, sum_both_high))
    dq, dk, dv = attend_back(order, q_rot, k_rot, v_b, lse, grad_heads, cos, sin)
    q_unit = qkv[:, :cols] * inv_q
    k_unit = qkv[:, cols : 2 * cols] * inv_k
    inner = jnp.stack(
        [jnp.sum(dq * gain_q * q_unit, axis=-1), jnp.sum(dk * gain_k * k_unit, axis=-1)], axis=0
    )
    inner = sum_z(jnp.pad(inner, ((0, 6), (0, 0))), ways, 8) / width
    grad_q_gain = jnp.sum(dq * q_unit, axis=0)
    grad_k_gain = jnp.sum(dk * k_unit, axis=0)
    grad_q = (inv_q * (dq * gain_q - q_unit * inner[0][:, None])).astype(BF16)
    grad_k = (inv_k * (dk * gain_k - k_unit * inner[1][:, None])).astype(BF16)
    grad_qkv = jnp.concatenate([grad_q, grad_k, dv], axis=1)
    grad_normed_part = by_transpose(grad_qkv, qkv_weight)
    grad_attend_gain = jnp.sum(grad_normed_part * (tokens_all.astype(F32) * inverse_in), axis=0)
    part, sum_down_high = lax.optimization_barrier((grad_normed_part.astype(BF16), sum_down_high))
    grad_normed = rs_z(part, ways, 9).astype(F32)
    own_inverse = lax.dynamic_slice_in_dim(inverse_in, first_row, tok_dev, axis=0)
    input_grad = grad_resid + norm_back(grad_normed, own_f * own_inverse, own_inverse, attend_gain)

    place = lambda part: lax.dynamic_update_slice(jnp.zeros((width,), F32), part, (z * cols,))
    extra = jnp.concatenate(
        [
            jnp.stack([grad_attend_gain, place(grad_q_gain), place(grad_k_gain), grad_mix_gain], axis=1),
            grad_router_w,
            jnp.zeros((width, SMALL - 4 - EXPERTS), F32),
        ],
        axis=1,
    )
    grad_qkv_w = jnp.concatenate([cross_rows(normed, grad_qkv), extra], axis=1).astype(BF16)
    grad_qkv_w = lax.psum_scatter(grad_qkv_w, "dp", scatter_dimension=0, tiled=True)
    grad_qkv_w = exchange_z(grad_qkv_w, ways, 10).reshape(ways, -1, 3 * cols + SMALL)
    grad_w = [
        grad_qkv_w[:, :, i * cols : (i + 1) * cols].transpose(1, 0, 2).reshape(-1, width).astype(F32)
        for i in range(3)
    ]
    planes = [jnp.concatenate([sum_both_low[0, i], sum_both_high[0, i]], axis=0) for i in range(2)]
    out_gate, out_up = planes[0].astype(F32), planes[1].astype(F32)
    out_down = jnp.concatenate([sum_down_low[0], sum_down_high[0]], axis=0).astype(F32)
    packed = jnp.sum(grad_qkv_w[:, :, 3 * cols :].astype(F32), axis=0)
    return (
        output,
        input_grad,
        packed[:, 0],
        grad_w[0],
        grad_w[1],
        grad_w[2],
        out_out,
        packed[:, 1],
        packed[:, 2],
        packed[:, 3],
        packed[:, 4 : 4 + EXPERTS],
        out_gate,
        out_up,
        out_down,
    )


def solution(mesh):
    rows = P(BOTH, None)
    vec = P(BOTH)
    expert = P("expert", "dp", None)
    group = P("dp", None)
    return jax.shard_map(
        body,
        mesh=mesh,
        in_specs=(rows, rows, vec, rows, rows, rows, rows, vec, vec, vec, rows, expert, expert, expert)
        + (group, group, group, P("dp", None, None)),
        out_specs=(rows, rows, vec, rows, rows, rows, rows, vec, vec, vec, rows, expert, expert, expert),
        check_vma=False,
    )
```

```python
import functools

import jax
import jax.numpy as jnp
from jax import lax
from jax.experimental import pallas as pl
from jax.experimental.pallas import tpu as pltpu
from jax.sharding import PartitionSpec as P

HEADS = 16
HEAD_DIM = 128
TOPK = 8
EXPERTS = 16
GTOK = 1536
CAP = 768
PROMPT = 1024
CLEN = 128
BLOCKS = GTOK // CLEN
TILE = 256
ROWS = 768
FTILE = 256
NTILE = 384
EPS = 1e-05
BOTH = ("dp", "expert")
F32 = jnp.float32
BF16 = jnp.bfloat16
SCALE = HEAD_DIM ** (-0.5)
NEG = -1e30
SMALL = 128
MESH = pl.DeviceIdType.MESH


def norm_back(grad_rows, unit_rows, inverse, gain_vec):
    grad_unit = grad_rows * gain_vec
    inner_mean = jnp.mean(grad_unit * unit_rows, axis=-1, keepdims=True)
    return inverse * (grad_unit - unit_rows * inner_mean)


def cross_rows(left, right):
    return lax.dot_general(left, right, (((0,), (0,)), ((), ())), preferred_element_type=F32)


def by_transpose(left, right):
    return lax.dot_general(left, right, (((1,), (1,)), ((), ())), preferred_element_type=F32)


def plain(left, right):
    return lax.dot_general(left, right, (((1,), (0,)), ((), ())), preferred_element_type=F32)


def causal(rows):
    return lax.broadcasted_iota(jnp.int32, (rows, rows), 1) <= lax.broadcasted_iota(
        jnp.int32, (rows, rows), 0
    )


def tiles():
    out = []
    for i in range(PROMPT // TILE):
        keys = [(0, i * TILE, False)] if i else []
        out.append((i * TILE, TILE, keys + [(i * TILE, TILE, True)]))
    for c in range(PROMPT // CLEN, BLOCKS):
        out.append((c * CLEN, CLEN, [(0, PROMPT, False), (c * CLEN, CLEN, True)]))
    return out


def rope(values, cos_rows, sin_rows):
    return values * cos_rows + pltpu.roll(values, HEAD_DIM // 2, 1) * sin_rows


def attend_kernel(
    order, q_pre, k_pre, v_pre, inv_q, inv_k, gain_q, gain_k, cos, sin, q_rot, k_rot, v_out, mixed, lse
):
    for i in range(BLOCKS):
        here = pl.ds(i * CLEN, CLEN)
        there = pl.ds(pl.multiple_of(order[i] * CLEN, CLEN), CLEN)
        cos_rows, sin_rows = cos[there, :], sin[there, :]
        q_n = q_pre[there, :] * inv_q[there, :] * gain_q[...]
        k_n = k_pre[there, :] * inv_k[there, :] * gain_k[...]
        q_rot[here, :] = rope(q_n, cos_rows, sin_rows).astype(BF16)
        k_rot[here, :] = rope(k_n, cos_rows, sin_rows).astype(BF16)
        v_out[here, :] = v_pre[there, :].astype(BF16)
    for start, rows, keys in tiles():
        q = q_rot[pl.ds(start, rows), :]
        parts = []
        for k_start, k_rows, masked in keys:
            s = by_transpose(q, k_rot[pl.ds(k_start, k_rows), :]) * SCALE
            parts.append(jnp.where(causal(rows), s, NEG) if masked else s)
        top = functools.reduce(jnp.maximum, [jnp.max(s, axis=1, keepdims=True) for s in parts])
        exps = [jnp.exp(s - top) for s in parts]
        total = functools.reduce(lambda a, b: a + b, [jnp.sum(e, axis=1, keepdims=True) for e in exps])
        over = 1.0 / total
        result = None
        for e, (k_start, k_rows, _) in zip(exps, keys):
            term = plain((e * over).astype(BF16), v_out[pl.ds(k_start, k_rows), :])
            result = term if result is None else result + term
        lse[pl.ds(start, rows), :] = jnp.broadcast_to(top + jnp.log(total), (rows, HEAD_DIM))
        for j in range(rows // CLEN):
            block = start // CLEN + j
            there = pl.ds(pl.multiple_of(order[block] * CLEN, CLEN), CLEN)
            mixed[there, :] = result[j * CLEN : (j + 1) * CLEN].astype(BF16)


def attend(order, qkv, inv_q, inv_k, gain_q, gain_k, cos, sin):
    heads = qkv.shape[1] // (3 * HEAD_DIM)
    head = lambda off: pl.BlockSpec((GTOK, HEAD_DIM), lambda h, o: (0, h + off))
    whole = lambda w: pl.BlockSpec((GTOK, w), lambda h, o: (0, 0))
    gain = pl.BlockSpec((1, HEAD_DIM), lambda h, o: (0, h))
    wide = jax.ShapeDtypeStruct((GTOK, heads * HEAD_DIM), BF16)
    return pl.pallas_call(
        attend_kernel,
        grid_spec=pltpu.PrefetchScalarGridSpec(
            num_scalar_prefetch=1,
            grid=(heads,),
            in_specs=[head(0), head(heads), head(2 * heads), whole(1), whole(1), gain, gain]
            + [whole(HEAD_DIM)] * 2,
            out_specs=[head(0)] * 5,
        ),
        out_shape=[wide] * 4 + [jax.ShapeDtypeStruct((GTOK, heads * HEAD_DIM), F32)],
        compiler_params=pltpu.CompilerParams(vmem_limit_bytes=48 * 2**20),
    )(order, qkv, qkv, qkv, inv_q, inv_k, gain_q, gain_k, cos, sin)


def attend_back_kernel(
    order, q_rot, k_rot, v_in, lse, grad_mixed, cos, sin, dq_out, dk_out, dv_out, grads, dq, dk, dv
):
    for i in range(BLOCKS):
        there = pl.ds(pl.multiple_of(order[i] * CLEN, CLEN), CLEN)
        grads[pl.ds(i * CLEN, CLEN), :] = grad_mixed[there, :]
    dk[...] = jnp.zeros_like(dk)
    dv[...] = jnp.zeros_like(dv)
    for start, rows, keys in tiles():
        here = pl.ds(start, rows)
        q, g, level = q_rot[here, :], grads[here, :], lse[here, 0:1]
        probs, grad_probs, delta = [], [], 0.0
        for k_start, k_rows, masked in keys:
            s = by_transpose(q, k_rot[pl.ds(k_start, k_rows), :]) * SCALE
            s = jnp.where(causal(rows), s, NEG) if masked else s
            p = jnp.exp(s - level)
            gp = by_transpose(g, v_in[pl.ds(k_start, k_rows), :])
            delta = delta + jnp.sum(p * gp, axis=1, keepdims=True)
            probs.append(p)
            grad_probs.append(gp)
        total = None
        for p, gp, (k_start, k_rows, _) in zip(probs, grad_probs, keys):
            there = pl.ds(k_start, k_rows)
            raw = (p * (gp - delta) * SCALE).astype(BF16)
            term = plain(raw, k_rot[there, :])
            total = term if total is None else total + term
            dk[there, :] += cross_rows(raw, q)
            dv[there, :] += cross_rows(p.astype(BF16), g)
        dq[here, :] = total
    for i in range(BLOCKS):
        here = pl.ds(i * CLEN, CLEN)
        there = pl.ds(pl.multiple_of(order[i] * CLEN, CLEN), CLEN)
        cos_rows, sin_rows = cos[there, :], sin[there, :]
        dq_out[there, :] = rope(dq[here, :], cos_rows, -sin_rows)
        dk_out[there, :] = rope(dk[here, :], cos_rows, -sin_rows)
        dv_out[there, :] = dv[here, :].astype(BF16)


def attend_back(order, q_rot, k_rot, v_in, lse, grad_mixed, cos, sin):
    heads = q_rot.shape[1] // HEAD_DIM
    head = pl.BlockSpec((GTOK, HEAD_DIM), lambda h, o: (0, h))
    whole = pl.BlockSpec((GTOK, HEAD_DIM), lambda h, o: (0, 0))
    wide = lambda t: jax.ShapeDtypeStruct((GTOK, heads * HEAD_DIM), t)
    return pl.pallas_call(
        attend_back_kernel,
        grid_spec=pltpu.PrefetchScalarGridSpec(
            num_scalar_prefetch=1,
            grid=(heads,),
            in_specs=[head] * 5 + [whole] * 2,
            out_specs=[head] * 3,
            scratch_shapes=[
                pltpu.VMEM((GTOK, HEAD_DIM), BF16),
                pltpu.VMEM((GTOK, HEAD_DIM), F32),
                pltpu.VMEM((GTOK, HEAD_DIM), F32),
                pltpu.VMEM((GTOK, HEAD_DIM), F32),
            ],
        ),
        out_shape=[wide(F32), wide(F32), wide(BF16)],
        compiler_params=pltpu.CompilerParams(vmem_limit_bytes=48 * 2**20),
    )(order, q_rot, k_rot, v_in, lse, grad_mixed, cos, sin)


ANY = pl.BlockSpec(memory_space=pl.ANY)
VM = pl.BlockSpec(memory_space=pltpu.VMEM)
DMA = pltpu.SemaphoreType.DMA


def params(cid, mib=60):
    return pltpu.CompilerParams(collective_id=cid, has_side_effects=True, vmem_limit_bytes=mib * 2**20)


def peer(i):
    return {"expert": i}


def remote(src, dst, send_sem, recv_sem, to):
    return pltpu.make_async_remote_copy(
        src_ref=src,
        dst_ref=dst,
        send_sem=send_sem,
        recv_sem=recv_sem,
        device_id=to if isinstance(to, dict) else peer(to),
        device_id_type=MESH,
    )


def greet_line(n, others=()):
    p = lax.axis_index("expert")
    bar = pltpu.get_barrier_semaphore()

    @pl.when(p > 0)
    def _():
        pl.semaphore_signal(bar, inc=1, device_id=peer(p - 1), device_id_type=MESH)

    @pl.when(p < n - 1)
    def _():
        pl.semaphore_signal(bar, inc=1, device_id=peer(p + 1), device_id_type=MESH)

    for other in others:
        pl.semaphore_signal(bar, inc=1, device_id=other, device_id_type=MESH)
    pl.semaphore_wait(bar, (p > 0).astype(jnp.int32) + (p < n - 1).astype(jnp.int32) + len(others))
    return p


def greet_all(n):
    p = lax.axis_index("expert")
    bar = pltpu.get_barrier_semaphore()
    for s in range(1, n):
        pl.semaphore_signal(bar, inc=1, device_id=peer(lax.rem(p + s, n)), device_id_type=MESH)
    pl.semaphore_wait(bar, n - 1)
    return p


class Gather:
    sems = lambda n, pieces=1: [DMA((n * pieces,))] * 3

    def __init__(self, p, n, own, at, sems, pieces=1):
        self.p, self.n, self.own, self.at, self.pieces = p, n, own, at, pieces
        self.to_right, self.to_left, self.recv = sems

    def right(self, src, j, c):
        i = j * self.pieces + c
        return remote(src, self.at(j, c), self.to_right.at[i], self.recv.at[i], self.p + 1)

    def left(self, src, j, c):
        i = j * self.pieces + c
        return remote(src, self.at(j, c), self.to_left.at[i], self.recv.at[i], self.p - 1)

    def start(self, c=0):
        @pl.when(self.p < self.n - 1)
        def _():
            self.right(self.own(c), self.p, c).start()

        @pl.when(self.p > 0)
        def _():
            self.left(self.own(c), self.p, c).start()

    def step(self, s, use=None, c=0):
        p, n = self.p, self.n
        j, k = p - s, p + s

        @pl.when(j >= 0)
        def _():
            self.right(self.at(j, c), j, c).wait_recv()

            @pl.when(p < n - 1)
            def _():
                self.right(self.at(j, c), j, c).start()

        @pl.when(k < n)
        def _():
            self.left(self.at(k, c), k, c).wait_recv()

            @pl.when(p > 0)
            def _():
                self.left(self.at(k, c), k, c).start()

        if use is not None:
            for i, here in ((j, j >= 0), (k, k < n)):
                pl.when(here)(functools.partial(use, i))

    def finish(self):
        for j in range(self.n):
            for c in range(self.pieces):

                @pl.when((j <= self.p) & (self.p < self.n - 1))
                def _():
                    self.right(self.own(c), j, c).wait_send()

                @pl.when((j >= self.p) & (self.p > 0))
                def _():
                    self.left(self.own(c), j, c).wait_send()


class Reduce:
    pieces, depth = 4, 2
    sems = lambda n: [DMA((n * Reduce.pieces,))] * 4
    boxes = lambda n, rows, width: [pltpu.VMEM((n * Reduce.pieces, rows // Reduce.pieces, width), BF16)] * 2

    def __init__(self, p, n, rows, part, make, boxes, sems):
        self.p, self.n, self.rows, self.part, self.make = p, n, rows, part, make
        self.from_left, self.from_right = boxes
        self.to_right, self.to_left, self.recv_r, self.recv_l = sems

    def at(self, j, c):
        size = self.rows // self.pieces
        return self.part.at[pl.ds(pl.multiple_of(j * self.rows + c * size, size), size)]

    def right(self, j, c):
        i = j * self.pieces + c
        return remote(self.at(j, c), self.from_left.at[i], self.to_right.at[i], self.recv_r.at[i], self.p + 1)

    def left(self, j, c):
        i = j * self.pieces + c
        return remote(self.at(j, c), self.from_right.at[i], self.to_left.at[i], self.recv_l.at[i], self.p - 1)

    def add(self, j, c, box):
        total = self.at(j, c)[...].astype(F32) + box[j * self.pieces + c].astype(F32)
        self.at(j, c)[...] = total.astype(BF16)

    def pass_on(self, m, count, ends, shard, copy, box):
        @pl.when((m >= 0) & (m < count))
        def _():
            j, c = shard(lax.div(m, self.pieces)), lax.rem(m, self.pieces)
            pl.when(c == 0)(lambda: self.make(j))

            @pl.when(ends)
            def _():
                copy(j, c).wait_recv()
                self.add(j, c, box)

            @pl.when(m >= self.depth)
            def _():
                before = m - self.depth
                copy(shard(lax.div(before, self.pieces)), lax.rem(before, self.pieces)).wait_send()

            copy(j, c).start()

    def tick(self, t):
        p, n = self.p, self.n
        to_right = lambda: self.pass_on(t - p, (n - 1 - p) * self.pieces, p > 0, lambda s: n - 1 - s, self.right, self.from_left)
        to_left = lambda: self.pass_on(t - (n - 1 - p), p * self.pieces, p < n - 1, lambda s: s, self.left, self.from_right)
        to_right()
        to_left()

    def run(self, beside=lambda t: None):
        @pl.loop(0, (self.n - 1) * self.pieces + self.n - 1)
        def _(t):
            beside(t)
            self.tick(t)

    def finish(self, out, base=None):
        p, n, size = self.p, self.n, self.rows // self.pieces
        self.make(p)
        for c in range(self.pieces):

            @pl.when(p > 0)
            def _():
                self.right(p, c).wait_recv()
                self.add(p, c, self.from_left)

            @pl.when(p < n - 1)
            def _():
                self.left(p, c).wait_recv()
                self.add(p, c, self.from_right)

            here = pl.ds(c * size, size)
            if base is None:
                out[here] = self.at(p, c)[...]
            else:
                out[here] = (base[here].astype(F32) + self.at(p, c)[...].astype(F32)).astype(out.dtype)
        for i in range(self.depth):
            for count, shard, copy in (
                ((n - 1 - p) * self.pieces, lambda s: n - 1 - s, self.right),
                (p * self.pieces, lambda s: s, self.left),
            ):
                m = count - 1 - i

                @pl.when(m >= 0)
                def _():
                    copy(shard(lax.div(m, self.pieces)), lax.rem(m, self.pieces)).wait_send()


def rows_of(ref, rows):
    return lambda j: ref.at[pl.ds(pl.multiple_of(j * rows, rows), rows)]


def ag_kernel(n, rows, x, *rest):
    count = (len(rest) - 7) // 2
    blocks, out, fulls = rest[:count], rest[count], rest[count + 1 : 2 * count + 1]
    to_right, to_left, recv, local, sent, came = rest[2 * count + 1 :]
    d = lax.axis_index("dp")
    core, by_x, by_y = lax.rem(d, 2), lax.rem(d // 2, 2), d // 4
    d_x, d_y, d_c = d + 2 - 4 * by_x, d + 4 - 8 * by_y, d + 1 - 2 * core
    d_far = d_x + 4 - 8 * by_y
    x_way, y_way, c_way = {"dp": d_x}, {"dp": d_y}, {"dp": d_c}
    p = greet_line(n, (x_way, y_way, c_way) if count else ())
    at = rows_of(out, rows)
    own = pltpu.make_async_copy(x, at(p), local.at[0])
    own.start()
    line = Gather(p, n, lambda c: x, lambda j, c: at(j), (to_right, to_left, recv))
    line.start()

    def send(a, src, first, size, kind, way):
        dst = fulls[a].at[pl.ds(pl.multiple_of(first, size), size)]
        return remote(dst if src is None else src, dst, sent.at[a, kind], came.at[a, kind], way)

    def moves(a):
        size = blocks[a].shape[0]
        half = size // 2
        return [
            lambda: send(a, blocks[a], d * size, size, 0, x_way),
            lambda: send(a, blocks[a], d * size, size, 1, y_way),
            lambda: send(a, blocks[a], d * size, size, 2, c_way),
            lambda: send(a, None, d_x * size, half, 3, y_way),
            lambda: send(a, None, d_y * size + half, half, 4, x_way),
            lambda: send(a, None, d_x * size, size, 5, c_way),
            lambda: send(a, None, d_y * size, size, 6, c_way),
            lambda: send(a, None, d_far * size, size, 7, c_way),
        ]

    all_moves = [moves(a) for a in range(count)]
    locals_ = [
        pltpu.make_async_copy(
            blocks[a],
            fulls[a].at[pl.ds(pl.multiple_of(d * blocks[a].shape[0], blocks[a].shape[0]), blocks[a].shape[0])],
            local.at[a + 1],
        )
        for a in range(count)
    ]
    for a in range(count):
        locals_[a].start()
        for k in range(3):
            all_moves[a][k]().start()
    line.step(1)
    for a in range(count):
        for k in (0, 1):
            all_moves[a][k]().wait_recv()
        for k in (3, 4, 5, 6):
            all_moves[a][k]().start()
    for s in range(2, n):
        line.step(s)
        if s == 2:
            for a in range(count):
                for k in (3, 4):
                    all_moves[a][k]().wait_recv()
                all_moves[a][7]().start()
    for a in range(count):
        locals_[a].wait()
        for k in (2, 5, 6, 7):
            all_moves[a][k]().wait_recv()
        for k in range(8):
            all_moves[a][k]().wait_send()
    own.wait()
    line.finish()


def ag_z(x, n, cid, blocks=()):
    rows = x.shape[0]
    count = len(blocks)
    grown = lambda b, k: jax.ShapeDtypeStruct((k * b.shape[0],) + b.shape[1:], b.dtype)
    return pl.pallas_call(
        functools.partial(ag_kernel, n, rows),
        out_shape=[grown(x, n)] + [grown(b, 8) for b in blocks],
        in_specs=[ANY] * (1 + count),
        out_specs=[ANY] * (1 + count),
        scratch_shapes=Gather.sems(n) + [DMA((1 + count,)), DMA((max(count, 1), 8)), DMA((max(count, 1), 8))],
        compiler_params=params(cid),
    )(x, *blocks)


def gather_kernel(n, rows, x, slot, small, grads, logits, rows_out, grads_out, *rest):
    shards, picked, picked_grads, to_right, to_left, recv, out_sems = rest
    p = greet_line(n)
    experts = slot.shape[1]
    line = Gather(p, n, lambda c: x, lambda j, c: shards.at[j], (to_right, to_left, recv))
    line.start()

    def pick(j, e):
        places = lax.broadcasted_iota(jnp.int32, (CAP, rows), 0)
        return (slot[j, e : e + 1] == places).astype(F32).astype(BF16)

    def use(j, block, first=False):
        logits[pl.ds(pl.multiple_of(j * rows, rows), rows), :] = plain(block[...], small[...])
        for e in range(experts):
            new = plain(pick(j, e), block[...])
            picked[e] = new.astype(BF16) if first else (picked[e].astype(F32) + new).astype(BF16)

    def copy_out(e, src, dst, k):
        return pltpu.make_async_copy(src.at[e], dst.at[e], out_sems.at[k, e])

    use(p, x, True)
    for e in range(experts):
        for j in range(n):
            new = plain(pick(j, e), grads[j * rows : (j + 1) * rows])
            picked_grads[e] = new.astype(BF16) if j == 0 else (picked_grads[e].astype(F32) + new).astype(BF16)
        copy_out(e, picked_grads, grads_out, 1).start()
    for s in range(1, n):
        line.step(s, lambda j: use(j, shards.at[j]))
    for e in range(experts):
        copy_out(e, picked, rows_out, 0).start()
    for e in range(experts):
        copy_out(e, picked, rows_out, 0).wait()
        copy_out(e, picked_grads, grads_out, 1).wait()
    line.finish()


def gather_rows(x, slot, small, grads, n, cid):
    rows, width = x.shape
    experts = slot.shape[1]
    wide = (experts, CAP, width)
    return pl.pallas_call(
        functools.partial(gather_kernel, n, rows),
        out_shape=[
            jax.ShapeDtypeStruct((n * rows, small.shape[1]), F32),
            jax.ShapeDtypeStruct(wide, BF16),
            jax.ShapeDtypeStruct(wide, BF16),
        ],
        in_specs=[VM] * 4,
        out_specs=[VM, ANY, ANY],
        scratch_shapes=[pltpu.VMEM((n, rows, width), BF16), pltpu.VMEM(wide, BF16), pltpu.VMEM(wide, BF16)]
        + Gather.sems(n)
        + [DMA((2, experts))],
        compiler_params=params(cid),
    )(x, slot, small, grads)


def rs_kernel(n, rows, part, out, left_box, right_box, *sems):
    p = greet_line(n)
    line = Reduce(p, n, rows, part, lambda j: None, (left_box, right_box), sems)
    line.run()
    line.finish(out)


def rs_z(part, n, cid):
    rows, width = part.shape[0] // n, part.shape[1]
    return pl.pallas_call(
        functools.partial(rs_kernel, n, rows),
        out_shape=jax.ShapeDtypeStruct((rows, width), BF16),
        in_specs=[VM],
        out_specs=VM,
        scratch_shapes=Reduce.boxes(n, rows, width) + Reduce.sems(n),
        compiler_params=params(cid),
    )(part)


def combine(part, rows, slot, weight, blocks):
    def make(j):
        total, e = None, 0
        for block in blocks:
            for i in range(block.shape[0]):
                places = lax.broadcasted_iota(jnp.int32, (rows, CAP), 1)
                chosen = slot[j, :, e : e + 1] == places
                scale = 1.0 if weight is None else weight[j, :, e : e + 1]
                term = plain(jnp.where(chosen, scale, 0.0).astype(BF16), block[i])
                total = term if total is None else total + term
                e += 1
        part[pl.ds(pl.multiple_of(j * rows, rows), rows), :] = total.astype(BF16)

    return make


def combine_kernel(n, rows, slot, low, high, out, part, left_box, right_box, *sems):
    p = greet_line(n)
    make = combine(part, rows, slot, None, (low, high))
    line = Reduce(p, n, rows, part, make, (left_box, right_box), sems)
    line.run()
    line.finish(out)


def combine_z(slot, low, high, n, cid):
    rows, width = slot.shape[1], low.shape[2]
    return pl.pallas_call(
        functools.partial(combine_kernel, n, rows),
        out_shape=jax.ShapeDtypeStruct((rows, width), BF16),
        in_specs=[VM] * 3,
        out_specs=VM,
        scratch_shapes=[pltpu.VMEM((n * rows, width), BF16)] + Reduce.boxes(n, rows, width) + Reduce.sems(n),
        compiler_params=params(cid),
    )(slot, low, high)


def both_kernel(n, rows, x, slot, weight, low, high, base, all_out, out, part, left_box, right_box, *sems):
    p = greet_line(n)
    at = rows_of(all_out, rows)
    own = pltpu.make_async_copy(x, at(p), sems[7])
    own.start()
    size = rows // Reduce.pieces
    piece = lambda j, c: all_out.at[pl.ds(pl.multiple_of(j * rows + c * size, size), size)]
    gather = Gather(p, n, lambda c: x.at[pl.ds(pl.multiple_of(c * size, size), size)], piece, sems[:3], Reduce.pieces)
    make = combine(part, rows, slot, weight, (low, high))
    line = Reduce(p, n, rows, part, make, (left_box, right_box), sems[3:7])
    gather.start(0)
    gather.start(1)

    def beside(t):
        pl.when(t + 2 < Reduce.pieces)(lambda: gather.start(t + 2))

        @pl.when((t >= 1) & (t - 1 < (n - 1) * Reduce.pieces))
        def _():
            gather.step(lax.div(t - 1, Reduce.pieces) + 1, c=lax.rem(t - 1, Reduce.pieces))

    line.run(beside)
    line.finish(out, base)
    own.wait()
    gather.finish()


def gather_and_combine(x, slot, weight, low, high, base, n, cid):
    rows, width = x.shape
    return pl.pallas_call(
        functools.partial(both_kernel, n, rows),
        out_shape=[jax.ShapeDtypeStruct((n * rows, width), x.dtype), jax.ShapeDtypeStruct((rows, width), BF16)],
        in_specs=[ANY] + [VM] * 5,
        out_specs=[ANY, VM],
        scratch_shapes=[pltpu.VMEM((n * rows, width), BF16)]
        + Reduce.boxes(n, rows, width)
        + Gather.sems(n, Reduce.pieces)
        + Reduce.sems(n)
        + [DMA],
        compiler_params=params(cid),
    )(x, slot, weight, low, high, base)


def a2a_kernel(n,rows,cols,x,out,send,recv,local):
    p=greet_all(n)
    src=lambda j: x.at[pl.ds(pl.multiple_of(j*rows,rows),rows)]
    dst=lambda c: out.at[:,pl.ds(pl.multiple_of(c*cols,cols),cols)]
    own=pltpu.make_async_copy(src(p),dst(p),local); own.start()
    def send_to(s):
        j=lax.rem(p+s,n)
        return pltpu.make_async_remote_copy(src_ref=src(j),dst_ref=dst(p),send_sem=send.at[s],recv_sem=recv.at[s],device_id=peer(j),device_id_type=MESH)
    for s in range(1,n): send_to(s).start()
    for s in range(1,n):
        c=lax.rem(p-s+n,n)
        pltpu.make_async_remote_copy(src_ref=src(p),dst_ref=dst(c),send_sem=send.at[s],recv_sem=recv.at[s],device_id=peer(c),device_id_type=MESH).wait_recv()
    for s in range(1,n): send_to(s).wait_send()
    own.wait()

def a2a_z(x,n,cid):
    rows=x.shape[0]//n; cols=x.shape[1]
    return pl.pallas_call(functools.partial(a2a_kernel,n,rows,cols),out_shape=jax.ShapeDtypeStruct((rows,n*cols),x.dtype),
        in_specs=[ANY],out_specs=ANY,scratch_shapes=[DMA((n,))]*2+[DMA],
        compiler_params=params(cid))(x)

def exchange_kernel(n, rows, x, out, send, recv, local):
    p = greet_all(n)
    at = lambda ref, j: ref.at[pl.ds(pl.multiple_of(j * rows, rows), rows)]
    own = pltpu.make_async_copy(at(x, p), at(out, p), local)
    own.start()

    def to(s):
        j = lax.rem(p + s, n)
        return pltpu.make_async_remote_copy(
            src_ref=at(x, j), dst_ref=at(out, p), send_sem=send.at[s], recv_sem=recv.at[s], device_id=peer(j),
            device_id_type=MESH,
        )

    for s in range(1, n):
        to(s).start()
    for s in range(1, n):
        to(s).wait_recv()
    for s in range(1, n):
        to(s).wait_send()
    own.wait()


def exchange_z(x, n, cid):
    return pl.pallas_call(
        functools.partial(exchange_kernel, n, x.shape[0] // n),
        out_shape=jax.ShapeDtypeStruct(x.shape, x.dtype),
        in_specs=[ANY],
        out_specs=ANY,
        scratch_shapes=[DMA((n,))] * 2 + [DMA],
        compiler_params=params(cid),
    )(x)


def sum_kernel(n,x,out,got,send,recv):
    p=greet_all(n)
    def send_to(s):
        return pltpu.make_async_remote_copy(src_ref=x,dst_ref=got.at[s],send_sem=send.at[s],recv_sem=recv.at[s],device_id=peer(lax.rem(p+s,n)),device_id_type=MESH)
    for s in range(1,n): send_to(s).start()
    tot=x[...]
    for s in range(1,n):
        send_to(s).wait_recv(); tot=tot+got[s]
    out[...]=tot
    for s in range(1,n): send_to(s).wait_send()

def sum_z(x,n,cid):
    return pl.pallas_call(functools.partial(sum_kernel,n),out_shape=jax.ShapeDtypeStruct(x.shape,x.dtype),in_specs=[VM],out_specs=VM,
        scratch_shapes=[pltpu.VMEM((n,)+x.shape,x.dtype)]+[DMA((n,))]*2,compiler_params=params(cid))(x)


def expert_kernel(
    slot, weight, x, g, gate, up, down, eo_out, gin_out, route_out, gu_out, gd_out, xt, w_col, both, scaled, eo, gin
):
    f = pl.program_id(1)
    tile = gate.shape[2]
    chunks = CAP // ROWS
    tokens = slot.shape[2]
    x, g = x.at[0], g.at[0]

    def one_hot(start):
        place = lax.broadcasted_iota(jnp.int32, (ROWS, tokens), 0) + start
        return slot[0] == place

    @pl.when(f == 0)
    def _():
        @pl.loop(0, chunks)
        def _(c):
            here = pl.ds(pl.multiple_of(c * ROWS, ROWS), ROWS)
            chosen = one_hot(c * ROWS)
            w_col[here, :] = jnp.sum(jnp.where(chosen, weight[0], 0.0), axis=1, keepdims=True)
            eo[here, :] = jnp.zeros((ROWS, x.shape[1]), F32)
            gin[here, :] = jnp.zeros((ROWS, x.shape[1]), F32)

        xt[...] = x[...].T

    @pl.loop(0, chunks)
    def _(c):
        here = pl.ds(pl.multiple_of(c * ROWS, ROWS), ROWS)
        a = plain(x[here, :], gate[0])
        b = plain(x[here, :], up[0])
        h = by_transpose(g[here, :], down[0]) * w_col[here, :]
        sig = 1.0 / (1.0 + jnp.exp(-a))
        silu = a * sig
        hidden = silu * b
        gg = (h * b * (sig * (1.0 + a * (1.0 - sig)))).astype(BF16)
        gu = (h * silu).astype(BF16)
        both[here, 0:tile] = gg
        both[here, tile : 2 * tile] = gu
        scaled[here, :] = (hidden * w_col[here, :]).astype(BF16)
        eo[here, :] += plain(hidden.astype(BF16), down[0])
        gin[here, :] += by_transpose(gg, gate[0]) + by_transpose(gu, up[0])

    pieces, rows = gu_out.shape[0], gu_out.shape[3]

    grad_both = plain(xt[...], both[...]).astype(BF16)
    for c in range(pieces):
        gu_out[c, 0, 0] = grad_both[c * rows : (c + 1) * rows, :tile]
        gu_out[c, 1, 0] = grad_both[c * rows : (c + 1) * rows, tile:]

    down_rows = gd_out.shape[2]
    grad_down = cross_rows(scaled[...], g[...]).astype(BF16)
    for c in range(gd_out.shape[0]):
        gd_out[c, 0] = grad_down[c * down_rows : (c + 1) * down_rows]

    @pl.when(f == pl.num_programs(1) - 1)
    def _():
        eo_out[0] = eo[...].astype(BF16)
        gin_out[0] = gin[...].astype(BF16)
        route = jnp.zeros((1, tokens), F32)
        for c in range(chunks):
            here = pl.ds(c * ROWS, ROWS)
            dots = jnp.sum(eo[here, :].astype(BF16).astype(F32) * g[here, :].astype(F32), axis=1, keepdims=True)
            route = route + jnp.sum(jnp.where(one_hot(c * ROWS), dots, 0.0), axis=0, keepdims=True)
        route_out[0] = route


def experts(first, count, dp, slot, weight, x, g, gate, up, down):
    tokens, width = slot.shape[2], x.shape[2]
    ff = gate.shape[2]
    steps = ff // FTILE
    line = pl.BlockSpec((1, 1, tokens), lambda e, f: (first + e, 0, 0))
    column = pl.BlockSpec((1, width, FTILE), lambda e, f: (first + e, 0, f))
    row = pl.BlockSpec((1, FTILE, width), lambda e, f: (first + e, f, 0))
    slots_in = pl.BlockSpec((1, CAP, width), lambda e, f: (first + e, 0, 0), pipeline_mode=pl.Buffered(2))
    slots_out = pl.BlockSpec((1, CAP, width), lambda e, f: (e, 0, 0), pipeline_mode=pl.Buffered(1))
    down_rows = ff // dp
    return pl.pallas_call(
        expert_kernel,
        grid=(count, steps),
        in_specs=[line, line, slots_in, slots_in, column, column, row],
        out_specs=[
            slots_out,
            slots_out,
            pl.BlockSpec((1, 1, tokens), lambda e, f: (e, 0, 0)),
            pl.BlockSpec((dp, 2, 1, width // dp, FTILE), lambda e, f: (0, 0, e, 0, f)),
            pl.BlockSpec((FTILE // down_rows, 1, down_rows, width), lambda e, f: (f, e, 0, 0)),
        ],
        out_shape=[
            jax.ShapeDtypeStruct((count, CAP, width), BF16),
            jax.ShapeDtypeStruct((count, CAP, width), BF16),
            jax.ShapeDtypeStruct((count, 1, tokens), F32),
            jax.ShapeDtypeStruct((dp, 2, count, width // dp, ff), BF16),
            jax.ShapeDtypeStruct((dp, count, down_rows, width), BF16),
        ],
        scratch_shapes=[
            pltpu.VMEM((width, CAP), BF16),
            pltpu.VMEM((CAP, 1), F32),
            pltpu.VMEM((CAP, 2 * FTILE), BF16),
            pltpu.VMEM((CAP, FTILE), BF16),
            pltpu.VMEM((CAP, width), F32),
            pltpu.VMEM((CAP, width), F32),
        ],
        compiler_params=pltpu.CompilerParams(vmem_limit_bytes=60 * 2**20),
    )(slot, weight, x, g, gate, up, down)


def row_moves(ways, dp):
    return [(d * ways + z, z * dp + d) for d in range(dp) for z in range(ways)]


def hops(up, down, count, ways):
    for _ in range(count):
        h = len(up)
        up = up + [lax.ppermute(up[-1], "expert", [(i, i + 1) for i in range(h - 1, ways - 1)])]
        down = down + [lax.ppermute(down[-1], "expert", [(i + 1, i) for i in range(ways - h)])]
    return up, down


def later(sent, other):
    up, down = sent
    last_up, last_down, other = lax.optimization_barrier((up[-1], down[-1], other))
    return up[:-1] + [last_up], down[:-1] + [last_down], other


def line_up(up, down, ways):
    line = jnp.concatenate(up[:0:-1] + down, axis=0)
    rows = down[0].shape[0]
    start = (ways - 1 - lax.axis_index("expert")) * rows
    return lax.dynamic_slice_in_dim(line, start, ways * rows, axis=0)


def norm_qkv_kernel(columns, x, gain, weight, out, normed, inverse, squares):
    values = x[...].astype(F32)
    inv = lax.rsqrt(jnp.mean(values * values, axis=1, keepdims=True) + EPS)
    rows = (values * inv * gain[...]).astype(BF16)
    inverse[...] = inv
    normed[...] = rows
    result = plain(rows, weight[:, :columns])
    out[...] = result
    third = columns // 3
    lanes = lax.broadcasted_iota(jnp.int32, (x.shape[0], 128), 1)
    sums = jnp.zeros((x.shape[0], 128), F32)
    for i in range(2):
        part = result[:, i * third : (i + 1) * third]
        sums = jnp.where(lanes == i, jnp.sum(part * part, axis=1, keepdims=True), sums)
    squares[...] = sums.T[:8]


def norm_qkv(x, gain, weight, columns):
    tokens, width = x.shape
    tile = lambda w: pl.BlockSpec((NTILE, w), lambda i: (i, 0))
    return pl.pallas_call(
        functools.partial(norm_qkv_kernel, columns),
        grid=(tokens // NTILE,),
        in_specs=[
            tile(width),
            pl.BlockSpec((1, width), lambda i: (0, 0)),
            pl.BlockSpec(weight.shape, lambda i: (0, 0), pipeline_mode=pl.Buffered(1)),
        ],
        out_specs=[tile(columns), tile(width), tile(1), pl.BlockSpec((8, NTILE), lambda i: (0, i))],
        out_shape=[
            jax.ShapeDtypeStruct((tokens, columns), F32),
            jax.ShapeDtypeStruct((tokens, width), BF16),
            jax.ShapeDtypeStruct((tokens, 1), F32),
            jax.ShapeDtypeStruct((8, tokens), F32),
        ],
        compiler_params=pltpu.CompilerParams(vmem_limit_bytes=48 * 2**20),
    )(x, gain, weight)


def block_order(segs, places):
    seg = segs.reshape(BLOCKS, CLEN)[:, 0]
    place = places.reshape(BLOCKS, CLEN)[:, 0]
    stand = jnp.where(seg == 0, place // CLEN, PROMPT // CLEN - 1 + seg)
    blocks = jnp.arange(BLOCKS, dtype=jnp.int32)
    return jnp.sum(jnp.where(stand[None, :] == blocks[:, None], blocks[None, :], 0), axis=1)


def slots(routes, priority):
    experts = jnp.arange(EXPERTS, dtype=jnp.int32)
    hits = jnp.any(routes[:, :, None] == experts[None, None, :], axis=1)
    index = jnp.arange(GTOK, dtype=jnp.int32)
    rank = jnp.sum(jnp.where(priority[:, None] == index[None, :], index[:, None], 0), axis=0)
    earlier = (rank[None, :] < rank[:, None]).astype(BF16)
    return hits, plain(earlier, hits.astype(BF16)).astype(jnp.int32)


def body(
    tokens,
    cotangent,
    attention_gain,
    query_weight,
    key_weight,
    value_weight,
    out_weight,
    query_norm,
    key_norm,
    mixture_gain,
    router_weight,
    gate_weight,
    up_weight,
    down_weight,
    segments,
    positions,
    priority,
    routes,
):
    tok_dev, width = tokens.shape
    experts_here = gate_weight.shape[0]
    ways = lax.axis_size("expert")
    z = lax.axis_index("expert")
    cols = width // ways
    first_row = z * tok_dev

    small = jnp.concatenate(
        [attention_gain[:, None], query_norm[:, None], key_norm[:, None], mixture_gain[:, None], router_weight],
        axis=1,
    )
    small = jnp.pad(small, ((0, 0), (0, SMALL - small.shape[1])))
    shard = jnp.stack([query_weight, key_weight, value_weight], axis=1)
    shard = shard.reshape(-1, 3, ways, cols).transpose(2, 0, 1, 3).reshape(ways, -1, 3 * cols)
    rest = jnp.concatenate([small, out_weight], axis=1)
    shard = jnp.concatenate([shard, jnp.broadcast_to(rest[None], (ways,) + rest.shape)], axis=2)
    shard = exchange_z(shard.reshape(-1, shard.shape[-1]), ways, 1)
    shards = shard[:, : 3 * cols + SMALL], shard[:, 3 * cols + SMALL :]
    if lax.axis_size("dp") == 8:
        tokens_all, dense, out_full = ag_z(tokens, ways, 2, shards)
    else:
        (tokens_all,) = ag_z(tokens, ways, 2)
        dense, out_full = (lax.all_gather(s, "dp", axis=0, tiled=True) for s in shards)
    qkv_weight = dense[:, : 3 * cols]
    small = dense[:, 3 * cols :]
    attend_gain = small[:, 0].astype(F32)
    mix_gain = small[:, 3].astype(F32)
    router_full = small[:, 4 : 4 + EXPERTS]
    my_gains = lax.dynamic_slice_in_dim(small[:, 1:3], z * cols, cols, axis=0).astype(F32)
    gain_q, gain_k = my_gains[:, 0][None], my_gains[:, 1][None]
    out_mine = lax.dynamic_slice_in_dim(out_full, z * cols, cols, axis=0)
    tokens_all, gate_weight, up_weight, down_weight = lax.optimization_barrier(
        (tokens_all, gate_weight, up_weight, down_weight)
    )
    gate_full = lax.all_gather(gate_weight, "dp", axis=1, tiled=True)
    up_full = lax.all_gather(up_weight, "dp", axis=1, tiled=True)
    down_full = lax.all_gather(down_weight, "dp", axis=1, tiled=True)
    steps = [ways // 2, (3 * ways) // 4]
    early, tokens_all = lax.optimization_barrier((cotangent, tokens_all))
    sent = hops([early], [early], steps[0] - 1, ways)

    segs, places = segments[0], positions[0]
    order = block_order(segs, places)
    frequency = 10000.0 ** (-jnp.arange(0, HEAD_DIM // 2, dtype=F32) * 2.0 / HEAD_DIM)
    angles = places.astype(F32)[:, None] * frequency[None, :]
    cos, sin = jnp.cos(angles), jnp.sin(angles)
    cos = jnp.concatenate([cos, cos], axis=1)
    sin = jnp.concatenate([-sin, sin], axis=1)
    hits, slot = slots(routes[0], priority[0])
    my_hits = lax.dynamic_slice_in_dim(hits, z * experts_here, experts_here, axis=1)
    my_slot = lax.dynamic_slice_in_dim(slot, z * experts_here, experts_here, axis=1)
    my_slot = jnp.where(my_hits & (my_slot < CAP), my_slot, -1)
    slot_lines = my_slot.T[:, None, :]
    slot_shards = my_slot.T.reshape(experts_here, ways, tok_dev).transpose(1, 0, 2)
    slot_cols = my_slot.reshape(ways, tok_dev, experts_here)

    qkv, normed, inverse_in, squares = norm_qkv(tokens_all, attend_gain[None], dense, 3 * cols)
    squares = sum_z(squares, ways, 3)
    up, down, squares = later(sent, squares)
    sent = hops(up, down, steps[1] - steps[0], ways)
    inv_q = lax.rsqrt(squares[0] / width + EPS)[:, None]
    inv_k = lax.rsqrt(squares[1] / width + EPS)[:, None]
    q_rot, k_rot, v_b, mixed_heads, lse = attend(order, qkv, inv_q, inv_k, gain_q, gain_k, cos, sin)
    mixed = a2a_z(mixed_heads, ways, 4)
    up, down, mixed = later(sent, mixed)
    grad_all = line_up(*hops(up, down, ways - steps[1], ways), ways)
    own_f = tokens.astype(F32)
    resid = own_f + plain(mixed, out_full)
    mix_inverse = lax.rsqrt(jnp.mean(resid * resid, axis=-1, keepdims=True) + EPS)
    mix_unit = resid * mix_inverse
    mix = (mix_unit * mix_gain).astype(BF16)
    logits, inputs, grad_rows = gather_rows(mix, slot_shards, small, grad_all, ways, 5)

    router_all = jax.nn.softmax(logits[:, 4 : 4 + EXPERTS], axis=-1)
    my_weight = lax.dynamic_slice_in_dim(router_all, z * experts_here, experts_here, axis=1)
    weight_lines = my_weight.T[:, None, :]
    weight_cols = my_weight.reshape(ways, tok_dev, experts_here)
    half = experts_here // 2
    work = (half, lax.axis_size("dp"), slot_lines, weight_lines, inputs, grad_rows, gate_full, up_full, down_full)
    out_low, in_low, route_low, both_low, down_low = experts(0, *work)
    sum_both_low = lax.psum_scatter(both_low, "dp", scatter_dimension=0, tiled=True)
    sum_down_low = lax.psum_scatter(down_low, "dp", scatter_dimension=0, tiled=True)
    out_high, in_high, route_high, both_high, down_high = experts(half, *work)
    sum_both_high = lax.psum_scatter(both_high, "dp", scatter_dimension=0, tiled=True)
    sum_down_high = lax.psum_scatter(down_high, "dp", scatter_dimension=0, tiled=True)
    my_route_grad = jnp.concatenate([route_low, route_high], axis=0)[:, 0]
    route_grad = lax.all_to_all(my_route_grad, "expert", split_axis=1, concat_axis=0, tiled=True).T
    grad_routed = combine_z(slot_cols, in_low, in_high, ways, 6).astype(F32)

    router = lax.dynamic_slice_in_dim(router_all, first_row, tok_dev, axis=0)
    grad_logits = (router * (route_grad - jnp.sum(router * route_grad, axis=-1, keepdims=True))).astype(BF16)
    grad_router_w = cross_rows(mix, grad_logits)
    grad_mix = grad_routed + by_transpose(grad_logits, router_full)
    grad_mix_gain = jnp.sum(grad_mix * mix_unit, axis=0)
    grad_resid = cotangent.astype(F32) + norm_back(grad_mix, mix_unit, mix_inverse, mix_gain)
    grad_branch = grad_resid.astype(BF16)
    grad_branch, sum_both_low, sum_down_low = lax.optimization_barrier((grad_branch, sum_both_low, sum_down_low))
    branch_all, output = gather_and_combine(grad_branch, slot_cols, weight_cols, out_low, out_high, resid, ways, 7)
    grad_heads = by_transpose(branch_all, out_mine).astype(BF16)
    grad_out_w = cross_rows(mixed_heads, branch_all).astype(BF16)
    out_out = lax.psum_scatter(grad_out_w, "dp", scatter_dimension=0, tiled=True)
    out_out = lax.ppermute(out_out, BOTH, row_moves(ways, lax.axis_size("dp"))).astype(F32)

    grad_heads, sum_both_high = lax.optimization_barrier((grad_heads, sum_both_high))
    dq, dk, dv = attend_back(order, q_rot, k_rot, v_b, lse, grad_heads, cos, sin)
    q_unit = qkv[:, :cols] * inv_q
    k_unit = qkv[:, cols : 2 * cols] * inv_k
    inner = jnp.stack(
        [jnp.sum(dq * gain_q * q_unit, axis=-1), jnp.sum(dk * gain_k * k_unit, axis=-1)], axis=0
    )
    inner = sum_z(jnp.pad(inner, ((0, 6), (0, 0))), ways, 8) / width
    grad_q_gain = jnp.sum(dq * q_unit, axis=0)
    grad_k_gain = jnp.sum(dk * k_unit, axis=0)
    grad_q = (inv_q * (dq * gain_q - q_unit * inner[0][:, None])).astype(BF16)
    grad_k = (inv_k * (dk * gain_k - k_unit * inner[1][:, None])).astype(BF16)
    grad_qkv = jnp.concatenate([grad_q, grad_k, dv], axis=1)
    grad_normed_part = by_transpose(grad_qkv, qkv_weight)
    grad_attend_gain = jnp.sum(grad_normed_part * (tokens_all.astype(F32) * inverse_in), axis=0)
    part, sum_down_high = lax.optimization_barrier((grad_normed_part.astype(BF16), sum_down_high))
    grad_normed = rs_z(part, ways, 9).astype(F32)
    own_inverse = lax.dynamic_slice_in_dim(inverse_in, first_row, tok_dev, axis=0)
    input_grad = grad_resid + norm_back(grad_normed, own_f * own_inverse, own_inverse, attend_gain)

    place = lambda part: lax.dynamic_update_slice(jnp.zeros((width,), F32), part, (z * cols,))
    extra = jnp.concatenate(
        [
            jnp.stack([grad_attend_gain, place(grad_q_gain), place(grad_k_gain), grad_mix_gain], axis=1),
            grad_router_w,
            jnp.zeros((width, SMALL - 4 - EXPERTS), F32),
        ],
        axis=1,
    )
    grad_qkv_w = jnp.concatenate([cross_rows(normed, grad_qkv), extra], axis=1).astype(BF16)
    grad_qkv_w = lax.psum_scatter(grad_qkv_w, "dp", scatter_dimension=0, tiled=True)
    grad_qkv_w = exchange_z(grad_qkv_w, ways, 10).reshape(ways, -1, 3 * cols + SMALL)
    grad_w = [
        grad_qkv_w[:, :, i * cols : (i + 1) * cols].transpose(1, 0, 2).reshape(-1, width).astype(F32)
        for i in range(3)
    ]
    planes = [jnp.concatenate([sum_both_low[0, i], sum_both_high[0, i]], axis=0) for i in range(2)]
    out_gate, out_up = planes[0].astype(F32), planes[1].astype(F32)
    out_down = jnp.concatenate([sum_down_low[0], sum_down_high[0]], axis=0).astype(F32)
    packed = jnp.sum(grad_qkv_w[:, :, 3 * cols :].astype(F32), axis=0)
    return (
        output,
        input_grad,
        packed[:, 0],
        grad_w[0],
        grad_w[1],
        grad_w[2],
        out_out,
        packed[:, 1],
        packed[:, 2],
        packed[:, 3],
        packed[:, 4 : 4 + EXPERTS],
        out_gate,
        out_up,
        out_down,
    )


def solution(mesh):
    rows = P(BOTH, None)
    vec = P(BOTH)
    expert = P("expert", "dp", None)
    group = P("dp", None)
    return jax.shard_map(
        body,
        mesh=mesh,
        in_specs=(rows, rows, vec, rows, rows, rows, rows, vec, vec, vec, rows, expert, expert, expert)
        + (group, group, group, P("dp", None, None)),
        out_specs=(rows, rows, vec, rows, rows, rows, rows, vec, vec, vec, rows, expert, expert, expert),
        check_vma=False,
    )
```

```python
import functools

import jax
import jax.numpy as jnp
from jax import lax
from jax.experimental import pallas as pl
from jax.experimental.pallas import tpu as pltpu
from jax.sharding import PartitionSpec as P

HEADS = 16
HEAD_DIM = 128
TOPK = 8
EXPERTS = 16
GTOK = 1536
CAP = 768
PROMPT = 1024
CLEN = 128
BLOCKS = GTOK // CLEN
TILE = 256
ROWS = 768
FTILE = 256
NTILE = 384
WTILE = 512
EPS = 1e-05
BOTH = ("dp", "expert")
F32 = jnp.float32
BF16 = jnp.bfloat16
SCALE = HEAD_DIM ** (-0.5)
NEG = -1e30
SMALL = 128
MESH = pl.DeviceIdType.MESH


def norm_back(grad_rows, unit_rows, inverse, gain_vec):
    grad_unit = grad_rows * gain_vec
    inner_mean = jnp.mean(grad_unit * unit_rows, axis=-1, keepdims=True)
    return inverse * (grad_unit - unit_rows * inner_mean)


def cross_rows(left, right):
    return lax.dot_general(left, right, (((0,), (0,)), ((), ())), preferred_element_type=F32)


def by_transpose(left, right):
    return lax.dot_general(left, right, (((1,), (1,)), ((), ())), preferred_element_type=F32)


def plain(left, right):
    return lax.dot_general(left, right, (((1,), (0,)), ((), ())), preferred_element_type=F32)


def causal(rows):
    return lax.broadcasted_iota(jnp.int32, (rows, rows), 1) <= lax.broadcasted_iota(
        jnp.int32, (rows, rows), 0
    )


def tiles():
    out = []
    for i in range(PROMPT // TILE):
        keys = [(0, i * TILE, False)] if i else []
        out.append((i * TILE, TILE, keys + [(i * TILE, TILE, True)]))
    for c in range(PROMPT // CLEN, BLOCKS):
        out.append((c * CLEN, CLEN, [(0, PROMPT, False), (c * CLEN, CLEN, True)]))
    return out


def rope(values, cos_rows, sin_rows):
    return values * cos_rows + pltpu.roll(values, HEAD_DIM // 2, 1) * sin_rows


def attend_kernel(
    order, q_pre, k_pre, v_pre, inv_q, inv_k, gain_q, gain_k, cos, sin, q_rot, k_rot, v_out, mixed, lse
):
    for i in range(BLOCKS):
        here = pl.ds(i * CLEN, CLEN)
        there = pl.ds(pl.multiple_of(order[i] * CLEN, CLEN), CLEN)
        cos_rows, sin_rows = cos[there, :], sin[there, :]
        q_n = q_pre[there, :] * inv_q[there, :] * gain_q[...]
        k_n = k_pre[there, :] * inv_k[there, :] * gain_k[...]
        q_rot[here, :] = rope(q_n, cos_rows, sin_rows).astype(BF16)
        k_rot[here, :] = rope(k_n, cos_rows, sin_rows).astype(BF16)
        v_out[here, :] = v_pre[there, :].astype(BF16)
    for start, rows, keys in tiles():
        q = q_rot[pl.ds(start, rows), :]
        parts = []
        for k_start, k_rows, masked in keys:
            s = by_transpose(q, k_rot[pl.ds(k_start, k_rows), :]) * SCALE
            parts.append(jnp.where(causal(rows), s, NEG) if masked else s)
        top = functools.reduce(jnp.maximum, [jnp.max(s, axis=1, keepdims=True) for s in parts])
        exps = [jnp.exp(s - top) for s in parts]
        total = functools.reduce(lambda a, b: a + b, [jnp.sum(e, axis=1, keepdims=True) for e in exps])
        over = 1.0 / total
        result = None
        for e, (k_start, k_rows, _) in zip(exps, keys):
            term = plain((e * over).astype(BF16), v_out[pl.ds(k_start, k_rows), :])
            result = term if result is None else result + term
        lse[pl.ds(start, rows), :] = jnp.broadcast_to(top + jnp.log(total), (rows, HEAD_DIM))
        for j in range(rows // CLEN):
            block = start // CLEN + j
            there = pl.ds(pl.multiple_of(order[block] * CLEN, CLEN), CLEN)
            mixed[there, :] = result[j * CLEN : (j + 1) * CLEN].astype(BF16)


def attend(order, qkv, inv_q, inv_k, gain_q, gain_k, cos, sin):
    heads = qkv.shape[1] // (3 * HEAD_DIM)
    head = lambda off: pl.BlockSpec((GTOK, HEAD_DIM), lambda h, o: (0, h + off))
    whole = lambda w: pl.BlockSpec((GTOK, w), lambda h, o: (0, 0))
    gain = pl.BlockSpec((1, HEAD_DIM), lambda h, o: (0, h))
    wide = jax.ShapeDtypeStruct((GTOK, heads * HEAD_DIM), BF16)
    return pl.pallas_call(
        attend_kernel,
        grid_spec=pltpu.PrefetchScalarGridSpec(
            num_scalar_prefetch=1,
            grid=(heads,),
            in_specs=[head(0), head(heads), head(2 * heads), whole(1), whole(1), gain, gain]
            + [whole(HEAD_DIM)] * 2,
            out_specs=[head(0)] * 5,
        ),
        out_shape=[wide] * 4 + [jax.ShapeDtypeStruct((GTOK, heads * HEAD_DIM), F32)],
        compiler_params=pltpu.CompilerParams(vmem_limit_bytes=48 * 2**20),
    )(order, qkv, qkv, qkv, inv_q, inv_k, gain_q, gain_k, cos, sin)


def attend_back_kernel(
    order, q_rot, k_rot, v_in, lse, grad_mixed, cos, sin, dq_out, dk_out, dv_out, grads, dq, dk, dv
):
    for i in range(BLOCKS):
        there = pl.ds(pl.multiple_of(order[i] * CLEN, CLEN), CLEN)
        grads[pl.ds(i * CLEN, CLEN), :] = grad_mixed[there, :]
    dk[...] = jnp.zeros_like(dk)
    dv[...] = jnp.zeros_like(dv)
    for start, rows, keys in tiles():
        here = pl.ds(start, rows)
        q, g, level = q_rot[here, :], grads[here, :], lse[here, 0:1]
        probs, grad_probs, delta = [], [], 0.0
        for k_start, k_rows, masked in keys:
            s = by_transpose(q, k_rot[pl.ds(k_start, k_rows), :]) * SCALE
            s = jnp.where(causal(rows), s, NEG) if masked else s
            p = jnp.exp(s - level)
            gp = by_transpose(g, v_in[pl.ds(k_start, k_rows), :])
            delta = delta + jnp.sum(p * gp, axis=1, keepdims=True)
            probs.append(p)
            grad_probs.append(gp)
        total = None
        for p, gp, (k_start, k_rows, _) in zip(probs, grad_probs, keys):
            there = pl.ds(k_start, k_rows)
            raw = (p * (gp - delta) * SCALE).astype(BF16)
            term = plain(raw, k_rot[there, :])
            total = term if total is None else total + term
            dk[there, :] += cross_rows(raw, q)
            dv[there, :] += cross_rows(p.astype(BF16), g)
        dq[here, :] = total
    for i in range(BLOCKS):
        here = pl.ds(i * CLEN, CLEN)
        there = pl.ds(pl.multiple_of(order[i] * CLEN, CLEN), CLEN)
        cos_rows, sin_rows = cos[there, :], sin[there, :]
        dq_out[there, :] = rope(dq[here, :], cos_rows, -sin_rows)
        dk_out[there, :] = rope(dk[here, :], cos_rows, -sin_rows)
        dv_out[there, :] = dv[here, :].astype(BF16)


def attend_back(order, q_rot, k_rot, v_in, lse, grad_mixed, cos, sin):
    heads = q_rot.shape[1] // HEAD_DIM
    head = pl.BlockSpec((GTOK, HEAD_DIM), lambda h, o: (0, h))
    whole = pl.BlockSpec((GTOK, HEAD_DIM), lambda h, o: (0, 0))
    wide = lambda t: jax.ShapeDtypeStruct((GTOK, heads * HEAD_DIM), t)
    return pl.pallas_call(
        attend_back_kernel,
        grid_spec=pltpu.PrefetchScalarGridSpec(
            num_scalar_prefetch=1,
            grid=(heads,),
            in_specs=[head] * 5 + [whole] * 2,
            out_specs=[head] * 3,
            scratch_shapes=[
                pltpu.VMEM((GTOK, HEAD_DIM), BF16),
                pltpu.VMEM((GTOK, HEAD_DIM), F32),
                pltpu.VMEM((GTOK, HEAD_DIM), F32),
                pltpu.VMEM((GTOK, HEAD_DIM), F32),
            ],
        ),
        out_shape=[wide(F32), wide(F32), wide(BF16)],
        compiler_params=pltpu.CompilerParams(vmem_limit_bytes=48 * 2**20),
    )(order, q_rot, k_rot, v_in, lse, grad_mixed, cos, sin)


ANY = pl.BlockSpec(memory_space=pl.ANY)
VM = pl.BlockSpec(memory_space=pltpu.VMEM)
DMA = pltpu.SemaphoreType.DMA


def params(cid, mib=60):
    return pltpu.CompilerParams(collective_id=cid, has_side_effects=True, vmem_limit_bytes=mib * 2**20)


def peer(i):
    return {"expert": i}


def remote(src, dst, send_sem, recv_sem, to):
    return pltpu.make_async_remote_copy(
        src_ref=src,
        dst_ref=dst,
        send_sem=send_sem,
        recv_sem=recv_sem,
        device_id=to if isinstance(to, dict) else peer(to),
        device_id_type=MESH,
    )


def greet_line(n, others=()):
    p = lax.axis_index("expert")
    bar = pltpu.get_barrier_semaphore()

    @pl.when(p > 0)
    def _():
        pl.semaphore_signal(bar, inc=1, device_id=peer(p - 1), device_id_type=MESH)

    @pl.when(p < n - 1)
    def _():
        pl.semaphore_signal(bar, inc=1, device_id=peer(p + 1), device_id_type=MESH)

    for other in others:
        pl.semaphore_signal(bar, inc=1, device_id=other, device_id_type=MESH)
    pl.semaphore_wait(bar, (p > 0).astype(jnp.int32) + (p < n - 1).astype(jnp.int32) + len(others))
    return p


def greet_all(n):
    p = lax.axis_index("expert")
    bar = pltpu.get_barrier_semaphore()
    for s in range(1, n):
        pl.semaphore_signal(bar, inc=1, device_id=peer(lax.rem(p + s, n)), device_id_type=MESH)
    pl.semaphore_wait(bar, n - 1)
    return p


class Gather:
    sems = lambda n, pieces=1: [DMA((n * pieces,))] * 3

    def __init__(self, p, n, own, at, sems, pieces=1):
        self.p, self.n, self.own, self.at, self.pieces = p, n, own, at, pieces
        self.to_right, self.to_left, self.recv = sems

    def right(self, src, j, c):
        i = j * self.pieces + c
        return remote(src, self.at(j, c), self.to_right.at[i], self.recv.at[i], self.p + 1)

    def left(self, src, j, c):
        i = j * self.pieces + c
        return remote(src, self.at(j, c), self.to_left.at[i], self.recv.at[i], self.p - 1)

    def start(self, c=0):
        @pl.when(self.p < self.n - 1)
        def _():
            self.right(self.own(c), self.p, c).start()

        @pl.when(self.p > 0)
        def _():
            self.left(self.own(c), self.p, c).start()

    def step(self, s, use=None, c=0):
        p, n = self.p, self.n
        j, k = p - s, p + s

        @pl.when(j >= 0)
        def _():
            self.right(self.at(j, c), j, c).wait_recv()

            @pl.when(p < n - 1)
            def _():
                self.right(self.at(j, c), j, c).start()

        @pl.when(k < n)
        def _():
            self.left(self.at(k, c), k, c).wait_recv()

            @pl.when(p > 0)
            def _():
                self.left(self.at(k, c), k, c).start()

        if use is not None:
            for i, here in ((j, j >= 0), (k, k < n)):
                pl.when(here)(functools.partial(use, i))

    def finish(self):
        for j in range(self.n):
            for c in range(self.pieces):

                @pl.when((j <= self.p) & (self.p < self.n - 1))
                def _():
                    self.right(self.own(c), j, c).wait_send()

                @pl.when((j >= self.p) & (self.p > 0))
                def _():
                    self.left(self.own(c), j, c).wait_send()


class Reduce:
    pieces, depth = 4, 2
    sems = lambda n: [DMA((n * Reduce.pieces,))] * 4
    boxes = lambda n, rows, width: [pltpu.VMEM((n * Reduce.pieces, rows // Reduce.pieces, width), BF16)] * 2

    def __init__(self, p, n, rows, part, make, boxes, sems):
        self.p, self.n, self.rows, self.part, self.make = p, n, rows, part, make
        self.from_left, self.from_right = boxes
        self.to_right, self.to_left, self.recv_r, self.recv_l = sems

    def at(self, j, c):
        size = self.rows // self.pieces
        return self.part.at[pl.ds(pl.multiple_of(j * self.rows + c * size, size), size)]

    def right(self, j, c):
        i = j * self.pieces + c
        return remote(self.at(j, c), self.from_left.at[i], self.to_right.at[i], self.recv_r.at[i], self.p + 1)

    def left(self, j, c):
        i = j * self.pieces + c
        return remote(self.at(j, c), self.from_right.at[i], self.to_left.at[i], self.recv_l.at[i], self.p - 1)

    def add(self, j, c, box):
        total = self.at(j, c)[...].astype(F32) + box[j * self.pieces + c].astype(F32)
        self.at(j, c)[...] = total.astype(BF16)

    def pass_on(self, m, count, ends, shard, copy, box):
        @pl.when((m >= 0) & (m < count))
        def _():
            j, c = shard(lax.div(m, self.pieces)), lax.rem(m, self.pieces)
            pl.when(c == 0)(lambda: self.make(j))

            @pl.when(ends)
            def _():
                copy(j, c).wait_recv()
                self.add(j, c, box)

            @pl.when(m >= self.depth)
            def _():
                before = m - self.depth
                copy(shard(lax.div(before, self.pieces)), lax.rem(before, self.pieces)).wait_send()

            copy(j, c).start()

    def tick(self, t):
        p, n = self.p, self.n
        to_right = lambda: self.pass_on(t - p, (n - 1 - p) * self.pieces, p > 0, lambda s: n - 1 - s, self.right, self.from_left)
        to_left = lambda: self.pass_on(t - (n - 1 - p), p * self.pieces, p < n - 1, lambda s: s, self.left, self.from_right)
        to_right()
        to_left()

    def run(self, beside=lambda t: None):
        @pl.loop(0, (self.n - 1) * self.pieces + self.n - 1)
        def _(t):
            beside(t)
            self.tick(t)

    def finish(self, out, base=None):
        p, n, size = self.p, self.n, self.rows // self.pieces
        self.make(p)
        for c in range(self.pieces):

            @pl.when(p > 0)
            def _():
                self.right(p, c).wait_recv()
                self.add(p, c, self.from_left)

            @pl.when(p < n - 1)
            def _():
                self.left(p, c).wait_recv()
                self.add(p, c, self.from_right)

            here = pl.ds(c * size, size)
            if base is None:
                out[here] = self.at(p, c)[...]
            else:
                out[here] = (base[here].astype(F32) + self.at(p, c)[...].astype(F32)).astype(out.dtype)
        for i in range(self.depth):
            for count, shard, copy in (
                ((n - 1 - p) * self.pieces, lambda s: n - 1 - s, self.right),
                (p * self.pieces, lambda s: s, self.left),
            ):
                m = count - 1 - i

                @pl.when(m >= 0)
                def _():
                    copy(shard(lax.div(m, self.pieces)), lax.rem(m, self.pieces)).wait_send()


def rows_of(ref, rows):
    return lambda j: ref.at[pl.ds(pl.multiple_of(j * rows, rows), rows)]


def ag_kernel(n, rows, x, *rest):
    count = (len(rest) - 7) // 2
    blocks, out, fulls = rest[:count], rest[count], rest[count + 1 : 2 * count + 1]
    to_right, to_left, recv, local, sent, came = rest[2 * count + 1 :]
    d = lax.axis_index("dp")
    core, by_x, by_y = lax.rem(d, 2), lax.rem(d // 2, 2), d // 4
    d_x, d_y, d_c = d + 2 - 4 * by_x, d + 4 - 8 * by_y, d + 1 - 2 * core
    d_far = d_x + 4 - 8 * by_y
    x_way, y_way, c_way = {"dp": d_x}, {"dp": d_y}, {"dp": d_c}
    p = greet_line(n, (x_way, y_way, c_way) if count else ())
    at = rows_of(out, rows)
    own = pltpu.make_async_copy(x, at(p), local.at[0])
    own.start()
    line = Gather(p, n, lambda c: x, lambda j, c: at(j), (to_right, to_left, recv))
    line.start()

    def send(a, src, first, size, kind, way):
        dst = fulls[a].at[pl.ds(pl.multiple_of(first, size), size)]
        return remote(dst if src is None else src, dst, sent.at[a, kind], came.at[a, kind], way)

    def moves(a):
        size = blocks[a].shape[0]
        half = size // 2
        return [
            lambda: send(a, blocks[a], d * size, size, 0, x_way),
            lambda: send(a, blocks[a], d * size, size, 1, y_way),
            lambda: send(a, blocks[a], d * size, size, 2, c_way),
            lambda: send(a, None, d_x * size, half, 3, y_way),
            lambda: send(a, None, d_y * size + half, half, 4, x_way),
            lambda: send(a, None, d_x * size, size, 5, c_way),
            lambda: send(a, None, d_y * size, size, 6, c_way),
            lambda: send(a, None, d_far * size, size, 7, c_way),
        ]

    all_moves = [moves(a) for a in range(count)]
    locals_ = [
        pltpu.make_async_copy(
            blocks[a],
            fulls[a].at[pl.ds(pl.multiple_of(d * blocks[a].shape[0], blocks[a].shape[0]), blocks[a].shape[0])],
            local.at[a + 1],
        )
        for a in range(count)
    ]
    for a in range(count):
        locals_[a].start()
        for k in range(3):
            all_moves[a][k]().start()
    line.step(1)
    for a in range(count):
        for k in (0, 1):
            all_moves[a][k]().wait_recv()
        for k in (3, 4, 5, 6):
            all_moves[a][k]().start()
    for s in range(2, n):
        line.step(s)
        if s == 2:
            for a in range(count):
                for k in (3, 4):
                    all_moves[a][k]().wait_recv()
                all_moves[a][7]().start()
    for a in range(count):
        locals_[a].wait()
        for k in (2, 5, 6, 7):
            all_moves[a][k]().wait_recv()
        for k in range(8):
            all_moves[a][k]().wait_send()
    own.wait()
    line.finish()


def ag_z(x, n, cid, blocks=()):
    rows = x.shape[0]
    count = len(blocks)
    grown = lambda b, k: jax.ShapeDtypeStruct((k * b.shape[0],) + b.shape[1:], b.dtype)
    return pl.pallas_call(
        functools.partial(ag_kernel, n, rows),
        out_shape=[grown(x, n)] + [grown(b, 8) for b in blocks],
        in_specs=[ANY] * (1 + count),
        out_specs=[ANY] * (1 + count),
        scratch_shapes=Gather.sems(n) + [DMA((1 + count,)), DMA((max(count, 1), 8)), DMA((max(count, 1), 8))],
        compiler_params=params(cid),
    )(x, *blocks)


def gather_kernel(n, rows, x, slot, small, grads, logits, rows_out, grads_out, *rest):
    shards, picked, picked_grads, to_right, to_left, recv, out_sems = rest
    p = greet_line(n)
    experts = slot.shape[1]
    line = Gather(p, n, lambda c: x, lambda j, c: shards.at[j], (to_right, to_left, recv))
    line.start()

    def pick(j, e):
        places = lax.broadcasted_iota(jnp.int32, (CAP, rows), 0)
        return (slot[j, e : e + 1] == places).astype(F32).astype(BF16)

    def use(j, block, first=False):
        logits[pl.ds(pl.multiple_of(j * rows, rows), rows), :] = plain(block[...], small[...])
        for e in range(experts):
            new = plain(pick(j, e), block[...])
            picked[e] = new.astype(BF16) if first else (picked[e].astype(F32) + new).astype(BF16)

    def copy_out(e, src, dst, k):
        return pltpu.make_async_copy(src.at[e], dst.at[e], out_sems.at[k, e])

    use(p, x, True)
    for e in range(experts):
        for j in range(n):
            new = plain(pick(j, e), grads[j * rows : (j + 1) * rows])
            picked_grads[e] = new.astype(BF16) if j == 0 else (picked_grads[e].astype(F32) + new).astype(BF16)
        copy_out(e, picked_grads, grads_out, 1).start()
    for s in range(1, n):
        line.step(s, lambda j: use(j, shards.at[j]))
    for e in range(experts):
        copy_out(e, picked, rows_out, 0).start()
    for e in range(experts):
        copy_out(e, picked, rows_out, 0).wait()
        copy_out(e, picked_grads, grads_out, 1).wait()
    line.finish()


def gather_rows(x, slot, small, grads, n, cid):
    rows, width = x.shape
    experts = slot.shape[1]
    wide = (experts, CAP, width)
    return pl.pallas_call(
        functools.partial(gather_kernel, n, rows),
        out_shape=[
            jax.ShapeDtypeStruct((n * rows, small.shape[1]), F32),
            jax.ShapeDtypeStruct(wide, BF16),
            jax.ShapeDtypeStruct(wide, BF16),
        ],
        in_specs=[VM] * 4,
        out_specs=[VM, ANY, ANY],
        scratch_shapes=[pltpu.VMEM((n, rows, width), BF16), pltpu.VMEM(wide, BF16), pltpu.VMEM(wide, BF16)]
        + Gather.sems(n)
        + [DMA((2, experts))],
        compiler_params=params(cid),
    )(x, slot, small, grads)


def rs_kernel(n, rows, part, out, left_box, right_box, *sems):
    p = greet_line(n)
    line = Reduce(p, n, rows, part, lambda j: None, (left_box, right_box), sems)
    line.run()
    line.finish(out)


def rs_z(part, n, cid):
    rows, width = part.shape[0] // n, part.shape[1]
    return pl.pallas_call(
        functools.partial(rs_kernel, n, rows),
        out_shape=jax.ShapeDtypeStruct((rows, width), BF16),
        in_specs=[VM],
        out_specs=VM,
        scratch_shapes=Reduce.boxes(n, rows, width) + Reduce.sems(n),
        compiler_params=params(cid),
    )(part)


def combine(part, rows, slot, weight, blocks):
    def make(j):
        total, e = None, 0
        for block in blocks:
            for i in range(block.shape[0]):
                places = lax.broadcasted_iota(jnp.int32, (rows, CAP), 1)
                chosen = slot[j, :, e : e + 1] == places
                scale = 1.0 if weight is None else weight[j, :, e : e + 1]
                term = plain(jnp.where(chosen, scale, 0.0).astype(BF16), block[i])
                total = term if total is None else total + term
                e += 1
        part[pl.ds(pl.multiple_of(j * rows, rows), rows), :] = total.astype(BF16)

    return make


def combine_kernel(n, rows, slot, low, high, out, part, left_box, right_box, *sems):
    p = greet_line(n)
    make = combine(part, rows, slot, None, (low, high))
    line = Reduce(p, n, rows, part, make, (left_box, right_box), sems)
    line.run()
    line.finish(out)


def combine_z(slot, low, high, n, cid):
    rows, width = slot.shape[1], low.shape[2]
    return pl.pallas_call(
        functools.partial(combine_kernel, n, rows),
        out_shape=jax.ShapeDtypeStruct((rows, width), BF16),
        in_specs=[VM] * 3,
        out_specs=VM,
        scratch_shapes=[pltpu.VMEM((n * rows, width), BF16)] + Reduce.boxes(n, rows, width) + Reduce.sems(n),
        compiler_params=params(cid),
    )(slot, low, high)


def both_kernel(n, rows, x, slot, weight, low, high, base, all_out, out, part, left_box, right_box, *sems):
    p = greet_line(n)
    at = rows_of(all_out, rows)
    own = pltpu.make_async_copy(x, at(p), sems[7])
    own.start()
    size = rows // Reduce.pieces
    piece = lambda j, c: all_out.at[pl.ds(pl.multiple_of(j * rows + c * size, size), size)]
    gather = Gather(p, n, lambda c: x.at[pl.ds(pl.multiple_of(c * size, size), size)], piece, sems[:3], Reduce.pieces)
    make = combine(part, rows, slot, weight, (low, high))
    line = Reduce(p, n, rows, part, make, (left_box, right_box), sems[3:7])
    gather.start(0)
    gather.start(1)

    def beside(t):
        pl.when(t + 2 < Reduce.pieces)(lambda: gather.start(t + 2))

        @pl.when((t >= 1) & (t - 1 < (n - 1) * Reduce.pieces))
        def _():
            gather.step(lax.div(t - 1, Reduce.pieces) + 1, c=lax.rem(t - 1, Reduce.pieces))

    line.run(beside)
    line.finish(out, base)
    own.wait()
    gather.finish()


def gather_and_combine(x, slot, weight, low, high, base, n, cid):
    rows, width = x.shape
    return pl.pallas_call(
        functools.partial(both_kernel, n, rows),
        out_shape=[jax.ShapeDtypeStruct((n * rows, width), x.dtype), jax.ShapeDtypeStruct((rows, width), BF16)],
        in_specs=[ANY] + [VM] * 5,
        out_specs=[ANY, VM],
        scratch_shapes=[pltpu.VMEM((n * rows, width), BF16)]
        + Reduce.boxes(n, rows, width)
        + Gather.sems(n, Reduce.pieces)
        + Reduce.sems(n)
        + [DMA],
        compiler_params=params(cid),
    )(x, slot, weight, low, high, base)


def a2a_kernel(n,rows,cols,x,out,send,recv,local):
    p=greet_all(n)
    src=lambda j: x.at[pl.ds(pl.multiple_of(j*rows,rows),rows)]
    dst=lambda c: out.at[:,pl.ds(pl.multiple_of(c*cols,cols),cols)]
    own=pltpu.make_async_copy(src(p),dst(p),local); own.start()
    def send_to(s):
        j=lax.rem(p+s,n)
        return pltpu.make_async_remote_copy(src_ref=src(j),dst_ref=dst(p),send_sem=send.at[s],recv_sem=recv.at[s],device_id=peer(j),device_id_type=MESH)
    for s in range(1,n): send_to(s).start()
    for s in range(1,n):
        c=lax.rem(p-s+n,n)
        pltpu.make_async_remote_copy(src_ref=src(p),dst_ref=dst(c),send_sem=send.at[s],recv_sem=recv.at[s],device_id=peer(c),device_id_type=MESH).wait_recv()
    for s in range(1,n): send_to(s).wait_send()
    own.wait()

def a2a_z(x,n,cid):
    rows=x.shape[0]//n; cols=x.shape[1]
    return pl.pallas_call(functools.partial(a2a_kernel,n,rows,cols),out_shape=jax.ShapeDtypeStruct((rows,n*cols),x.dtype),
        in_specs=[ANY],out_specs=ANY,scratch_shapes=[DMA((n,))]*2+[DMA],
        compiler_params=params(cid))(x)

def exchange_kernel(n, rows, x, out, send, recv, local):
    p = greet_all(n)
    at = lambda ref, j: ref.at[pl.ds(pl.multiple_of(j * rows, rows), rows)]
    own = pltpu.make_async_copy(at(x, p), at(out, p), local)
    own.start()

    def to(s):
        j = lax.rem(p + s, n)
        return pltpu.make_async_remote_copy(
            src_ref=at(x, j), dst_ref=at(out, p), send_sem=send.at[s], recv_sem=recv.at[s], device_id=peer(j),
            device_id_type=MESH,
        )

    for s in range(1, n):
        to(s).start()
    for s in range(1, n):
        to(s).wait_recv()
    for s in range(1, n):
        to(s).wait_send()
    own.wait()


def exchange_z(x, n, cid):
    return pl.pallas_call(
        functools.partial(exchange_kernel, n, x.shape[0] // n),
        out_shape=jax.ShapeDtypeStruct(x.shape, x.dtype),
        in_specs=[ANY],
        out_specs=ANY,
        scratch_shapes=[DMA((n,))] * 2 + [DMA],
        compiler_params=params(cid),
    )(x)


def sum_kernel(n,x,out,got,send,recv):
    p=greet_all(n)
    def send_to(s):
        return pltpu.make_async_remote_copy(src_ref=x,dst_ref=got.at[s],send_sem=send.at[s],recv_sem=recv.at[s],device_id=peer(lax.rem(p+s,n)),device_id_type=MESH)
    for s in range(1,n): send_to(s).start()
    tot=x[...]
    for s in range(1,n):
        send_to(s).wait_recv(); tot=tot+got[s]
    out[...]=tot
    for s in range(1,n): send_to(s).wait_send()

def sum_z(x,n,cid):
    return pl.pallas_call(functools.partial(sum_kernel,n),out_shape=jax.ShapeDtypeStruct(x.shape,x.dtype),in_specs=[VM],out_specs=VM,
        scratch_shapes=[pltpu.VMEM((n,)+x.shape,x.dtype)]+[DMA((n,))]*2,compiler_params=params(cid))(x)


def expert_kernel(
    slot, weight, x, g, gate, up, down, eo_out, gin_out, route_out, gu_out, gd_out, xt, w_col, both, scaled, eo, gin
):
    f = pl.program_id(1)
    tile = gate.shape[2]
    chunks = CAP // ROWS
    tokens = slot.shape[2]
    x, g = x.at[0], g.at[0]

    def one_hot(start):
        place = lax.broadcasted_iota(jnp.int32, (ROWS, tokens), 0) + start
        return slot[0] == place

    @pl.when(f == 0)
    def _():
        @pl.loop(0, chunks)
        def _(c):
            here = pl.ds(pl.multiple_of(c * ROWS, ROWS), ROWS)
            chosen = one_hot(c * ROWS)
            w_col[here, :] = jnp.sum(jnp.where(chosen, weight[0], 0.0), axis=1, keepdims=True)
            eo[here, :] = jnp.zeros((ROWS, x.shape[1]), F32)
            gin[here, :] = jnp.zeros((ROWS, x.shape[1]), F32)

        xt[...] = x[...].T

    @pl.loop(0, chunks)
    def _(c):
        here = pl.ds(pl.multiple_of(c * ROWS, ROWS), ROWS)
        a = plain(x[here, :], gate[0])
        b = plain(x[here, :], up[0])
        h = by_transpose(g[here, :], down[0]) * w_col[here, :]
        sig = 1.0 / (1.0 + jnp.exp(-a))
        silu = a * sig
        hidden = silu * b
        gg = (h * b * (sig * (1.0 + a * (1.0 - sig)))).astype(BF16)
        gu = (h * silu).astype(BF16)
        both[here, 0:tile] = gg
        both[here, tile : 2 * tile] = gu
        scaled[here, :] = (hidden * w_col[here, :]).astype(BF16)
        eo[here, :] += plain(hidden.astype(BF16), down[0])
        gin[here, :] += by_transpose(gg, gate[0]) + by_transpose(gu, up[0])

    pieces, rows = gu_out.shape[0], gu_out.shape[3]

    grad_both = plain(xt[...], both[...]).astype(BF16)
    for c in range(pieces):
        gu_out[c, 0, 0] = grad_both[c * rows : (c + 1) * rows, :tile]
        gu_out[c, 1, 0] = grad_both[c * rows : (c + 1) * rows, tile:]

    down_rows = gd_out.shape[2]
    grad_down = cross_rows(scaled[...], g[...]).astype(BF16)
    for c in range(gd_out.shape[0]):
        gd_out[c, 0] = grad_down[c * down_rows : (c + 1) * down_rows]

    @pl.when(f == pl.num_programs(1) - 1)
    def _():
        eo_out[0] = eo[...].astype(BF16)
        gin_out[0] = gin[...].astype(BF16)
        route = jnp.zeros((1, tokens), F32)
        for c in range(chunks):
            here = pl.ds(c * ROWS, ROWS)
            dots = jnp.sum(eo[here, :].astype(BF16).astype(F32) * g[here, :].astype(F32), axis=1, keepdims=True)
            route = route + jnp.sum(jnp.where(one_hot(c * ROWS), dots, 0.0), axis=0, keepdims=True)
        route_out[0] = route


def experts(first, count, dp, slot, weight, x, g, gate, up, down):
    tokens, width = slot.shape[2], x.shape[2]
    ff = gate.shape[2]
    steps = ff // FTILE
    line = pl.BlockSpec((1, 1, tokens), lambda e, f: (first + e, 0, 0))
    column = pl.BlockSpec((1, width, FTILE), lambda e, f: (first + e, 0, f))
    row = pl.BlockSpec((1, FTILE, width), lambda e, f: (first + e, f, 0))
    slots_in = pl.BlockSpec((1, CAP, width), lambda e, f: (first + e, 0, 0), pipeline_mode=pl.Buffered(2))
    slots_out = pl.BlockSpec((1, CAP, width), lambda e, f: (e, 0, 0), pipeline_mode=pl.Buffered(1))
    down_rows = ff // dp
    return pl.pallas_call(
        expert_kernel,
        grid=(count, steps),
        in_specs=[line, line, slots_in, slots_in, column, column, row],
        out_specs=[
            slots_out,
            slots_out,
            pl.BlockSpec((1, 1, tokens), lambda e, f: (e, 0, 0)),
            pl.BlockSpec((dp, 2, 1, width // dp, FTILE), lambda e, f: (0, 0, e, 0, f)),
            pl.BlockSpec((FTILE // down_rows, 1, down_rows, width), lambda e, f: (f, e, 0, 0)),
        ],
        out_shape=[
            jax.ShapeDtypeStruct((count, CAP, width), BF16),
            jax.ShapeDtypeStruct((count, CAP, width), BF16),
            jax.ShapeDtypeStruct((count, 1, tokens), F32),
            jax.ShapeDtypeStruct((dp, 2, count, width // dp, ff), BF16),
            jax.ShapeDtypeStruct((dp, count, down_rows, width), BF16),
        ],
        scratch_shapes=[
            pltpu.VMEM((width, CAP), BF16),
            pltpu.VMEM((CAP, 1), F32),
            pltpu.VMEM((CAP, 2 * FTILE), BF16),
            pltpu.VMEM((CAP, FTILE), BF16),
            pltpu.VMEM((CAP, width), F32),
            pltpu.VMEM((CAP, width), F32),
        ],
        compiler_params=pltpu.CompilerParams(vmem_limit_bytes=60 * 2**20),
    )(slot, weight, x, g, gate, up, down)


def row_moves(ways, dp):
    return [(d * ways + z, z * dp + d) for d in range(dp) for z in range(ways)]


def hops(up, down, count, ways):
    for _ in range(count):
        h = len(up)
        up = up + [lax.ppermute(up[-1], "expert", [(i, i + 1) for i in range(h - 1, ways - 1)])]
        down = down + [lax.ppermute(down[-1], "expert", [(i + 1, i) for i in range(ways - h)])]
    return up, down


def later(sent, other):
    up, down = sent
    last_up, last_down, other = lax.optimization_barrier((up[-1], down[-1], other))
    return up[:-1] + [last_up], down[:-1] + [last_down], other


def line_up(up, down, ways):
    line = jnp.concatenate(up[:0:-1] + down, axis=0)
    rows = down[0].shape[0]
    start = (ways - 1 - lax.axis_index("expert")) * rows
    return lax.dynamic_slice_in_dim(line, start, ways * rows, axis=0)


def norm_qkv_kernel(columns, x, gain, weight, out, normed, inverse, squares):
    values = x[...].astype(F32)
    inv = lax.rsqrt(jnp.mean(values * values, axis=1, keepdims=True) + EPS)
    rows = (values * inv * gain[...]).astype(BF16)
    inverse[...] = inv
    normed[...] = rows
    result = plain(rows, weight[:, :columns])
    out[...] = result
    third = columns // 3
    lanes = lax.broadcasted_iota(jnp.int32, (x.shape[0], 128), 1)
    sums = jnp.zeros((x.shape[0], 128), F32)
    for i in range(2):
        part = result[:, i * third : (i + 1) * third]
        sums = jnp.where(lanes == i, jnp.sum(part * part, axis=1, keepdims=True), sums)
    squares[...] = sums.T[:8]


def norm_qkv(x, gain, weight, columns):
    tokens, width = x.shape
    tile = lambda w: pl.BlockSpec((NTILE, w), lambda i: (i, 0))
    return pl.pallas_call(
        functools.partial(norm_qkv_kernel, columns),
        grid=(tokens // NTILE,),
        in_specs=[
            tile(width),
            pl.BlockSpec((1, width), lambda i: (0, 0)),
            pl.BlockSpec(weight.shape, lambda i: (0, 0), pipeline_mode=pl.Buffered(1)),
        ],
        out_specs=[tile(columns), tile(width), tile(1), pl.BlockSpec((8, NTILE), lambda i: (0, i))],
        out_shape=[
            jax.ShapeDtypeStruct((tokens, columns), F32),
            jax.ShapeDtypeStruct((tokens, width), BF16),
            jax.ShapeDtypeStruct((tokens, 1), F32),
            jax.ShapeDtypeStruct((8, tokens), F32),
        ],
        compiler_params=pltpu.CompilerParams(vmem_limit_bytes=48 * 2**20),
    )(x, gain, weight)


def weight_grad_kernel(left, right, extra, out):
    columns = right.shape[1]
    out[:, :columns] = cross_rows(left[...], right[...]).astype(BF16)
    out[:, columns:] = extra[...].astype(BF16)


def weight_grad(left, right, extra):
    tokens, width = left.shape
    columns, more = right.shape[1], extra.shape[1]
    return pl.pallas_call(
        weight_grad_kernel,
        grid=(width // WTILE,),
        in_specs=[
            pl.BlockSpec((tokens, WTILE), lambda i: (0, i)),
            pl.BlockSpec((tokens, columns), lambda i: (0, 0)),
            pl.BlockSpec((WTILE, more), lambda i: (i, 0)),
        ],
        out_specs=pl.BlockSpec((WTILE, columns + more), lambda i: (i, 0)),
        out_shape=jax.ShapeDtypeStruct((width, columns + more), BF16),
        compiler_params=pltpu.CompilerParams(vmem_limit_bytes=48 * 2**20),
    )(left, right, extra)


def block_order(segs, places):
    seg = segs.reshape(BLOCKS, CLEN)[:, 0]
    place = places.reshape(BLOCKS, CLEN)[:, 0]
    stand = jnp.where(seg == 0, place // CLEN, PROMPT // CLEN - 1 + seg)
    blocks = jnp.arange(BLOCKS, dtype=jnp.int32)
    return jnp.sum(jnp.where(stand[None, :] == blocks[:, None], blocks[None, :], 0), axis=1)


def slots(routes, priority):
    experts = jnp.arange(EXPERTS, dtype=jnp.int32)
    hits = jnp.any(routes[:, :, None] == experts[None, None, :], axis=1)
    index = jnp.arange(GTOK, dtype=jnp.int32)
    rank = jnp.sum(jnp.where(priority[:, None] == index[None, :], index[:, None], 0), axis=0)
    earlier = (rank[None, :] < rank[:, None]).astype(BF16)
    return hits, plain(earlier, hits.astype(BF16)).astype(jnp.int32)


def body(
    tokens,
    cotangent,
    attention_gain,
    query_weight,
    key_weight,
    value_weight,
    out_weight,
    query_norm,
    key_norm,
    mixture_gain,
    router_weight,
    gate_weight,
    up_weight,
    down_weight,
    segments,
    positions,
    priority,
    routes,
):
    tok_dev, width = tokens.shape
    experts_here = gate_weight.shape[0]
    ways = lax.axis_size("expert")
    z = lax.axis_index("expert")
    cols = width // ways
    first_row = z * tok_dev

    small = jnp.concatenate(
        [attention_gain[:, None], query_norm[:, None], key_norm[:, None], mixture_gain[:, None], router_weight],
        axis=1,
    )
    small = jnp.pad(small, ((0, 0), (0, SMALL - small.shape[1])))
    shard = jnp.stack([query_weight, key_weight, value_weight], axis=1)
    shard = shard.reshape(-1, 3, ways, cols).transpose(2, 0, 1, 3).reshape(ways, -1, 3 * cols)
    rest = jnp.concatenate([small, out_weight], axis=1)
    shard = jnp.concatenate([shard, jnp.broadcast_to(rest[None], (ways,) + rest.shape)], axis=2)
    shard = exchange_z(shard.reshape(-1, shard.shape[-1]), ways, 1)
    shards = shard[:, : 3 * cols + SMALL], shard[:, 3 * cols + SMALL :]
    if lax.axis_size("dp") == 8:
        tokens_all, dense, out_full = ag_z(tokens, ways, 2, shards)
    else:
        (tokens_all,) = ag_z(tokens, ways, 2)
        dense, out_full = (lax.all_gather(s, "dp", axis=0, tiled=True) for s in shards)
    qkv_weight = dense[:, : 3 * cols]
    small = dense[:, 3 * cols :]
    attend_gain = small[:, 0].astype(F32)
    mix_gain = small[:, 3].astype(F32)
    router_full = small[:, 4 : 4 + EXPERTS]
    my_gains = lax.dynamic_slice_in_dim(small[:, 1:3], z * cols, cols, axis=0).astype(F32)
    gain_q, gain_k = my_gains[:, 0][None], my_gains[:, 1][None]
    out_mine = lax.dynamic_slice_in_dim(out_full, z * cols, cols, axis=0)
    tokens_all, gate_weight, up_weight, down_weight = lax.optimization_barrier(
        (tokens_all, gate_weight, up_weight, down_weight)
    )
    gate_full = lax.all_gather(gate_weight, "dp", axis=1, tiled=True)
    up_full = lax.all_gather(up_weight, "dp", axis=1, tiled=True)
    down_full = lax.all_gather(down_weight, "dp", axis=1, tiled=True)
    steps = [ways // 2, (3 * ways) // 4]
    early, tokens_all = lax.optimization_barrier((cotangent, tokens_all))
    sent = hops([early], [early], steps[0] - 1, ways)

    segs, places = segments[0], positions[0]
    order = block_order(segs, places)
    frequency = 10000.0 ** (-jnp.arange(0, HEAD_DIM // 2, dtype=F32) * 2.0 / HEAD_DIM)
    angles = places.astype(F32)[:, None] * frequency[None, :]
    cos, sin = jnp.cos(angles), jnp.sin(angles)
    cos = jnp.concatenate([cos, cos], axis=1)
    sin = jnp.concatenate([-sin, sin], axis=1)
    hits, slot = slots(routes[0], priority[0])
    my_hits = lax.dynamic_slice_in_dim(hits, z * experts_here, experts_here, axis=1)
    my_slot = lax.dynamic_slice_in_dim(slot, z * experts_here, experts_here, axis=1)
    my_slot = jnp.where(my_hits & (my_slot < CAP), my_slot, -1)
    slot_lines = my_slot.T[:, None, :]
    slot_shards = my_slot.T.reshape(experts_here, ways, tok_dev).transpose(1, 0, 2)
    slot_cols = my_slot.reshape(ways, tok_dev, experts_here)

    qkv, normed, inverse_in, squares = norm_qkv(tokens_all, attend_gain[None], dense, 3 * cols)
    up, down, squares = later(sent, squares)
    sent = hops(up, down, steps[1] - steps[0], ways)
    squares = sum_z(squares, ways, 3)
    up, down, squares = later(sent, squares)
    grad_all = line_up(*hops(up, down, ways - steps[1], ways), ways)
    inv_q = lax.rsqrt(squares[0] / width + EPS)[:, None]
    inv_k = lax.rsqrt(squares[1] / width + EPS)[:, None]
    q_rot, k_rot, v_b, mixed_heads, lse = attend(order, qkv, inv_q, inv_k, gain_q, gain_k, cos, sin)
    mixed = a2a_z(mixed_heads, ways, 4)
    own_f = tokens.astype(F32)
    resid = own_f + plain(mixed, out_full)
    mix_inverse = lax.rsqrt(jnp.mean(resid * resid, axis=-1, keepdims=True) + EPS)
    mix_unit = resid * mix_inverse
    mix = (mix_unit * mix_gain).astype(BF16)
    logits, inputs, grad_rows = gather_rows(mix, slot_shards, small, grad_all, ways, 5)

    router_all = jax.nn.softmax(logits[:, 4 : 4 + EXPERTS], axis=-1)
    my_weight = lax.dynamic_slice_in_dim(router_all, z * experts_here, experts_here, axis=1)
    weight_lines = my_weight.T[:, None, :]
    weight_cols = my_weight.reshape(ways, tok_dev, experts_here)
    half = experts_here // 2
    work = (half, lax.axis_size("dp"), slot_lines, weight_lines, inputs, grad_rows, gate_full, up_full, down_full)
    out_low, in_low, route_low, both_low, down_low = experts(0, *work)
    sum_both_low = lax.psum_scatter(both_low, "dp", scatter_dimension=0, tiled=True)
    sum_down_low = lax.psum_scatter(down_low, "dp", scatter_dimension=0, tiled=True)
    out_high, in_high, route_high, both_high, down_high = experts(half, *work)
    sum_both_high = lax.psum_scatter(both_high, "dp", scatter_dimension=0, tiled=True)
    sum_down_high = lax.psum_scatter(down_high, "dp", scatter_dimension=0, tiled=True)
    my_route_grad = jnp.concatenate([route_low, route_high], axis=0)[:, 0]
    route_grad = lax.all_to_all(my_route_grad, "expert", split_axis=1, concat_axis=0, tiled=True).T
    grad_routed = combine_z(slot_cols, in_low, in_high, ways, 6).astype(F32)

    router = lax.dynamic_slice_in_dim(router_all, first_row, tok_dev, axis=0)
    grad_logits = (router * (route_grad - jnp.sum(router * route_grad, axis=-1, keepdims=True))).astype(BF16)
    grad_router_w = cross_rows(mix, grad_logits)
    grad_mix = grad_routed + by_transpose(grad_logits, router_full)
    grad_mix_gain = jnp.sum(grad_mix * mix_unit, axis=0)
    grad_resid = cotangent.astype(F32) + norm_back(grad_mix, mix_unit, mix_inverse, mix_gain)
    grad_branch = grad_resid.astype(BF16)
    grad_branch, sum_both_low, sum_down_low = lax.optimization_barrier((grad_branch, sum_both_low, sum_down_low))
    branch_all, output = gather_and_combine(grad_branch, slot_cols, weight_cols, out_low, out_high, resid, ways, 7)
    grad_heads = by_transpose(branch_all, out_mine).astype(BF16)
    grad_out_w = cross_rows(mixed_heads, branch_all).astype(BF16)
    out_out = lax.psum_scatter(grad_out_w, "dp", scatter_dimension=0, tiled=True)
    out_out = lax.ppermute(out_out, BOTH, row_moves(ways, lax.axis_size("dp"))).astype(F32)

    grad_heads, sum_both_high = lax.optimization_barrier((grad_heads, sum_both_high))
    dq, dk, dv = attend_back(order, q_rot, k_rot, v_b, lse, grad_heads, cos, sin)
    q_unit = qkv[:, :cols] * inv_q
    k_unit = qkv[:, cols : 2 * cols] * inv_k
    inner = jnp.stack(
        [jnp.sum(dq * gain_q * q_unit, axis=-1), jnp.sum(dk * gain_k * k_unit, axis=-1)], axis=0
    )
    inner = sum_z(jnp.pad(inner, ((0, 6), (0, 0))), ways, 8) / width
    grad_q_gain = jnp.sum(dq * q_unit, axis=0)
    grad_k_gain = jnp.sum(dk * k_unit, axis=0)
    grad_q = (inv_q * (dq * gain_q - q_unit * inner[0][:, None])).astype(BF16)
    grad_k = (inv_k * (dk * gain_k - k_unit * inner[1][:, None])).astype(BF16)
    grad_qkv = jnp.concatenate([grad_q, grad_k, dv], axis=1)
    grad_normed_part = by_transpose(grad_qkv, qkv_weight)
    grad_attend_gain = jnp.sum(grad_normed_part * (tokens_all.astype(F32) * inverse_in), axis=0)
    part, sum_down_high = lax.optimization_barrier((grad_normed_part.astype(BF16), sum_down_high))
    grad_normed = rs_z(part, ways, 9).astype(F32)
    own_inverse = lax.dynamic_slice_in_dim(inverse_in, first_row, tok_dev, axis=0)
    input_grad = grad_resid + norm_back(grad_normed, own_f * own_inverse, own_inverse, attend_gain)

    place = lambda part: lax.dynamic_update_slice(jnp.zeros((width,), F32), part, (z * cols,))
    extra = jnp.concatenate(
        [
            jnp.stack([grad_attend_gain, place(grad_q_gain), place(grad_k_gain), grad_mix_gain], axis=1),
            grad_router_w,
            jnp.zeros((width, SMALL - 4 - EXPERTS), F32),
        ],
        axis=1,
    )
    grad_qkv_w = weight_grad(normed, grad_qkv, extra)
    grad_qkv_w = lax.psum_scatter(grad_qkv_w, "dp", scatter_dimension=0, tiled=True)
    grad_qkv_w = exchange_z(grad_qkv_w, ways, 10).reshape(ways, -1, 3 * cols + SMALL)
    grad_w = [
        grad_qkv_w[:, :, i * cols : (i + 1) * cols].transpose(1, 0, 2).reshape(-1, width).astype(F32)
        for i in range(3)
    ]
    planes = [jnp.concatenate([sum_both_low[0, i], sum_both_high[0, i]], axis=0) for i in range(2)]
    out_gate, out_up = planes[0].astype(F32), planes[1].astype(F32)
    out_down = jnp.concatenate([sum_down_low[0], sum_down_high[0]], axis=0).astype(F32)
    packed = jnp.sum(grad_qkv_w[:, :, 3 * cols :].astype(F32), axis=0)
    return (
        output,
        input_grad,
        packed[:, 0],
        grad_w[0],
        grad_w[1],
        grad_w[2],
        out_out,
        packed[:, 1],
        packed[:, 2],
        packed[:, 3],
        packed[:, 4 : 4 + EXPERTS],
        out_gate,
        out_up,
        out_down,
    )


def solution(mesh):
    rows = P(BOTH, None)
    vec = P(BOTH)
    expert = P("expert", "dp", None)
    group = P("dp", None)
    return jax.shard_map(
        body,
        mesh=mesh,
        in_specs=(rows, rows, vec, rows, rows, rows, rows, vec, vec, vec, rows, expert, expert, expert)
        + (group, group, group, P("dp", None, None)),
        out_specs=(rows, rows, vec, rows, rows, rows, rows, vec, vec, vec, rows, expert, expert, expert),
        check_vma=False,
    )
```
